512 devices in a mesh: det: 64 (over x, z), tm: 8 (over y, core).
Axes of the slice: x: 4, y: 4, z: 16, core: 2. Of those that a mesh axis runs over, the one named last changes fastest.
Arguments:
- timestream: bfloat16 [8192, 1024], P('det', 'tm'), may hold values from -6 to 6
- pointing: int32 [8192, 1024], P('det', 'tm'), may hold values from 0 to 65535
- detector_band: int32 [8192], P('det'), may hold values from 0 to 19
- mode_loading: bfloat16 [8192, 64], P('det'), may hold values from -0.29492188 to 0.29492188
- mode_mix: float32 [20, 64, 64], replicated, may hold values from -0.36 to 0.36
- noise_weight: float32 [8192], P('det'), may hold values from 0.3 to 3
- ownership: int32 [512], replicated, may hold values from 0 to 511, each once
Outputs:
- amplitudes: float32 [1280, 1024], P(None, 'tm')
- sky_map: float32 [512, 128], P('det')
The draws below stay inside these ranges and needn't reach their ends.
Inputs may be any that keep to these rules, and one draw needn't show every extreme that they name: `ownership`: each tile appears once.
All inputs are finite; a program needn't handle non-finite values.
Results may differ from the reference program's by a relative error of at most 0.0037.
Values sent between devices are 32-bit elements; how exact they have to be, the bound alone decides.
No kernel may reach another device: no remote copies, remote signals or barrier semaphores. Data moves between devices by JAX's collectives and lax.ppermute only.
A program may use at most 64 MiB of HBM per device.

```python
import math
import jax
import jax.numpy as jnp
import numpy as np
from jax import lax

BANDS = 20
MODES = 64
TILE_PIX = 128
NTILES = 512
NDET = 8192
NTIME = 1024
NPIX = 65536


def set_ends(result, stream_key, least, largest):
    shape = result.shape
    place = [jax.random.randint(jax.random.fold_in(stream_key, axis), (), 0, shape[axis]) for axis in range(len(shape))]
    result = result.at[tuple(place)].set(least)
    longest = shape.index(max(shape))
    place[longest] = (place[longest] + 1) % shape[longest]
    return result.at[tuple(place)].set(largest)


def level_of(rng, extent, split, smallest, largest):
    loudness = 1.0
    for axis_at, parts in split:
        heights = jax.random.uniform(jax.random.fold_in(jax.random.fold_in(rng, 6), axis_at), (parts,), jnp.float32, smallest / len(split), largest / len(split))
        loudness = loudness * jnp.repeat(jnp.exp(heights), extent[axis_at] // parts).reshape((-1,) + (1,) * (len(extent) - 1 - axis_at))
    return loudness


def cumulative_ranks(number_of, slope):
    portions = [(1 << 20) // math.isqrt(standing ** slope) + 1 for standing in range(1, number_of + 1)]
    scale = 1 + sum(portions) // (1 << 30)
    return np.cumsum(np.array([max(1, weight // scale) for weight in portions]))


def ranked_ids(stream_key, extent, number_of, lean):
    table = cumulative_ranks(number_of, lean)
    pick = jax.random.randint(jax.random.fold_in(stream_key, 1), extent, 0, int(table[number_of - 1]))
    rank = jnp.searchsorted(jnp.asarray(table, jnp.int32), pick, side="right")
    return jax.random.permutation(jax.random.fold_in(stream_key, 2), number_of)[rank].astype(jnp.int32)


def centred(key, dims, width, limit, cuts=(), held_as=jnp.bfloat16):
    factor_of = level_of(key, dims, cuts, -0.22, 0.18) if cuts else 1.0
    drawn = jax.random.normal(key, dims, jnp.float32) * width * factor_of
    return jnp.minimum(jnp.maximum(drawn, -limit), limit).astype(held_as)


def setup_inputs(seed: int = 0) -> dict:
    seeds = jax.random.split(jax.random.key(seed), 8)
    timestream = centred(seeds[0], (NDET, NTIME), 1.0, 6.0, ((0, 64), (1, 8)))
    pointing = set_ends(ranked_ids(seeds[1], (NDET, NTIME), NPIX, 1), jax.random.fold_in(seeds[1], 3), 0, NPIX - 1).astype(jnp.int32)
    detector_band = set_ends(jax.random.randint(seeds[2], (NDET,), 0, BANDS), jax.random.fold_in(seeds[2], 1), 0, BANDS - 1).astype(jnp.int32)
    mode_loading = centred(seeds[3], (NDET, MODES), ((NDET / BANDS) ** -0.5), 0.29492188, ((0, 64),))
    mode_mix = centred(seeds[4], (BANDS, MODES, MODES), 0.06, 0.36, (), jnp.float32)
    noise_weight = jnp.clip(jnp.exp(math.log(3.0) - 2.3025851 * jax.random.uniform(seeds[5], (NDET,), jnp.float32) ** level_of(seeds[5], (NDET,), ((0, 64),), -0.2, 0.2)), 0.3, 3.0)
    ownership = jax.random.permutation(seeds[6], NTILES).astype(jnp.int32)
    return dict(timestream=timestream, pointing=pointing, detector_band=detector_band, mode_loading=mode_loading, mode_mix=mode_mix, noise_weight=noise_weight, ownership=ownership)


HIGHEST = lax.Precision.HIGHEST


def reference(timestream, pointing, detector_band, mode_loading, mode_mix, noise_weight, ownership):
    onehot = (detector_band[:, None] == jnp.arange(BANDS, dtype=jnp.int32)[None, :]).astype(jnp.float32)
    loading = (onehot[:, :, None] * mode_loading.astype(jnp.float32)[:, None, :]).reshape(NDET, BANDS * MODES)
    tod_wide = timestream.astype(jnp.float32)
    projected = jnp.dot(loading.T, tod_wide, precision=HIGHEST)
    blocks = projected.reshape(BANDS, MODES, NTIME)
    mixing = jnp.einsum("bmn,bnt->bmt", mode_mix, blocks, precision=HIGHEST)
    amplitudes = (blocks + mixing).reshape(BANDS * MODES, NTIME)
    amp_rounded = amplitudes.astype(jnp.bfloat16)
    weighted = (noise_weight[:, None] * tod_wide).astype(jnp.bfloat16)
    fitted = jnp.dot(loading, amp_rounded.astype(jnp.float32), precision=HIGHEST)
    correction = (noise_weight[:, None] * fitted).astype(jnp.bfloat16)
    difference = weighted.astype(jnp.float32) - correction.astype(jnp.float32)
    flat_map = jnp.zeros((NPIX,), jnp.float32).at[pointing.reshape(-1)].add(difference.reshape(-1))
    sky_map = flat_map.reshape(NTILES, TILE_PIX)[ownership]
    return amplitudes, sky_map
```

```python
import functools

import jax
import jax.numpy as jnp
from jax import lax
from jax.experimental import pallas as pl
from jax.experimental.pallas import tpu as pltpu
from jax.sharding import Mesh, PartitionSpec as P

TILE_PIX = 128
HALF = 256
GROUP = 8


def project_kernel(pad, loading_t_ref, band_ref, ts_ref, out_ref):
    modes, dets = loading_t_ref.shape
    slot = lax.broadcasted_iota(jnp.int32, (pad, dets), 0)
    pick = jnp.where(slot == band_ref[...], 1.0, 0.0).astype(jnp.float32)
    loading = loading_t_ref[...].astype(jnp.float32)
    wide = (loading[:, None, :] * pick[None, :, :]).reshape(modes * pad, dets)
    out_ref[...] = jnp.dot(
        wide.astype(jnp.bfloat16), ts_ref[...], preferred_element_type=jnp.float32
    )


def split(x):
    high = x.astype(jnp.bfloat16)
    low = (x - high.astype(jnp.float32)).astype(jnp.bfloat16)
    return high, low


def map_kernel(
    bands, pad, own_ref, proj_ref, mix_ref, loading_t_ref, band_ref, noise_ref, ts_ref,
    point_ref, amp_ref, map_ref, hi_s, lo_s, plus_s, minus_s, acc_s
):
    modes, dets = loading_t_ref.shape
    times = ts_ref.shape[1]
    rounded = []
    for b in range(bands):
        p = proj_ref[pl.ds(b, modes, stride=pad), :]
        mh, ml = split(mix_ref[b])
        ph, plow = split(p)
        mixing = jnp.dot(
            jnp.concatenate([mh, ml, mh], axis=1),
            jnp.concatenate([ph, ph, plow], axis=0),
            preferred_element_type=jnp.float32,
        )
        amp = p + mixing
        amp_ref[b * modes:(b + 1) * modes, :] = amp
        rounded.append(amp.astype(jnp.bfloat16))
    amp_rounded = jnp.concatenate(rounded, axis=0)

    loading_f = loading_t_ref[...].astype(jnp.float32)
    loading2 = jnp.concatenate([loading_f, loading_f], axis=0).T
    band_col = jnp.broadcast_to(band_ref[...], (2 * modes, dets)).astype(jnp.float32).T
    noise_col = jnp.broadcast_to(noise_ref[...], (times, dets)).T
    lane_band = (lax.broadcasted_iota(jnp.int32, (dets, 2 * modes), 1) // modes).astype(jnp.float32)
    band_off = band_col - lane_band
    wide = jnp.concatenate(
        [
            jnp.where(band_off == float(b), loading2, 0.0).astype(jnp.bfloat16)
            for b in range(0, bands, 2)
        ],
        axis=1,
    )
    fitted = jnp.dot(wide, amp_rounded, preferred_element_type=jnp.float32)
    weighted = (noise_col * ts_ref[...].astype(jnp.float32)).astype(jnp.bfloat16)
    correction = (noise_col * fitted).astype(jnp.bfloat16)
    plus_s[...] = weighted.astype(jnp.float32)
    minus_s[...] = -correction.astype(jnp.float32)
    point = point_ref[...]
    hi_s[...] = (point >> 8).astype(jnp.float32)
    lo_s[...] = (point & 255).astype(jnp.float32)
    acc_s[...] = jnp.zeros_like(acc_s)
    ids = lax.broadcasted_iota(jnp.int32, (HALF, times), 0).astype(jnp.float32).astype(jnp.bfloat16)
    ids = ids.reshape(HALF // 16, 16, times)
    one = jnp.ones((), jnp.bfloat16)
    zero = jnp.zeros((), jnp.bfloat16)

    def row(ref, i):
        return jnp.broadcast_to(ref[pl.ds(i, 1), :], (16, times)).astype(jnp.bfloat16)[None]

    def body(g, carry):
        left, right = [], []
        for k in range(GROUP):
            i = g * GROUP + k
            upper = jnp.where(row(hi_s, i) == ids, one, zero).reshape(HALF, times)
            lower = row(lo_s, i) == ids
            left += [upper, upper]
            right.append(jnp.where(lower, row(plus_s, i), zero).reshape(HALF, times))
            right.append(jnp.where(lower, row(minus_s, i), zero).reshape(HALF, times))
        added = lax.dot_general(
            jnp.concatenate(left, axis=1),
            jnp.concatenate(right, axis=1),
            (((1,), (1,)), ((), ())),
            preferred_element_type=jnp.float32,
        )
        acc_s[0] += added[:, :TILE_PIX]
        acc_s[1] += added[:, TILE_PIX:]
        return carry

    lax.fori_loop(0, dets // GROUP, body, 0, unroll=4)

    def place(r, carry):
        tile = own_ref[r]
        map_ref[pl.ds(r, 1), :] = acc_s[tile & 1, pl.ds(tile >> 1, 1), :]
        return carry

    lax.fori_loop(0, map_ref.shape[0], place, 0, unroll=8)


def per_device(
    timestream, pointing, detector_band, mode_loading, mode_mix, noise_weight, ownership
):
    dets, times = timestream.shape
    bands, modes = mode_mix.shape[:2]
    pad = -(-bands // 8) * 8
    loading_t = mode_loading.T
    band_row = detector_band[None, :]
    noise_row = noise_weight[None, :]
    tiles = ownership.shape[0]
    vmem = pl.BlockSpec(memory_space=pltpu.VMEM)
    params = pltpu.CompilerParams(vmem_limit_bytes=32 * 1024 * 1024)

    local = pl.pallas_call(
        functools.partial(project_kernel, pad),
        out_shape=jax.ShapeDtypeStruct((modes * pad, times), jnp.float32),
        in_specs=[vmem] * 3,
        out_specs=vmem,
        compiler_params=params,
    )(loading_t, band_row, timestream)

    nx, nz = lax.axis_size("x"), lax.axis_size("z")
    swapped = lax.all_to_all(local, "x", 0, 0, tiled=True)
    share = swapped.reshape(nx, -1, times).sum(0)
    swapped = lax.all_to_all(share, "z", 0, 0, tiled=True)
    share = swapped.reshape(nz, -1, times).sum(0)
    projected = lax.all_gather(share, ("x", "z"), axis=0, tiled=True)

    amplitudes, part = pl.pallas_call(
        functools.partial(map_kernel, bands, pad),
        out_shape=(
            jax.ShapeDtypeStruct((bands * modes, times), jnp.float32),
            jax.ShapeDtypeStruct((tiles, TILE_PIX), jnp.float32),
        ),
        in_specs=[pl.BlockSpec(memory_space=pltpu.SMEM)] + [vmem] * 7,
        out_specs=(vmem, vmem),
        scratch_shapes=[
            pltpu.VMEM((dets, times), jnp.float32),
            pltpu.VMEM((dets, times), jnp.float32),
            pltpu.VMEM((dets, times), jnp.float32),
            pltpu.VMEM((dets, times), jnp.float32),
            pltpu.VMEM((2, HALF, TILE_PIX), jnp.float32),
        ],
        compiler_params=params,
    )(ownership, projected, mode_mix, loading_t, band_row, noise_row, timestream, pointing)

    ndet = nx * nz
    swapped = lax.all_to_all(part, ("x", "z"), 0, 0, tiled=True)
    share = swapped.reshape(ndet, -1, TILE_PIX).sum(0)
    blocks = lax.all_gather(share, ("y", "core"), axis=0, tiled=False)
    return amplitudes, blocks.sum(0)


def solution(mesh):
    fine = Mesh(mesh.devices.reshape(4, 16, 4, 2), ("x", "z", "y", "core"))
    det, tm = ("x", "z"), ("y", "core")
    placed = (P(det, tm), P(det, tm), P(det), P(det, None), P(), P(det), P())
    return jax.shard_map(
        per_device,
        mesh=fine,
        in_specs=placed,
        out_specs=(P(None, tm), P(det, None)),
        check_vma=False,
    )
```

```python
import functools

import jax
import jax.numpy as jnp
from jax import lax
from jax.experimental import pallas as pl
from jax.experimental.pallas import tpu as pltpu
from jax.sharding import Mesh, PartitionSpec as P

TILE_PIX = 128
HALF = 256
GROUP = 8
EXTRA = 8
F32 = jnp.float32
BF16 = jnp.bfloat16


def lanes(rows, width):
    return lax.broadcasted_iota(jnp.int32, (rows, 128), 1) // width


def turn(x, amount):
    amount %= 128
    return pltpu.roll(x, amount, 1) if amount else x


def split(x):
    high = x.astype(BF16)
    low = (x - high.astype(F32)).astype(BF16)
    return high, low


def pack_kernel(nx, loading_t_ref, band_ref, noise_ref, ts_ref, point_ref, out_ref):
    modes, dets = loading_t_ref.shape
    width = ts_ref.shape[1] // nx
    rows = dets + EXTRA
    ts = ts_ref[...].astype(F32)
    point = point_ref[...].astype(F32)
    loading_t = loading_t_ref[...].astype(F32)
    loading = jnp.concatenate([jnp.zeros((128 - modes, dets), F32), loading_t], axis=0).T
    group = lanes(dets, width)
    for d in range(nx):
        body = jnp.where(group == 0, turn(ts, -width * d), turn(point, width - width * d))
        out_ref[d * rows:d * rows + dets, :] = jnp.where(group < 2, body, loading)
        out_ref[d * rows + dets:(d + 1) * rows, :] = jnp.concatenate(
            [band_ref[...].astype(F32), noise_ref[...], jnp.zeros((EXTRA - 2, dets), F32)], axis=0
        )


def project_kernel(nx, modes, pad, got_ref, out_ref):
    rows = got_ref.shape[0] // nx
    dets = rows - EXTRA
    width = 128 // nx
    per = modes * width // 128
    group = lanes(dets, width)
    slot = lax.broadcasted_iota(jnp.int32, (pad, dets), 0).astype(F32)
    left, right = [], []
    for s in range(nx):
        chunk = got_ref[s * rows:s * rows + dets, :]
        loading_t = chunk.T[128 - modes:, :]
        ts = jnp.where(group == 0, chunk, 0.0)
        pick = jnp.where(slot == got_ref[s * rows + dets:s * rows + dets + 1, :], 1.0, 0.0)
        for j in range(modes // per):
            part = loading_t[j * per:(j + 1) * per, :]
            left.append((part[:, None, :] * pick[None]).reshape(per * pad, dets).astype(BF16))
            right.append(turn(ts, width * j).astype(BF16))
    out_ref[...] = jnp.dot(
        jnp.concatenate(left, axis=1), jnp.concatenate(right, axis=0), preferred_element_type=F32
    )


def fit_kernel(
    nx, bands, pad, proj_ref, mix_ref, got_ref, amp_ref, plus_ref, minus_ref, hi_ref, lo_ref
):
    modes = mix_ref.shape[1]
    rows = got_ref.shape[0] // nx
    dets = rows - EXTRA
    width = 128 // nx
    per = modes // nx
    group = lanes(per, width)
    rounded = []
    for b in range(bands):
        mine = proj_ref[pl.ds(b, per, stride=pad), :]
        turned = [turn(mine, width * k) for k in range(nx)]
        pieces = []
        for j in range(nx):
            piece = turned[(0 - j) % nx]
            for g in range(1, nx):
                piece = jnp.where(group == g, turned[(g - j) % nx], piece)
            pieces.append(piece)
        p = jnp.concatenate(pieces, axis=0)
        mh, ml = split(mix_ref[b])
        ph, plow = split(p)
        amp = p + jnp.dot(
            jnp.concatenate([mh, ml, mh], axis=1),
            jnp.concatenate([ph, ph, plow], axis=0),
            preferred_element_type=F32,
        )
        rounded.append(amp.astype(BF16))
        packed = amp[:per, :]
        for j in range(1, nx):
            packed = jnp.where(group == j, amp[j * per:(j + 1) * per, :], packed)
        amp_ref[b * per:(b + 1) * per, :] = packed
    amp_rounded = jnp.concatenate(rounded, axis=0)

    det_group = lanes(dets, width)
    lane_band = lanes(dets, modes).astype(F32)
    wides, noises = [], []
    for s in range(nx):
        chunk = got_ref[s * rows:s * rows + dets, :]
        tail = got_ref[s * rows + dets:(s + 1) * rows, :]
        columns = jnp.concatenate([tail, jnp.zeros((128 - EXTRA, dets), F32)], axis=0).T
        band_off = jnp.broadcast_to(columns[:, 0:1], (dets, 128)) - lane_band
        noises.append(jnp.broadcast_to(columns[:, 1:2], (dets, 128)))
        loading2 = jnp.where(lanes(dets, modes) == 0, turn(chunk, modes), chunk)
        wides.append(
            jnp.concatenate(
                [
                    jnp.where(band_off == float(b), loading2, 0.0).astype(BF16)
                    for b in range(0, bands, 2)
                ],
                axis=1,
            )
        )
    fits = jnp.dot(jnp.concatenate(wides, axis=0), amp_rounded, preferred_element_type=F32)
    for s in range(nx):
        chunk = got_ref[s * rows:s * rows + dets, :]
        here = (noises[s], turn(chunk, width * s), turn(chunk, width * (s - 1)), fits[s * dets:(s + 1) * dets, :])
        total = here if s == 0 else tuple(
            jnp.where(det_group == s, a, b) for a, b in zip(here, total)
        )
    noise, ts, point, fitted = total
    plus_ref[...] = (noise * ts).astype(BF16).astype(F32)
    minus_ref[...] = -(noise * fitted).astype(BF16).astype(F32)
    point = point.astype(jnp.int32)
    hi_ref[...] = (point >> 8).astype(F32)
    lo_ref[...] = (point & 255).astype(F32)


def bin_kernel(shape, own_ref, plus_ref, minus_ref, hi_ref, lo_ref, map_ref, acc_s):
    dets, times = plus_ref.shape
    nx, nz, nt = shape
    acc_s[...] = jnp.zeros_like(acc_s)
    ids = lax.broadcasted_iota(jnp.int32, (HALF, times), 0).astype(F32).astype(BF16)
    ids = ids.reshape(HALF // 16, 16, times)
    one = jnp.ones((), BF16)
    zero = jnp.zeros((), BF16)

    def row(ref, i):
        return jnp.broadcast_to(ref[pl.ds(i, 1), :], (16, times)).astype(BF16)[None]

    def body(g, carry):
        left, right = [], []
        for k in range(GROUP):
            i = g * GROUP + k
            upper = jnp.where(row(hi_ref, i) == ids, one, zero).reshape(HALF, times)
            lower = row(lo_ref, i) == ids
            left += [upper, upper]
            right.append(jnp.where(lower, row(plus_ref, i), zero).reshape(HALF, times))
            right.append(jnp.where(lower, row(minus_ref, i), zero).reshape(HALF, times))
        added = lax.dot_general(
            jnp.concatenate(left, axis=1),
            jnp.concatenate(right, axis=1),
            (((1,), (1,)), ((), ())),
            preferred_element_type=F32,
        )
        acc_s[0] += added[:, :TILE_PIX]
        acc_s[1] += added[:, TILE_PIX:]
        return carry

    lax.fori_loop(0, dets // GROUP, body, 0, unroll=4)

    def place(r, carry):
        tile = own_ref[r]
        x, z, k = r // (nz * nt), r // nt % nz, r % nt
        map_ref[pl.ds((x * nt + k) * nz + z, 1), :] = acc_s[tile & 1, pl.ds(tile >> 1, 1), :]
        return carry

    lax.fori_loop(0, nx * nz * nt, place, 0, unroll=8)


def gather_kernel(nx, bands, *refs):
    parts, out_ref = refs[:nx], refs[nx]
    per = parts[0].shape[0] // bands
    width = 128 // nx
    group = lanes(per, width)
    mine = lax.axis_index("x")
    sources = [lax.rem(mine + nx - k, nx) for k in range(nx)]
    for b in range(bands):
        for j in range(nx):
            total = jnp.zeros((per, 128), F32)
            for k in range(nx):
                piece = parts[k][b * per:(b + 1) * per, :]
                moved = pltpu.roll(piece, lax.rem(sources[k] + nx - j, nx) * width, 1)
                total = jnp.where(group == sources[k], moved, total)
            out_ref[(b * nx + j) * per:(b * nx + j + 1) * per, :] = total


def per_device(
    timestream, pointing, detector_band, mode_loading, mode_mix, noise_weight, ownership
):
    dets, times = timestream.shape
    bands, modes = mode_mix.shape[:2]
    pad = -(-bands // 8) * 8
    tiles = ownership.shape[0]
    nx, nz = lax.axis_size("x"), lax.axis_size("z")
    nt = lax.axis_size("y") * lax.axis_size("core")
    vmem = pl.BlockSpec(memory_space=pltpu.VMEM)
    smem = pl.BlockSpec(memory_space=pltpu.SMEM)
    params = pltpu.CompilerParams(vmem_limit_bytes=32 * 1024 * 1024)

    def call(kernel, shapes, args, specs=None, scratch=(), cost=None):
        return pl.pallas_call(
            kernel,
            out_shape=tuple(jax.ShapeDtypeStruct(s, F32) for s in shapes),
            in_specs=specs or [vmem] * len(args),
            out_specs=tuple(vmem for _ in shapes),
            scratch_shapes=scratch,
            compiler_params=params,
            cost_estimate=cost,
        )(*args)

    (packed,) = call(
        functools.partial(pack_kernel, nx),
        [(nx * (dets + EXTRA), 128)],
        (mode_loading.T, detector_band[None, :], noise_weight[None, :], timestream, pointing),
    )
    got = lax.all_to_all(packed, "x", 0, 0, tiled=True)
    (local,) = call(
        functools.partial(project_kernel, nx, modes, pad), [(nz * pad, 128)], (got,)
    )
    swapped = lax.all_to_all(local, "z", 0, 0, tiled=True)
    share = swapped.reshape(nz, pad, 128).sum(0)
    spread = jnp.broadcast_to(share[None], (nz, pad, 128)).reshape(nz * pad, 128)
    projected = lax.all_to_all(spread, "z", 0, 0, tiled=True)
    amp, plus, minus, hi, lo = call(
        functools.partial(fit_kernel, nx, bands, pad),
        [(bands * modes // nx, 128)] + [(dets, times)] * 4,
        (projected, mode_mix, got),
    )
    moved = [
        lax.ppermute(amp, "x", [(i, (i + k) % nx) for i in range(nx)]) for k in range(1, nx)
    ]
    (part,) = call(
        functools.partial(bin_kernel, (nx, nz, nt)),
        [(tiles, TILE_PIX)],
        (ownership, plus, minus, hi, lo),
        specs=[smem] + [vmem] * 4,
        scratch=[pltpu.VMEM((2, HALF, TILE_PIX), F32)],
        cost=pl.CostEstimate(flops=4 * dets * times * HALF * HALF, bytes_accessed=1 << 19, transcendentals=0),
    )
    swapped = lax.all_to_all(part, ("x", "y", "core"), 0, 0, tiled=True)
    share = swapped.reshape(nx * nt, nz, 1, TILE_PIX).sum(0)
    spread = jnp.broadcast_to(share[:, None], (nz, nt, 1, TILE_PIX)).reshape(nz * nt, TILE_PIX)
    swapped = lax.all_to_all(spread, ("z", "y", "core"), 0, 0, tiled=True)
    sky_map = swapped.reshape(nz, nt, TILE_PIX).sum(0)
    (amplitudes,) = call(
        functools.partial(gather_kernel, nx, bands), [(bands * modes, times)], (amp, *moved)
    )
    return amplitudes, sky_map


def solution(mesh):
    fine = Mesh(mesh.devices.reshape(4, 16, 4, 2), ("x", "z", "y", "core"))
    det, tm = ("x", "z"), ("y", "core")
    placed = (P(det, tm), P(det, tm), P(det), P(det, None), P(), P(det), P())
    return jax.shard_map(
        per_device,
        mesh=fine,
        in_specs=placed,
        out_specs=(P(None, tm), P(det, None)),
        check_vma=False,
    )
```

```python
import functools

import jax
import jax.numpy as jnp
from jax import lax
from jax.experimental import pallas as pl
from jax.experimental.pallas import tpu as pltpu
from jax.sharding import Mesh, PartitionSpec as P

TILE_PIX = 128
HALF = 256
GROUP = 8
EXTRA = 8
F32 = jnp.float32
BF16 = jnp.bfloat16


def lanes(rows, width):
    return lax.broadcasted_iota(jnp.int32, (rows, 128), 1) // width


def turn(x, amount):
    amount %= 128
    return pltpu.roll(x, amount, 1) if amount else x


def split(x):
    high = x.astype(BF16)
    low = (x - high.astype(F32)).astype(BF16)
    return high, low


def pack_kernel(nx, *refs):
    sources, (out_ref, *held, sems) = refs[:5], refs[5:]
    copies = [
        pltpu.make_async_copy(src, dst, sems.at[n]) for n, (src, dst) in enumerate(zip(sources, held))
    ]
    for copy in copies:
        copy.start()
    for copy in copies:
        copy.wait()
    loading_t_ref, band_ref, noise_ref, ts_ref, point_ref = held
    modes, dets = loading_t_ref.shape
    width = ts_ref.shape[1] // nx
    rows = dets + EXTRA
    ts = ts_ref[...].astype(F32)
    point = point_ref[...].astype(F32)
    loading_t = loading_t_ref[...].astype(F32)
    loading = jnp.concatenate([jnp.zeros((128 - modes, dets), F32), loading_t], axis=0).T
    group = lanes(dets, width)
    for d in range(nx):
        body = jnp.where(group == 0, turn(ts, -width * d), turn(point, width - width * d))
        out_ref[d * rows:d * rows + dets, :] = jnp.where(group < 2, body, loading)
        out_ref[d * rows + dets:(d + 1) * rows, :] = jnp.concatenate(
            [band_ref[...].astype(F32), noise_ref[...], jnp.zeros((EXTRA - 2, dets), F32)], axis=0
        )


def project_kernel(nx, modes, pad, got_ref, out_ref):
    rows = got_ref.shape[0] // nx
    dets = rows - EXTRA
    width = 128 // nx
    per = modes * width // 128
    group = lanes(dets, width)
    slot = lax.broadcasted_iota(jnp.int32, (pad, dets), 0).astype(F32)
    left, right = [], []
    for s in range(nx):
        chunk = got_ref[s * rows:s * rows + dets, :]
        loading_t = chunk.T[128 - modes:, :]
        ts = jnp.where(group == 0, chunk, 0.0)
        pick = jnp.where(slot == got_ref[s * rows + dets:s * rows + dets + 1, :], 1.0, 0.0)
        for j in range(modes // per):
            part = loading_t[j * per:(j + 1) * per, :]
            left.append((part[:, None, :] * pick[None]).reshape(per * pad, dets).astype(BF16))
            right.append(turn(ts, width * j).astype(BF16))
    out_ref[...] = jnp.dot(
        jnp.concatenate(left, axis=1), jnp.concatenate(right, axis=0), preferred_element_type=F32
    )


def fit_kernel(
    nx, bands, pad, proj_ref, mix_ref, got_ref, amp_ref, plus_ref, minus_ref, hi_ref, lo_ref
):
    modes = mix_ref.shape[1]
    rows = got_ref.shape[0] // nx
    dets = rows - EXTRA
    width = 128 // nx
    per = modes // nx
    group = lanes(per, width)
    rounded = []
    for b in range(bands):
        mine = proj_ref[pl.ds(b, per, stride=pad), :]
        turned = [turn(mine, width * k) for k in range(nx)]
        pieces = []
        for j in range(nx):
            piece = turned[(0 - j) % nx]
            for g in range(1, nx):
                piece = jnp.where(group == g, turned[(g - j) % nx], piece)
            pieces.append(piece)
        p = jnp.concatenate(pieces, axis=0)
        mh, ml = split(mix_ref[b])
        ph, plow = split(p)
        amp = p + jnp.dot(
            jnp.concatenate([mh, ml, mh], axis=1),
            jnp.concatenate([ph, ph, plow], axis=0),
            preferred_element_type=F32,
        )
        rounded.append(amp.astype(BF16))
        packed = amp[:per, :]
        for j in range(1, nx):
            packed = jnp.where(group == j, amp[j * per:(j + 1) * per, :], packed)
        amp_ref[b * per:(b + 1) * per, :] = packed
    amp_rounded = jnp.concatenate(rounded, axis=0)

    det_group = lanes(dets, width)
    lane_band = lanes(dets, modes).astype(F32)
    wides, noises = [], []
    for s in range(nx):
        chunk = got_ref[s * rows:s * rows + dets, :]
        tail = got_ref[s * rows + dets:(s + 1) * rows, :]
        columns = jnp.concatenate([tail, jnp.zeros((128 - EXTRA, dets), F32)], axis=0).T
        band_off = jnp.broadcast_to(columns[:, 0:1], (dets, 128)) - lane_band
        noises.append(jnp.broadcast_to(columns[:, 1:2], (dets, 128)))
        loading2 = jnp.where(lanes(dets, modes) == 0, turn(chunk, modes), chunk)
        wides.append(
            jnp.concatenate(
                [
                    jnp.where(band_off == float(b), loading2, 0.0).astype(BF16)
                    for b in range(0, bands, 2)
                ],
                axis=1,
            )
        )
    fits = jnp.dot(jnp.concatenate(wides, axis=0), amp_rounded, preferred_element_type=F32)
    for s in range(nx):
        chunk = got_ref[s * rows:s * rows + dets, :]
        here = (noises[s], turn(chunk, width * s), turn(chunk, width * (s - 1)), fits[s * dets:(s + 1) * dets, :])
        total = here if s == 0 else tuple(
            jnp.where(det_group == s, a, b) for a, b in zip(here, total)
        )
    noise, ts, point, fitted = total
    plus_ref[...] = (noise * ts).astype(BF16).astype(F32)
    minus_ref[...] = -(noise * fitted).astype(BF16).astype(F32)
    point = point.astype(jnp.int32)
    hi_ref[...] = (point >> 8).astype(F32)
    lo_ref[...] = (point & 255).astype(F32)


def bin_kernel(shape, own_ref, plus_ref, minus_ref, hi_ref, lo_ref, map_ref, acc_s):
    dets, times = plus_ref.shape
    nx, nh, nl, nt = shape
    acc_s[...] = jnp.zeros_like(acc_s)
    ids = lax.broadcasted_iota(jnp.int32, (HALF, times), 0).astype(F32).astype(BF16)
    ids = ids.reshape(HALF // 16, 16, times)
    one = jnp.ones((), BF16)
    zero = jnp.zeros((), BF16)

    def row(ref, i):
        return jnp.broadcast_to(ref[pl.ds(i, 1), :], (16, times)).astype(BF16)[None]

    def body(g, carry):
        left, right = [], []
        for k in range(GROUP):
            i = g * GROUP + k
            upper = jnp.where(row(hi_ref, i) == ids, one, zero).reshape(HALF, times)
            lower = row(lo_ref, i) == ids
            left += [upper, upper]
            right.append(jnp.where(lower, row(plus_ref, i), zero).reshape(HALF, times))
            right.append(jnp.where(lower, row(minus_ref, i), zero).reshape(HALF, times))
        added = lax.dot_general(
            jnp.concatenate(left, axis=1),
            jnp.concatenate(right, axis=1),
            (((1,), (1,)), ((), ())),
            preferred_element_type=F32,
        )
        acc_s[0] += added[:, :TILE_PIX]
        acc_s[1] += added[:, TILE_PIX:]
        return carry

    lax.fori_loop(0, dets // GROUP, body, 0, unroll=4)

    rows = [(x, k, low, high) for x in range(nx) for k in range(nt) for low in range(nl) for high in range(nh)]
    for at, (x, k, low, high) in enumerate(rows):
        tile = own_ref[((x * nh + high) * nl + low) * nt + k]
        map_ref[at:at + 1, :] = acc_s[tile & 1, pl.ds(tile >> 1, 1), :]


def gather_kernel(nx, bands, parts_ref, out_ref):
    rows = parts_ref.shape[0] // nx
    per = rows // bands
    width = 128 // nx
    group = lanes(per, width)
    for b in range(bands):
        pieces = [parts_ref[s * rows + b * per:s * rows + (b + 1) * per, :] for s in range(nx)]
        for j in range(nx):
            total = turn(pieces[0], -width * j)
            for s in range(1, nx):
                total = jnp.where(group == s, turn(pieces[s], width * (s - j)), total)
            out_ref[(b * nx + j) * per:(b * nx + j + 1) * per, :] = total


def add_over(x, axes):
    swapped = lax.all_to_all(x, axes, 0, 0, tiled=True)
    return swapped.reshape((lax.axis_size(axes), -1) + x.shape[1:]).sum(0)


def copy_over(x, axes):
    count = lax.axis_size(axes)
    spread = jnp.broadcast_to(x[None], (count,) + x.shape).reshape((-1,) + x.shape[1:])
    return lax.all_to_all(spread, axes, 0, 0, tiled=True)


def per_device(
    timestream, pointing, detector_band, mode_loading, mode_mix, noise_weight, ownership
):
    dets, times = timestream.shape
    bands, modes = mode_mix.shape[:2]
    pad = -(-bands // 8) * 8
    tiles = ownership.shape[0]
    nx, nh, nl = lax.axis_size("x"), lax.axis_size("zh"), lax.axis_size("zl")
    nz = nh * nl
    nt = lax.axis_size("y") * lax.axis_size("core")
    vmem = pl.BlockSpec(memory_space=pltpu.VMEM)
    smem = pl.BlockSpec(memory_space=pltpu.SMEM)
    params = pltpu.CompilerParams(vmem_limit_bytes=32 * 1024 * 1024)

    def call(kernel, shapes, args, specs=None, scratch=(), cost=None, limit=params):
        return pl.pallas_call(
            kernel,
            out_shape=tuple(jax.ShapeDtypeStruct(s, F32) for s in shapes),
            in_specs=specs or [vmem] * len(args),
            out_specs=tuple(vmem for _ in shapes),
            scratch_shapes=scratch,
            compiler_params=limit,
            cost_estimate=cost,
        )(*args)

    inputs = (mode_loading.T, detector_band[None, :], noise_weight[None, :], timestream, pointing)
    (packed,) = call(
        functools.partial(pack_kernel, nx),
        [(nx * (dets + EXTRA), 128)],
        inputs,
        specs=[pl.BlockSpec(memory_space=pltpu.HBM)] * 5,
        scratch=[pltpu.VMEM(a.shape, a.dtype) for a in inputs] + [pltpu.SemaphoreType.DMA((5,))],
        limit=None,
    )
    got = lax.all_to_all(packed, "x", 0, 0, tiled=True)
    (local,) = call(
        functools.partial(project_kernel, nx, modes, pad), [(nz * pad, 128)], (got,)
    )
    share = add_over(local, "zl")
    share = add_over(share, "zh")
    projected = copy_over(copy_over(share, "zh"), "zl")
    amp, plus, minus, hi, lo = call(
        functools.partial(fit_kernel, nx, bands, pad),
        [(bands * modes // nx, 128)] + [(dets, times)] * 4,
        (projected, mode_mix, got),
    )
    gathered = copy_over(amp, "x")
    (part,) = call(
        functools.partial(bin_kernel, (nx, nh, nl, nt)),
        [(tiles, TILE_PIX)],
        (ownership, plus, minus, hi, lo),
        specs=[smem] + [vmem] * 4,
        scratch=[pltpu.VMEM((2, HALF, TILE_PIX), F32)],
        cost=pl.CostEstimate(flops=4 * dets * times * HALF * HALF, bytes_accessed=1 << 19, transcendentals=0),
    )
    part, gathered = lax.optimization_barrier((part, gathered))
    share = add_over(part, ("x", "y", "core"))
    share = add_over(add_over(share, "zl"), "zh")
    sky_map = copy_over(share, ("y", "core"))
    (amplitudes,) = call(
        functools.partial(gather_kernel, nx, bands), [(bands * modes, times)], (gathered,)
    )
    return amplitudes, sky_map


def solution(mesh):
    fine = Mesh(mesh.devices.reshape(4, 4, 4, 4, 2), ("x", "zh", "zl", "y", "core"))
    det, tm = ("x", "zh", "zl"), ("y", "core")
    placed = (P(det, tm), P(det, tm), P(det), P(det, None), P(), P(det), P())
    return jax.shard_map(
        per_device,
        mesh=fine,
        in_specs=placed,
        out_specs=(P(None, tm), P(det, None)),
        check_vma=False,
    )
```

```python
import functools

import jax
import jax.numpy as jnp
from jax import lax
from jax.experimental import pallas as pl
from jax.experimental.pallas import tpu as pltpu
from jax.sharding import Mesh, PartitionSpec as P

TILE_PIX = 128
HALF = 256
GROUP = 8
EXTRA = 8
F32 = jnp.float32
BF16 = jnp.bfloat16


def lanes(rows, width):
    return lax.broadcasted_iota(jnp.int32, (rows, 128), 1) // width


def turn(x, amount):
    amount %= 128
    return pltpu.roll(x, amount, 1) if amount else x


def split(x):
    high = x.astype(BF16)
    low = (x - high.astype(F32)).astype(BF16)
    return high, low


def pack_kernel(nx, *refs):
    sources, (out_ref, *held, sems) = refs[:5], refs[5:]
    copies = [
        pltpu.make_async_copy(src, dst, sems.at[n]) for n, (src, dst) in enumerate(zip(sources, held))
    ]
    for copy in copies:
        copy.start()
    for copy in copies:
        copy.wait()
    loading_t_ref, band_ref, noise_ref, ts_ref, point_ref = held
    modes, dets = loading_t_ref.shape
    width = ts_ref.shape[1] // nx
    rows = dets + EXTRA
    ts = ts_ref[...].astype(F32)
    point = point_ref[...].astype(F32)
    loading_t = loading_t_ref[...].astype(F32)
    loading = jnp.concatenate([jnp.zeros((128 - modes, dets), F32), loading_t], axis=0).T
    group = lanes(dets, width)
    for d in range(nx):
        body = jnp.where(group == 0, turn(ts, -width * d), turn(point, width - width * d))
        out_ref[d * rows:d * rows + dets, :] = jnp.where(group < 2, body, loading)
        out_ref[d * rows + dets:(d + 1) * rows, :] = jnp.concatenate(
            [band_ref[...].astype(F32), noise_ref[...], jnp.zeros((EXTRA - 2, dets), F32)], axis=0
        )


def project_kernel(nx, modes, pad, got_ref, out_ref):
    rows = got_ref.shape[0] // nx
    dets = rows - EXTRA
    width = 128 // nx
    per = modes * width // 128
    group = lanes(dets, width)
    slot = lax.broadcasted_iota(jnp.int32, (pad, dets), 0).astype(F32)
    left, right = [], []
    for s in range(nx):
        chunk = got_ref[s * rows:s * rows + dets, :]
        loading_t = chunk.T[128 - modes:, :]
        ts = jnp.where(group == 0, chunk, 0.0)
        pick = jnp.where(slot == got_ref[s * rows + dets:s * rows + dets + 1, :], 1.0, 0.0)
        for j in range(modes // per):
            part = loading_t[j * per:(j + 1) * per, :]
            left.append((part[:, None, :] * pick[None]).reshape(per * pad, dets).astype(BF16))
            right.append(turn(ts, width * j).astype(BF16))
    out_ref[...] = jnp.dot(
        jnp.concatenate(left, axis=1), jnp.concatenate(right, axis=0), preferred_element_type=F32
    )


def fit_kernel(
    nx, bands, pad, proj_ref, mix_ref, got_ref, amp_ref, plus_ref, minus_ref, hi_ref, lo_ref
):
    modes = mix_ref.shape[1]
    rows = got_ref.shape[0] // nx
    dets = rows - EXTRA
    width = 128 // nx
    per = modes // nx
    group = lanes(per, width)
    rounded = []
    for b in range(bands):
        mine = proj_ref[pl.ds(b, per, stride=pad), :]
        turned = [turn(mine, width * k) for k in range(nx)]
        pieces = []
        for j in range(nx):
            piece = turned[(0 - j) % nx]
            for g in range(1, nx):
                piece = jnp.where(group == g, turned[(g - j) % nx], piece)
            pieces.append(piece)
        p = jnp.concatenate(pieces, axis=0)
        mh, ml = split(mix_ref[b])
        ph, plow = split(p)
        amp = p + jnp.dot(
            jnp.concatenate([mh, ml, mh], axis=1),
            jnp.concatenate([ph, ph, plow], axis=0),
            preferred_element_type=F32,
        )
        rounded.append(amp.astype(BF16))
        packed = amp[:per, :]
        for j in range(1, nx):
            packed = jnp.where(group == j, amp[j * per:(j + 1) * per, :], packed)
        for d in range(nx):
            at = (d * bands + b) * per
            amp_ref[at:at + per, :] = packed
    amp_rounded = jnp.concatenate(rounded, axis=0)

    det_group = lanes(dets, width)
    lane_band = lanes(dets, modes).astype(F32)
    wides, noises = [], []
    for s in range(nx):
        chunk = got_ref[s * rows:s * rows + dets, :]
        tail = got_ref[s * rows + dets:(s + 1) * rows, :]
        columns = jnp.concatenate([tail, jnp.zeros((128 - EXTRA, dets), F32)], axis=0).T
        band_off = jnp.broadcast_to(columns[:, 0:1], (dets, 128)) - lane_band
        noises.append(jnp.broadcast_to(columns[:, 1:2], (dets, 128)))
        loading2 = jnp.where(lanes(dets, modes) == 0, turn(chunk, modes), chunk)
        wides.append(
            jnp.concatenate(
                [
                    jnp.where(band_off == float(b), loading2, 0.0).astype(BF16)
                    for b in range(0, bands, 2)
                ],
                axis=1,
            )
        )
    fits = jnp.dot(jnp.concatenate(wides, axis=0), amp_rounded, preferred_element_type=F32)
    for s in range(nx):
        chunk = got_ref[s * rows:s * rows + dets, :]
        here = (noises[s], turn(chunk, width * s), turn(chunk, width * (s - 1)), fits[s * dets:(s + 1) * dets, :])
        total = here if s == 0 else tuple(
            jnp.where(det_group == s, a, b) for a, b in zip(here, total)
        )
    noise, ts, point, fitted = total
    plus_ref[...] = (noise * ts).astype(BF16).astype(F32)
    minus_ref[...] = -(noise * fitted).astype(BF16).astype(F32)
    point = point.astype(jnp.int32)
    hi_ref[...] = (point >> 8).astype(F32)
    lo_ref[...] = (point & 255).astype(F32)


def bin_kernel(own_ref, plus_ref, minus_ref, hi_ref, lo_ref, map_ref, acc_s):
    dets, times = plus_ref.shape
    acc_s[...] = jnp.zeros_like(acc_s)
    ids = lax.broadcasted_iota(jnp.int32, (HALF, times), 0).astype(F32).astype(BF16)
    ids = ids.reshape(HALF // 16, 16, times)
    one = jnp.ones((), BF16)
    zero = jnp.zeros((), BF16)

    def row(ref, i):
        return jnp.broadcast_to(ref[pl.ds(i, 1), :], (16, times)).astype(BF16)[None]

    def body(g, carry):
        left, right = [], []
        for k in range(GROUP):
            i = g * GROUP + k
            upper = jnp.where(row(hi_ref, i) == ids, one, zero).reshape(HALF, times)
            lower = row(lo_ref, i) == ids
            left += [upper, upper]
            right.append(jnp.where(lower, row(plus_ref, i), zero).reshape(HALF, times))
            right.append(jnp.where(lower, row(minus_ref, i), zero).reshape(HALF, times))
        added = lax.dot_general(
            jnp.concatenate(left, axis=1),
            jnp.concatenate(right, axis=1),
            (((1,), (1,)), ((), ())),
            preferred_element_type=F32,
        )
        acc_s[0] += added[:, :TILE_PIX]
        acc_s[1] += added[:, TILE_PIX:]
        return carry

    lax.fori_loop(0, dets // GROUP, body, 0, unroll=4)

    for r in range(map_ref.shape[0]):
        tile = own_ref[r]
        map_ref[r:r + 1, :] = acc_s[tile & 1, pl.ds(tile >> 1, 1), :]


def gather_kernel(nx, bands, parts_ref, out_ref):
    rows = parts_ref.shape[0] // nx
    per = rows // bands
    width = 128 // nx
    group = lanes(per, width)
    for b in range(bands):
        pieces = [parts_ref[s * rows + b * per:s * rows + (b + 1) * per, :] for s in range(nx)]
        for j in range(nx):
            total = turn(pieces[0], -width * j)
            for s in range(1, nx):
                total = jnp.where(group == s, turn(pieces[s], width * (s - j)), total)
            out_ref[(b * nx + j) * per:(b * nx + j + 1) * per, :] = total


def add_over(x, axes):
    swapped = lax.all_to_all(x, axes, 0, 0, tiled=True)
    return swapped.reshape((lax.axis_size(axes), -1) + x.shape[1:]).sum(0)


def copy_over(x, axes):
    count = lax.axis_size(axes)
    spread = jnp.broadcast_to(x[None], (count,) + x.shape).reshape((-1,) + x.shape[1:])
    return lax.all_to_all(spread, axes, 0, 0, tiled=True)


def per_device(
    timestream, pointing, detector_band, mode_loading, mode_mix, noise_weight, ownership
):
    dets, times = timestream.shape
    bands, modes = mode_mix.shape[:2]
    pad = -(-bands // 8) * 8
    tiles = ownership.shape[0]
    nx, nh, nl = lax.axis_size("x"), lax.axis_size("zh"), lax.axis_size("zl")
    nz = nh * nl
    nt = lax.axis_size("y") * lax.axis_size("core")
    vmem = pl.BlockSpec(memory_space=pltpu.VMEM)
    smem = pl.BlockSpec(memory_space=pltpu.SMEM)
    params = pltpu.CompilerParams(vmem_limit_bytes=32 * 1024 * 1024)

    def call(kernel, shapes, args, specs=None, scratch=(), cost=None, limit=params):
        return pl.pallas_call(
            kernel,
            out_shape=tuple(jax.ShapeDtypeStruct(s, F32) for s in shapes),
            in_specs=specs or [vmem] * len(args),
            out_specs=tuple(vmem for _ in shapes),
            scratch_shapes=scratch,
            compiler_params=limit,
            cost_estimate=cost,
        )(*args)

    inputs = (mode_loading.T, detector_band[None, :], noise_weight[None, :], timestream, pointing)
    (packed,) = call(
        functools.partial(pack_kernel, nx),
        [(nx * (dets + EXTRA), 128)],
        inputs,
        specs=[pl.BlockSpec(memory_space=pltpu.HBM)] * 5,
        scratch=[pltpu.VMEM(a.shape, a.dtype) for a in inputs] + [pltpu.SemaphoreType.DMA((5,))],
        limit=None,
    )
    got = lax.all_to_all(packed, "x", 0, 0, tiled=True)
    (local,) = call(
        functools.partial(project_kernel, nx, modes, pad), [(nz * pad, 128)], (got,)
    )
    share = add_over(local, "zl")
    share = copy_over(share, "zh").reshape((nh,) + share.shape).sum(0)
    projected = copy_over(share, "zl")
    amp, plus, minus, hi, lo = call(
        functools.partial(fit_kernel, nx, bands, pad),
        [(bands * modes, 128)] + [(dets, times)] * 4,
        (projected, mode_mix, got),
    )
    gathered = lax.all_to_all(amp, "x", 0, 0, tiled=True)
    (part,) = call(
        bin_kernel,
        [(tiles, TILE_PIX)],
        (ownership, plus, minus, hi, lo),
        specs=[smem] + [vmem] * 4,
        scratch=[pltpu.VMEM((2, HALF, TILE_PIX), F32)],
        cost=pl.CostEstimate(flops=4 * dets * times * HALF * HALF, bytes_accessed=1 << 19, transcendentals=0),
    )
    part, gathered = lax.optimization_barrier((part, gathered))
    share = add_over(part, ("x", "zh", "zl"))
    sky_map = copy_over(share, ("y", "core")).reshape((nt,) + share.shape).sum(0)
    (amplitudes,) = call(
        functools.partial(gather_kernel, nx, bands), [(bands * modes, times)], (gathered,)
    )
    return amplitudes, sky_map


def solution(mesh):
    fine = Mesh(mesh.devices.reshape(4, 4, 4, 4, 2), ("x", "zh", "zl", "y", "core"))
    det, tm = ("x", "zh", "zl"), ("y", "core")
    placed = (P(det, tm), P(det, tm), P(det), P(det, None), P(), P(det), P())
    return jax.shard_map(
        per_device,
        mesh=fine,
        in_specs=placed,
        out_specs=(P(None, tm), P(det, None)),
        check_vma=False,
    )
```

```python
import functools

import jax
import jax.numpy as jnp
from jax import lax
from jax.experimental import pallas as pl
from jax.experimental.pallas import tpu as pltpu
from jax.sharding import Mesh, PartitionSpec as P

TILE_PIX = 128
HALF = 256
GROUP = 8
EXTRA = 8
F32 = jnp.float32
BF16 = jnp.bfloat16


def lanes(rows, width):
    return lax.broadcasted_iota(jnp.int32, (rows, 128), 1) // width


def turn(x, amount):
    amount %= 128
    return pltpu.roll(x, amount, 1) if amount else x


def split(x):
    high = x.astype(BF16)
    low = (x - high.astype(F32)).astype(BF16)
    return high, low


def pack_kernel(nx, *refs):
    sources, (out_ref, *held, sems) = refs[:5], refs[5:]
    copies = [
        pltpu.make_async_copy(src, dst, sems.at[n]) for n, (src, dst) in enumerate(zip(sources, held))
    ]
    for copy in copies:
        copy.start()
    for copy in copies:
        copy.wait()
    loading_t_ref, band_ref, noise_ref, ts_ref, point_ref = held
    modes, dets = loading_t_ref.shape
    width = ts_ref.shape[1] // nx
    rows = dets + EXTRA
    ts = ts_ref[...].astype(F32)
    point = point_ref[...].astype(F32)
    loading_t = loading_t_ref[...].astype(F32)
    loading = jnp.concatenate([jnp.zeros((128 - modes, dets), F32), loading_t], axis=0).T
    group = lanes(dets, width)
    for d in range(nx):
        body = jnp.where(group == 0, turn(ts, -width * d), turn(point, width - width * d))
        out_ref[d * rows:d * rows + dets, :] = jnp.where(group < 2, body, loading)
        out_ref[d * rows + dets:(d + 1) * rows, :] = jnp.concatenate(
            [band_ref[...].astype(F32), noise_ref[...], jnp.zeros((EXTRA - 2, dets), F32)], axis=0
        )


def project_kernel(nx, modes, pad, got_ref, out_ref):
    rows = got_ref.shape[0] // nx
    dets = rows - EXTRA
    width = 128 // nx
    per = modes * width // 128
    group = lanes(dets, width)
    slot = lax.broadcasted_iota(jnp.int32, (pad, dets), 0).astype(F32)
    left, right = [], []
    for s in range(nx):
        chunk = got_ref[s * rows:s * rows + dets, :]
        loading_t = chunk.T[128 - modes:, :]
        ts = jnp.where(group == 0, chunk, 0.0)
        pick = jnp.where(slot == got_ref[s * rows + dets:s * rows + dets + 1, :], 1.0, 0.0)
        for j in range(modes // per):
            part = loading_t[j * per:(j + 1) * per, :]
            left.append((part[:, None, :] * pick[None]).reshape(per * pad, dets).astype(BF16))
            right.append(turn(ts, width * j).astype(BF16))
    out_ref[...] = jnp.dot(
        jnp.concatenate(left, axis=1), jnp.concatenate(right, axis=0), preferred_element_type=F32
    )


def row(ref, i, times):
    return jnp.broadcast_to(ref[pl.ds(i, 1), :], (16, times)).astype(BF16)[None]


def add_bins(value_ref, hi_ref, lo_ref, acc_ref):
    dets, times = value_ref.shape
    ids = lax.broadcasted_iota(jnp.int32, (HALF, times), 0).astype(F32).astype(BF16)
    ids = ids.reshape(HALF // 16, 16, times)
    one = jnp.ones((), BF16)
    zero = jnp.zeros((), BF16)

    def body(g, carry):
        left, right = [], []
        for k in range(GROUP):
            i = g * GROUP + k
            upper = row(hi_ref, i, times) == ids
            lower = row(lo_ref, i, times) == ids
            left.append(jnp.where(upper, one, zero).reshape(HALF, times))
            right.append(jnp.where(lower, row(value_ref, i, times), zero).reshape(HALF, times))
        added = lax.dot_general(
            jnp.concatenate(left, axis=1),
            jnp.concatenate(right, axis=1),
            (((1,), (1,)), ((), ())),
            preferred_element_type=F32,
        )
        acc_ref[:HALF, :] += added[:, :TILE_PIX]
        acc_ref[HALF:, :] += added[:, TILE_PIX:]
        return carry

    lax.fori_loop(0, dets // GROUP, body, 0, unroll=4)


def weighted_kernel(
    nx, bands, modes, got_ref, wide_ref, noise_ref, hi_ref, lo_ref, acc_ref, value_s
):
    rows = got_ref.shape[0] // nx
    dets = rows - EXTRA
    width = 128 // nx
    group = lanes(dets, width)
    half = lanes(dets, modes)
    for s in range(nx):
        chunk = got_ref[s * rows:s * rows + dets, :]
        tail = got_ref[s * rows + dets:(s + 1) * rows, :]
        columns = jnp.concatenate([tail, jnp.zeros((128 - EXTRA, dets), F32)], axis=0).T
        band_off = jnp.broadcast_to(columns[:, 0:1], (dets, 128)) - half.astype(F32)
        loading2 = jnp.where(half == 0, turn(chunk, modes), chunk)
        for b in range(0, bands, 2):
            wide_ref[s * dets:(s + 1) * dets, b * modes:(b + 2) * modes] = jnp.where(
                band_off == float(b), loading2, 0.0
            ).astype(BF16)
        here = (
            jnp.broadcast_to(columns[:, 1:2], (dets, 128)),
            turn(chunk, width * s),
            turn(chunk, width * (s - 1)),
        )
        total = here if s == 0 else tuple(
            jnp.where(group == s, a, b) for a, b in zip(here, total)
        )
    noise, ts, point = total
    noise_ref[...] = noise
    value_s[...] = (noise * ts).astype(BF16).astype(F32)
    point = point.astype(jnp.int32)
    hi_ref[...] = (point >> 8).astype(F32)
    lo_ref[...] = (point & 255).astype(F32)
    acc_ref[...] = jnp.zeros_like(acc_ref)
    add_bins(value_s, hi_ref, lo_ref, acc_ref)


def correct_kernel(
    nx, bands, pad, own_ref, proj_ref, mix_ref, wide_ref, noise_ref, hi_ref, lo_ref, start_ref,
    amp_ref, map_ref, value_s, acc_s
):
    modes = mix_ref.shape[1]
    dets = noise_ref.shape[0]
    width = 128 // nx
    per = modes // nx
    group = lanes(per, width)
    rounded = []
    for b in range(bands):
        mine = proj_ref[pl.ds(b, per, stride=pad), :]
        turned = [turn(mine, width * k) for k in range(nx)]
        pieces = []
        for j in range(nx):
            piece = turned[(0 - j) % nx]
            for g in range(1, nx):
                piece = jnp.where(group == g, turned[(g - j) % nx], piece)
            pieces.append(piece)
        p = jnp.concatenate(pieces, axis=0)
        mh, ml = split(mix_ref[b])
        ph, plow = split(p)
        amp = p + jnp.dot(
            jnp.concatenate([mh, ml, mh], axis=1),
            jnp.concatenate([ph, ph, plow], axis=0),
            preferred_element_type=F32,
        )
        rounded.append(amp.astype(BF16))
        packed = amp[:per, :]
        for j in range(1, nx):
            packed = jnp.where(group == j, amp[j * per:(j + 1) * per, :], packed)
        amp_ref[b * per:(b + 1) * per, :] = packed
    fits = jnp.dot(wide_ref[...], jnp.concatenate(rounded, axis=0), preferred_element_type=F32)
    group = lanes(dets, width)
    fitted = fits[:dets, :]
    for s in range(1, nx):
        fitted = jnp.where(group == s, fits[s * dets:(s + 1) * dets, :], fitted)
    value_s[...] = -(noise_ref[...] * fitted).astype(BF16).astype(F32)
    acc_s[...] = start_ref[...]
    add_bins(value_s, hi_ref, lo_ref, acc_s)
    for r in range(map_ref.shape[0]):
        tile = own_ref[r]
        map_ref[r:r + 1, :] = acc_s[pl.ds((tile & 1) * HALF + (tile >> 1), 1), :]


def gather_kernel(nx, bands, *refs):
    parts, out_ref = refs[:nx], refs[nx]
    per = parts[0].shape[0] // bands
    width = 128 // nx
    group = lanes(per, width)
    mine = lax.axis_index("x")
    sources = [lax.rem(mine + nx - k, nx) for k in range(nx)]
    for b in range(bands):
        for j in range(nx):
            total = jnp.zeros((per, 128), F32)
            for k in range(nx):
                piece = parts[k][b * per:(b + 1) * per, :]
                moved = pltpu.roll(piece, lax.rem(sources[k] + nx - j, nx) * width, 1)
                total = jnp.where(group == sources[k], moved, total)
            out_ref[(b * nx + j) * per:(b * nx + j + 1) * per, :] = total


def add_over(x, axes):
    swapped = lax.all_to_all(x, axes, 0, 0, tiled=True)
    return swapped.reshape((lax.axis_size(axes), -1) + x.shape[1:]).sum(0)


def copy_over(x, axes):
    count = lax.axis_size(axes)
    spread = jnp.broadcast_to(x[None], (count,) + x.shape).reshape((-1,) + x.shape[1:])
    return lax.all_to_all(spread, axes, 0, 0, tiled=True)


def per_device(
    timestream, pointing, detector_band, mode_loading, mode_mix, noise_weight, ownership
):
    dets, times = timestream.shape
    bands, modes = mode_mix.shape[:2]
    pad = -(-bands // 8) * 8
    tiles = ownership.shape[0]
    nx, nh, nl = lax.axis_size("x"), lax.axis_size("zh"), lax.axis_size("zl")
    nz = nh * nl
    nt = lax.axis_size("y") * lax.axis_size("core")
    vmem = pl.BlockSpec(memory_space=pltpu.VMEM)
    smem = pl.BlockSpec(memory_space=pltpu.SMEM)
    params = pltpu.CompilerParams(vmem_limit_bytes=32 * 1024 * 1024)

    bin_cost = pl.CostEstimate(
        flops=2 * dets * times * HALF * HALF, bytes_accessed=1 << 21, transcendentals=0
    )

    def call(kernel, shapes, args, specs=None, scratch=(), cost=None, limit=params, types=None):
        return pl.pallas_call(
            kernel,
            out_shape=tuple(
                jax.ShapeDtypeStruct(s, t) for s, t in zip(shapes, types or [F32] * len(shapes))
            ),
            in_specs=specs or [vmem] * len(args),
            out_specs=tuple(vmem for _ in shapes),
            scratch_shapes=scratch,
            compiler_params=limit,
            cost_estimate=cost,
        )(*args)

    inputs = (mode_loading.T, detector_band[None, :], noise_weight[None, :], timestream, pointing)
    (packed,) = call(
        functools.partial(pack_kernel, nx),
        [(nx * (dets + EXTRA), 128)],
        inputs,
        specs=[pl.BlockSpec(memory_space=pltpu.HBM)] * 5,
        scratch=[pltpu.VMEM(a.shape, a.dtype) for a in inputs] + [pltpu.SemaphoreType.DMA((5,))],
        limit=None,
    )
    got = lax.all_to_all(packed, "x", 0, 0, tiled=True)
    (local,) = call(
        functools.partial(project_kernel, nx, modes, pad), [(nz * pad, 128)], (got,)
    )
    share, got = lax.optimization_barrier((add_over(local, "zl"), got))
    wide, noise, hi, lo, start = call(
        functools.partial(weighted_kernel, nx, bands, modes),
        [(nx * dets, bands * modes)] + [(dets, times)] * 3 + [(2 * HALF, TILE_PIX)],
        (got,),
        scratch=[pltpu.VMEM((dets, times), F32)],
        cost=bin_cost,
        types=[BF16] + [F32] * 4,
    )
    share = copy_over(share, "zh").reshape((nh,) + share.shape).sum(0)
    share, wide, noise, hi, lo, start = lax.optimization_barrier((share, wide, noise, hi, lo, start))
    projected = copy_over(share, "zl")
    amp, part = call(
        functools.partial(correct_kernel, nx, bands, pad),
        [(bands * modes // nx, 128), (tiles, TILE_PIX)],
        (ownership, projected, mode_mix, wide, noise, hi, lo, start),
        specs=[smem] + [vmem] * 7,
        scratch=[pltpu.VMEM((dets, times), F32), pltpu.VMEM((2 * HALF, TILE_PIX), F32)],
        cost=bin_cost,
    )
    moved = [
        lax.ppermute(amp, "x", [(i, (i + k) % nx) for i in range(nx)]) for k in range(1, nx)
    ]
    (amplitudes,) = call(
        functools.partial(gather_kernel, nx, bands), [(bands * modes, times)], (amp, *moved)
    )
    share = add_over(part, ("x", "zh", "zl"))
    share, amplitudes = lax.optimization_barrier((share, amplitudes))
    sky_map = copy_over(share, ("y", "core")).reshape((nt,) + share.shape).sum(0)
    return amplitudes, sky_map


def solution(mesh):
    fine = Mesh(mesh.devices.reshape(4, 4, 4, 4, 2), ("x", "zh", "zl", "y", "core"))
    det, tm = ("x", "zh", "zl"), ("y", "core")
    placed = (P(det, tm), P(det, tm), P(det), P(det, None), P(), P(det), P())
    return jax.shard_map(
        per_device,
        mesh=fine,
        in_specs=placed,
        out_specs=(P(None, tm), P(det, None)),
        check_vma=False,
    )
```

```python
import functools

import jax
import jax.numpy as jnp
from jax import lax
from jax.experimental import pallas as pl
from jax.experimental.pallas import tpu as pltpu
from jax.sharding import Mesh, PartitionSpec as P

TILE_PIX = 128
HALF = 256
GROUP = 8
EXTRA = 8
F32 = jnp.float32
BF16 = jnp.bfloat16


def lanes(rows, width):
    return lax.broadcasted_iota(jnp.int32, (rows, 128), 1) // width


def turn(x, amount):
    amount %= 128
    return pltpu.roll(x, amount, 1) if amount else x


def split(x):
    high = x.astype(BF16)
    low = (x - high.astype(F32)).astype(BF16)
    return high, low


def pack_kernel(nx, *refs):
    sources, (out_ref, *held, sems) = refs[:5], refs[5:]
    copies = [
        pltpu.make_async_copy(src, dst, sems.at[n]) for n, (src, dst) in enumerate(zip(sources, held))
    ]
    for copy in copies:
        copy.start()
    for copy in copies:
        copy.wait()
    loading_t_ref, band_ref, noise_ref, ts_ref, point_ref = held
    modes, dets = loading_t_ref.shape
    width = ts_ref.shape[1] // nx
    rows = dets + EXTRA
    ts = ts_ref[...].astype(F32)
    point = point_ref[...].astype(F32)
    loading_t = loading_t_ref[...].astype(F32)
    loading = jnp.concatenate([jnp.zeros((128 - modes, dets), F32), loading_t], axis=0).T
    group = lanes(dets, width)
    for d in range(nx):
        body = jnp.where(group == 0, turn(ts, -width * d), turn(point, width - width * d))
        out_ref[d * rows:d * rows + dets, :] = jnp.where(group < 2, body, loading)
        out_ref[d * rows + dets:(d + 1) * rows, :] = jnp.concatenate(
            [band_ref[...].astype(F32), noise_ref[...], jnp.zeros((EXTRA - 2, dets), F32)], axis=0
        )


def project_kernel(nx, modes, pad, got_ref, out_ref):
    rows = got_ref.shape[0] // nx
    dets = rows - EXTRA
    width = 128 // nx
    per = modes * width // 128
    group = lanes(dets, width)
    slot = lax.broadcasted_iota(jnp.int32, (pad, dets), 0).astype(F32)
    left, right = [], []
    for s in range(nx):
        chunk = got_ref[s * rows:s * rows + dets, :]
        loading_t = chunk.T[128 - modes:, :]
        ts = jnp.where(group == 0, chunk, 0.0)
        pick = jnp.where(slot == got_ref[s * rows + dets:s * rows + dets + 1, :], 1.0, 0.0)
        for j in range(modes // per):
            part = loading_t[j * per:(j + 1) * per, :]
            left.append((part[:, None, :] * pick[None]).reshape(per * pad, dets).astype(BF16))
            right.append(turn(ts, width * j).astype(BF16))
    out_ref[...] = jnp.dot(
        jnp.concatenate(left, axis=1), jnp.concatenate(right, axis=0), preferred_element_type=F32
    )


def row(ref, i, times):
    return jnp.broadcast_to(ref[pl.ds(i, 1), :], (16, times)).astype(BF16)[None]


def add_bins(value_ref, hi_ref, lo_ref, acc_ref):
    dets, times = value_ref.shape
    ids = lax.broadcasted_iota(jnp.int32, (HALF, times), 0).astype(F32).astype(BF16)
    ids = ids.reshape(HALF // 16, 16, times)
    one = jnp.ones((), BF16)
    zero = jnp.zeros((), BF16)

    def body(g, carry):
        left, right = [], []
        for k in range(GROUP):
            i = g * GROUP + k
            upper = row(hi_ref, i, times) == ids
            lower = row(lo_ref, i, times) == ids
            left.append(jnp.where(upper, one, zero).reshape(HALF, times))
            right.append(jnp.where(lower, row(value_ref, i, times), zero).reshape(HALF, times))
        added = lax.dot_general(
            jnp.concatenate(left, axis=1),
            jnp.concatenate(right, axis=1),
            (((1,), (1,)), ((), ())),
            preferred_element_type=F32,
        )
        acc_ref[:HALF, :] += added[:, :TILE_PIX]
        acc_ref[HALF:, :] += added[:, TILE_PIX:]
        return carry

    lax.fori_loop(0, dets // GROUP, body, 0, unroll=4)


def weighted_kernel(
    nx, bands, modes, got_ref, wide_ref, noise_ref, hi_ref, lo_ref, acc_ref, value_s
):
    rows = got_ref.shape[0] // nx
    dets = rows - EXTRA
    width = 128 // nx
    group = lanes(dets, width)
    half = lanes(dets, modes)
    for s in range(nx):
        chunk = got_ref[s * rows:s * rows + dets, :]
        tail = got_ref[s * rows + dets:(s + 1) * rows, :]
        columns = jnp.concatenate([tail, jnp.zeros((128 - EXTRA, dets), F32)], axis=0).T
        band_off = jnp.broadcast_to(columns[:, 0:1], (dets, 128)) - half.astype(F32)
        loading2 = jnp.where(half == 0, turn(chunk, modes), chunk)
        for b in range(0, bands, 2):
            wide_ref[s * dets:(s + 1) * dets, b * modes:(b + 2) * modes] = jnp.where(
                band_off == float(b), loading2, 0.0
            ).astype(BF16)
        here = (
            jnp.broadcast_to(columns[:, 1:2], (dets, 128)),
            turn(chunk, width * s),
            turn(chunk, width * (s - 1)),
        )
        total = here if s == 0 else tuple(
            jnp.where(group == s, a, b) for a, b in zip(here, total)
        )
    noise, ts, point = total
    noise_ref[...] = noise
    value_s[...] = (noise * ts).astype(BF16).astype(F32)
    point = point.astype(jnp.int32)
    hi_ref[...] = (point >> 8).astype(F32)
    lo_ref[...] = (point & 255).astype(F32)
    acc_ref[...] = jnp.zeros_like(acc_ref)
    add_bins(value_s, hi_ref, lo_ref, acc_ref)


def correct_kernel(
    nx, bands, pad, own_ref, proj_ref, mix_ref, wide_ref, noise_ref, hi_ref, lo_ref, start_ref,
    amp_ref, map_ref, value_s, acc_s
):
    modes = mix_ref.shape[1]
    dets = noise_ref.shape[0]
    width = 128 // nx
    per = modes // nx
    group = lanes(per, width)
    rounded = []
    for b in range(bands):
        mine = proj_ref[pl.ds(b, per, stride=pad), :]
        turned = [turn(mine, width * k) for k in range(nx)]
        pieces = []
        for j in range(nx):
            piece = turned[(0 - j) % nx]
            for g in range(1, nx):
                piece = jnp.where(group == g, turned[(g - j) % nx], piece)
            pieces.append(piece)
        p = jnp.concatenate(pieces, axis=0)
        mh, ml = split(mix_ref[b])
        ph, plow = split(p)
        amp = p + jnp.dot(
            jnp.concatenate([mh, ml, mh], axis=1),
            jnp.concatenate([ph, ph, plow], axis=0),
            preferred_element_type=F32,
        )
        rounded.append(amp.astype(BF16))
        packed = amp[:per, :]
        for j in range(1, nx):
            packed = jnp.where(group == j, amp[j * per:(j + 1) * per, :], packed)
        for copy in range(2):
            at = (copy * bands + b) * per
            amp_ref[at:at + per, :] = packed
    fits = jnp.dot(wide_ref[...], jnp.concatenate(rounded, axis=0), preferred_element_type=F32)
    group = lanes(dets, width)
    fitted = fits[:dets, :]
    for s in range(1, nx):
        fitted = jnp.where(group == s, fits[s * dets:(s + 1) * dets, :], fitted)
    value_s[...] = -(noise_ref[...] * fitted).astype(BF16).astype(F32)
    acc_s[...] = start_ref[...]
    add_bins(value_s, hi_ref, lo_ref, acc_s)
    for r in range(map_ref.shape[0]):
        tile = own_ref[r]
        map_ref[r:r + 1, :] = acc_s[pl.ds((tile & 1) * HALF + (tile >> 1), 1), :]


def gather_kernel(nx, bands, parts_ref, out_ref, held, sems):
    rows = held.shape[0] // nx
    copies = [
        pltpu.make_async_copy(
            parts_ref.at[pl.ds(2 * s * rows, rows), :], held.at[pl.ds(s * rows, rows), :], sems.at[s]
        )
        for s in range(nx)
    ]
    for copy in copies:
        copy.start()
    for copy in copies:
        copy.wait()
    per = rows // bands
    width = 128 // nx
    group = lanes(per, width)
    for b in range(bands):
        pieces = [held[s * rows + b * per:s * rows + (b + 1) * per, :] for s in range(nx)]
        for j in range(nx):
            total = turn(pieces[0], -width * j)
            for s in range(1, nx):
                total = jnp.where(group == s, turn(pieces[s], width * (s - j)), total)
            out_ref[(b * nx + j) * per:(b * nx + j + 1) * per, :] = total


def add_over(x, axes):
    swapped = lax.all_to_all(x, axes, 0, 0, tiled=True)
    return swapped.reshape((lax.axis_size(axes), -1) + x.shape[1:]).sum(0)


def copy_over(x, axes):
    count = lax.axis_size(axes)
    spread = jnp.broadcast_to(x[None], (count,) + x.shape).reshape((-1,) + x.shape[1:])
    return lax.all_to_all(spread, axes, 0, 0, tiled=True)


def per_device(
    timestream, pointing, detector_band, mode_loading, mode_mix, noise_weight, ownership
):
    dets, times = timestream.shape
    bands, modes = mode_mix.shape[:2]
    pad = -(-bands // 8) * 8
    tiles = ownership.shape[0]
    nx, nh, nl = lax.axis_size("x"), lax.axis_size("zh"), lax.axis_size("zl")
    nz = nh * nl
    nt = lax.axis_size("y") * lax.axis_size("core")
    vmem = pl.BlockSpec(memory_space=pltpu.VMEM)
    smem = pl.BlockSpec(memory_space=pltpu.SMEM)
    params = pltpu.CompilerParams(vmem_limit_bytes=32 * 1024 * 1024)

    bin_cost = pl.CostEstimate(
        flops=2 * dets * times * HALF * HALF, bytes_accessed=1 << 21, transcendentals=0
    )

    def call(kernel, shapes, args, specs=None, scratch=(), cost=None, limit=params, types=None):
        return pl.pallas_call(
            kernel,
            out_shape=tuple(
                jax.ShapeDtypeStruct(s, t) for s, t in zip(shapes, types or [F32] * len(shapes))
            ),
            in_specs=specs or [vmem] * len(args),
            out_specs=tuple(vmem for _ in shapes),
            scratch_shapes=scratch,
            compiler_params=limit,
            cost_estimate=cost,
        )(*args)

    inputs = (mode_loading.T, detector_band[None, :], noise_weight[None, :], timestream, pointing)
    (packed,) = call(
        functools.partial(pack_kernel, nx),
        [(nx * (dets + EXTRA), 128)],
        inputs,
        specs=[pl.BlockSpec(memory_space=pltpu.HBM)] * 5,
        scratch=[pltpu.VMEM(a.shape, a.dtype) for a in inputs] + [pltpu.SemaphoreType.DMA((5,))],
        limit=None,
    )
    got = lax.all_to_all(packed, "x", 0, 0, tiled=True)
    (local,) = call(
        functools.partial(project_kernel, nx, modes, pad), [(nz * pad, 128)], (got,)
    )
    share, got = lax.optimization_barrier((add_over(local, "zl"), got))
    wide, noise, hi, lo, start = call(
        functools.partial(weighted_kernel, nx, bands, modes),
        [(nx * dets, bands * modes)] + [(dets, times)] * 3 + [(2 * HALF, TILE_PIX)],
        (got,),
        scratch=[pltpu.VMEM((dets, times), F32)],
        cost=bin_cost,
        types=[BF16] + [F32] * 4,
    )
    share = copy_over(share, "zh").reshape((nh,) + share.shape).sum(0)
    share, wide, noise, hi, lo, start = lax.optimization_barrier((share, wide, noise, hi, lo, start))
    projected = copy_over(share, "zl")
    amp, part = call(
        functools.partial(correct_kernel, nx, bands, pad),
        [(2 * bands * modes // nx, 128), (tiles, TILE_PIX)],
        (ownership, projected, mode_mix, wide, noise, hi, lo, start),
        specs=[smem] + [vmem] * 7,
        scratch=[pltpu.VMEM((dets, times), F32), pltpu.VMEM((2 * HALF, TILE_PIX), F32)],
        cost=bin_cost,
    )
    gathered = lax.all_gather(amp, "x", axis=0, tiled=True)
    share = add_over(part, ("x", "zh", "zl"))
    sky_map = copy_over(share, ("y", "core")).reshape((nt,) + share.shape).sum(0)
    (amplitudes,) = call(
        functools.partial(gather_kernel, nx, bands),
        [(bands * modes, times)],
        (gathered,),
        specs=[pl.BlockSpec(memory_space=pltpu.HBM)],
        scratch=[pltpu.VMEM((bands * modes, 128), F32), pltpu.SemaphoreType.DMA((nx,))],
        limit=None,
    )
    return amplitudes, sky_map


def solution(mesh):
    fine = Mesh(mesh.devices.reshape(4, 4, 4, 4, 2), ("x", "zh", "zl", "y", "core"))
    det, tm = ("x", "zh", "zl"), ("y", "core")
    placed = (P(det, tm), P(det, tm), P(det), P(det, None), P(), P(det), P())
    return jax.shard_map(
        per_device,
        mesh=fine,
        in_specs=placed,
        out_specs=(P(None, tm), P(det, None)),
        check_vma=False,
    )
```

```python
import functools

import jax
import jax.numpy as jnp
from jax import lax
from jax.experimental import pallas as pl
from jax.experimental.pallas import tpu as pltpu
from jax.sharding import Mesh, PartitionSpec as P

TILE_PIX = 128
HALF = 256
GROUP = 8
EXTRA = 8
F32 = jnp.float32
BF16 = jnp.bfloat16


def lanes(rows, width):
    return lax.broadcasted_iota(jnp.int32, (rows, 128), 1) // width


def turn(x, amount):
    amount %= 128
    return pltpu.roll(x, amount, 1) if amount else x


def split(x):
    high = x.astype(BF16)
    low = (x - high.astype(F32)).astype(BF16)
    return high, low


def pack_kernel(nx, *refs):
    sources, (out_ref, *held, sems) = refs[:5], refs[5:]
    copies = [
        pltpu.make_async_copy(src, dst, sems.at[n]) for n, (src, dst) in enumerate(zip(sources, held))
    ]
    for copy in copies:
        copy.start()
    for copy in copies:
        copy.wait()
    loading_t_ref, band_ref, noise_ref, ts_ref, point_ref = held
    modes, dets = loading_t_ref.shape
    width = ts_ref.shape[1] // nx
    rows = dets + EXTRA
    ts = ts_ref[...].astype(F32)
    point = point_ref[...].astype(F32)
    loading_t = loading_t_ref[...].astype(F32)
    loading = jnp.concatenate([jnp.zeros((128 - modes, dets), F32), loading_t], axis=0).T
    group = lanes(dets, width)
    for d in range(nx):
        body = jnp.where(group == 0, turn(ts, -width * d), turn(point, width - width * d))
        out_ref[d * rows:d * rows + dets, :] = jnp.where(group < 2, body, loading)
        out_ref[d * rows + dets:(d + 1) * rows, :] = jnp.concatenate(
            [band_ref[...].astype(F32), noise_ref[...], jnp.zeros((EXTRA - 2, dets), F32)], axis=0
        )


def project_kernel(nx, modes, pad, got_ref, out_ref):
    rows = got_ref.shape[0] // nx
    dets = rows - EXTRA
    width = 128 // nx
    per = modes * width // 128
    group = lanes(dets, width)
    slot = lax.broadcasted_iota(jnp.int32, (pad, dets), 0).astype(F32)
    left, right = [], []
    for s in range(nx):
        chunk = got_ref[s * rows:s * rows + dets, :]
        loading_t = chunk.T[128 - modes:, :]
        ts = jnp.where(group == 0, chunk, 0.0)
        pick = jnp.where(slot == got_ref[s * rows + dets:s * rows + dets + 1, :], 1.0, 0.0)
        for j in range(modes // per):
            part = loading_t[j * per:(j + 1) * per, :]
            left.append((part[:, None, :] * pick[None]).reshape(per * pad, dets).astype(BF16))
            right.append(turn(ts, width * j).astype(BF16))
    out_ref[...] = jnp.dot(
        jnp.concatenate(left, axis=1), jnp.concatenate(right, axis=0), preferred_element_type=F32
    )


def row(ref, i, times):
    return jnp.broadcast_to(ref[pl.ds(i, 1), :], (16, times)).astype(BF16)[None]


def add_bins(value_ref, hi_ref, lo_ref, acc_ref):
    dets, times = value_ref.shape
    ids = lax.broadcasted_iota(jnp.int32, (HALF, times), 0).astype(F32).astype(BF16)
    ids = ids.reshape(HALF // 16, 16, times)
    one = jnp.ones((), BF16)
    zero = jnp.zeros((), BF16)

    def body(g, carry):
        left, right = [], []
        for k in range(GROUP):
            i = g * GROUP + k
            upper = row(hi_ref, i, times) == ids
            lower = row(lo_ref, i, times) == ids
            left.append(jnp.where(upper, one, zero).reshape(HALF, times))
            right.append(jnp.where(lower, row(value_ref, i, times), zero).reshape(HALF, times))
        added = lax.dot_general(
            jnp.concatenate(left, axis=1),
            jnp.concatenate(right, axis=1),
            (((1,), (1,)), ((), ())),
            preferred_element_type=F32,
        )
        acc_ref[:HALF, :] += added[:, :TILE_PIX]
        acc_ref[HALF:, :] += added[:, TILE_PIX:]
        return carry

    lax.fori_loop(0, dets // GROUP, body, 0, unroll=4)


def sum_kernel(count, parts_ref, out_ref):
    rows = parts_ref.shape[0] // count
    total = parts_ref[:rows, :]
    for s in range(1, count):
        total = total + parts_ref[s * rows:(s + 1) * rows, :]
    for s in range(out_ref.shape[0] // rows):
        out_ref[s * rows:(s + 1) * rows, :] = total


def weighted_kernel(
    nx, bands, modes, got_ref, own_ref, wide_ref, noise_ref, hi_ref, lo_ref, acc_ref, place_ref, value_s
):
    tiles = place_ref.shape[0]
    own = own_ref[...]
    own = jnp.broadcast_to(((own & 1) * HALF + (own >> 1)).astype(F32), (128, tiles))
    step = min(128, tiles)
    source = lax.broadcasted_iota(jnp.int32, (step, 2 * HALF), 1).astype(F32)
    for r in range(0, tiles, step):
        here = own[:, r:r + step].T[:, 0:1]
        place_ref[r:r + step, :] = jnp.where(
            jnp.broadcast_to(here, (step, 2 * HALF)) == source, 1.0, 0.0
        ).astype(BF16)
    rows = got_ref.shape[0] // nx
    dets = rows - EXTRA
    width = 128 // nx
    group = lanes(dets, width)
    half = lanes(dets, modes)
    for s in range(nx):
        chunk = got_ref[s * rows:s * rows + dets, :]
        tail = got_ref[s * rows + dets:(s + 1) * rows, :]
        columns = jnp.concatenate([tail, jnp.zeros((128 - EXTRA, dets), F32)], axis=0).T
        band_off = jnp.broadcast_to(columns[:, 0:1], (dets, 128)) - half.astype(F32)
        loading2 = jnp.where(half == 0, turn(chunk, modes), chunk)
        for b in range(0, bands, 2):
            wide_ref[s * dets:(s + 1) * dets, b * modes:(b + 2) * modes] = jnp.where(
                band_off == float(b), loading2, 0.0
            ).astype(BF16)
        here = (
            jnp.broadcast_to(columns[:, 1:2], (dets, 128)),
            turn(chunk, width * s),
            turn(chunk, width * (s - 1)),
        )
        total = here if s == 0 else tuple(
            jnp.where(group == s, a, b) for a, b in zip(here, total)
        )
    noise, ts, point = total
    noise_ref[...] = noise
    value_s[...] = (noise * ts).astype(BF16).astype(F32)
    point = point.astype(jnp.int32)
    hi_ref[...] = (point >> 8).astype(F32)
    lo_ref[...] = (point & 255).astype(F32)
    acc_ref[...] = jnp.zeros_like(acc_ref)
    add_bins(value_s, hi_ref, lo_ref, acc_ref)


def correct_kernel(
    nx, bands, pad, proj_ref, mix_ref, wide_ref, noise_ref, hi_ref, lo_ref, start_ref, place_ref,
    amp_ref, map_ref, value_s, acc_s
):
    modes = mix_ref.shape[1]
    dets = noise_ref.shape[0]
    width = 128 // nx
    per = modes // nx
    group = lanes(per, width)
    rounded = []
    for b in range(bands):
        mine = proj_ref[pl.ds(b, per, stride=pad), :]
        turned = [turn(mine, width * k) for k in range(nx)]
        pieces = []
        for j in range(nx):
            piece = turned[(0 - j) % nx]
            for g in range(1, nx):
                piece = jnp.where(group == g, turned[(g - j) % nx], piece)
            pieces.append(piece)
        p = jnp.concatenate(pieces, axis=0)
        mh, ml = split(mix_ref[b])
        ph, plow = split(p)
        amp = p + jnp.dot(
            jnp.concatenate([mh, ml, mh], axis=1),
            jnp.concatenate([ph, ph, plow], axis=0),
            preferred_element_type=F32,
        )
        rounded.append(amp.astype(BF16))
        packed = amp[:per, :]
        for j in range(1, nx):
            packed = jnp.where(group == j, amp[j * per:(j + 1) * per, :], packed)
        amp_ref[b * per:(b + 1) * per, :] = packed
    fits = jnp.dot(wide_ref[...], jnp.concatenate(rounded, axis=0), preferred_element_type=F32)
    group = lanes(dets, width)
    fitted = fits[:dets, :]
    for s in range(1, nx):
        fitted = jnp.where(group == s, fits[s * dets:(s + 1) * dets, :], fitted)
    value_s[...] = -(noise_ref[...] * fitted).astype(BF16).astype(F32)
    acc_s[...] = start_ref[...]
    add_bins(value_s, hi_ref, lo_ref, acc_s)
    high, low = split(acc_s[...])
    placed = jnp.dot(place_ref[...], jnp.concatenate([high, low], axis=1), preferred_element_type=F32)
    map_ref[...] = placed[:, :TILE_PIX] + placed[:, TILE_PIX:]


def gather_kernel(nx, bands, *refs):
    parts, out_ref = refs[:nx], refs[nx]
    per = parts[0].shape[0] // bands
    width = 128 // nx
    group = lanes(per, width)
    mine = lax.axis_index("x")
    sources = [lax.rem(mine + nx - k, nx) for k in range(nx)]
    for b in range(bands):
        for j in range(nx):
            total = jnp.zeros((per, 128), F32)
            for k in range(nx):
                piece = parts[k][b * per:(b + 1) * per, :]
                moved = pltpu.roll(piece, lax.rem(sources[k] + nx - j, nx) * width, 1)
                total = jnp.where(group == sources[k], moved, total)
            out_ref[(b * nx + j) * per:(b * nx + j + 1) * per, :] = total


def add_over(x, axes):
    swapped = lax.all_to_all(x, axes, 0, 0, tiled=True)
    return swapped.reshape((lax.axis_size(axes), -1) + x.shape[1:]).sum(0)


def copy_over(x, axes):
    count = lax.axis_size(axes)
    spread = jnp.broadcast_to(x[None], (count,) + x.shape).reshape((-1,) + x.shape[1:])
    return lax.all_to_all(spread, axes, 0, 0, tiled=True)


def per_device(
    timestream, pointing, detector_band, mode_loading, mode_mix, noise_weight, ownership
):
    dets, times = timestream.shape
    bands, modes = mode_mix.shape[:2]
    pad = -(-bands // 8) * 8
    tiles = ownership.shape[0]
    nx, nh, nl = lax.axis_size("x"), lax.axis_size("zh"), lax.axis_size("zl")
    nz = nh * nl
    nt = lax.axis_size("y") * lax.axis_size("core")
    vmem = pl.BlockSpec(memory_space=pltpu.VMEM)
    params = pltpu.CompilerParams(vmem_limit_bytes=32 * 1024 * 1024)

    bin_cost = pl.CostEstimate(
        flops=2 * dets * times * HALF * HALF, bytes_accessed=1 << 21, transcendentals=0
    )

    def call(kernel, shapes, args, specs=None, scratch=(), cost=None, limit=params, types=None):
        return pl.pallas_call(
            kernel,
            out_shape=tuple(
                jax.ShapeDtypeStruct(s, t) for s, t in zip(shapes, types or [F32] * len(shapes))
            ),
            in_specs=specs or [vmem] * len(args),
            out_specs=tuple(vmem for _ in shapes),
            scratch_shapes=scratch,
            compiler_params=limit,
            cost_estimate=cost,
        )(*args)

    inputs = (mode_loading.T, detector_band[None, :], noise_weight[None, :], timestream, pointing)
    (packed,) = call(
        functools.partial(pack_kernel, nx),
        [(nx * (dets + EXTRA), 128)],
        inputs,
        specs=[pl.BlockSpec(memory_space=pltpu.HBM)] * 5,
        scratch=[pltpu.VMEM(a.shape, a.dtype) for a in inputs] + [pltpu.SemaphoreType.DMA((5,))],
        limit=None,
    )
    got = lax.all_to_all(packed, "x", 0, 0, tiled=True)
    (local,) = call(
        functools.partial(project_kernel, nx, modes, pad), [(nz * pad, 128)], (got,)
    )
    swapped = lax.all_to_all(local, "zl", 0, 0, tiled=True)
    (copies,) = call(
        functools.partial(sum_kernel, nl), [(nh * local.shape[0] // nl, 128)], (swapped,)
    )
    copies, got = lax.optimization_barrier((copies, got))
    wide, noise, hi, lo, start, place = call(
        functools.partial(weighted_kernel, nx, bands, modes),
        [(nx * dets, bands * modes)] + [(dets, times)] * 3 + [(2 * HALF, TILE_PIX), (tiles, 2 * HALF)],
        (got, ownership[None, :]),
        scratch=[pltpu.VMEM((dets, times), F32)],
        cost=bin_cost,
        types=[BF16] + [F32] * 4 + [BF16],
    )
    share = add_over(copies, "zh")
    share, wide, noise, hi, lo, start, place = lax.optimization_barrier(
        (share, wide, noise, hi, lo, start, place)
    )
    projected = copy_over(share, "zl")
    amp, part = call(
        functools.partial(correct_kernel, nx, bands, pad),
        [(bands * modes // nx, 128), (tiles, TILE_PIX)],
        (projected, mode_mix, wide, noise, hi, lo, start, place),
        scratch=[pltpu.VMEM((dets, times), F32), pltpu.VMEM((2 * HALF, TILE_PIX), F32)],
        cost=bin_cost,
    )
    moved = [
        lax.ppermute(amp, "x", [(i, (i + k) % nx) for i in range(nx)]) for k in range(1, nx)
    ]
    share = add_over(part, ("x", "zh", "zl"))
    share, *moved = lax.optimization_barrier((share, *moved))
    sky_map = copy_over(share, ("y", "core")).reshape((nt,) + share.shape).sum(0)
    (amplitudes,) = call(
        functools.partial(gather_kernel, nx, bands), [(bands * modes, times)], (amp, *moved)
    )
    return amplitudes, sky_map


def solution(mesh):
    fine = Mesh(mesh.devices.reshape(4, 4, 4, 4, 2), ("x", "zh", "zl", "y", "core"))
    det, tm = ("x", "zh", "zl"), ("y", "core")
    placed = (P(det, tm), P(det, tm), P(det), P(det, None), P(), P(det), P())
    return jax.shard_map(
        per_device,
        mesh=fine,
        in_specs=placed,
        out_specs=(P(None, tm), P(det, None)),
        check_vma=False,
    )
```

```python
import functools

import jax
import jax.numpy as jnp
from jax import lax
from jax.experimental import pallas as pl
from jax.experimental.pallas import tpu as pltpu
from jax.sharding import Mesh, PartitionSpec as P

TILE_PIX = 128
HALF = 256
GROUP = 8
EXTRA = 8
F32 = jnp.float32
BF16 = jnp.bfloat16


def lanes(rows, width):
    return lax.broadcasted_iota(jnp.int32, (rows, 128), 1) // width


def turn(x, amount):
    amount %= 128
    return pltpu.roll(x, amount, 1) if amount else x


def split(x):
    high = x.astype(BF16)
    low = (x - high.astype(F32)).astype(BF16)
    return high, low


def pack_kernel(nx, *refs):
    sources, (out_ref, *held, sems) = refs[:5], refs[5:]
    copies = [
        pltpu.make_async_copy(src, dst, sems.at[n]) for n, (src, dst) in enumerate(zip(sources, held))
    ]
    for copy in copies:
        copy.start()
    for copy in copies:
        copy.wait()
    loading_t_ref, band_ref, noise_ref, ts_ref, point_ref = held
    modes, dets = loading_t_ref.shape
    width = ts_ref.shape[1] // nx
    rows = dets + EXTRA
    ts = ts_ref[...].astype(F32)
    point = point_ref[...].astype(F32)
    loading_t = loading_t_ref[...].astype(F32)
    loading = jnp.concatenate([jnp.zeros((128 - modes, dets), F32), loading_t], axis=0).T
    group = lanes(dets, width)
    for d in range(nx):
        body = jnp.where(group == 0, turn(ts, -width * d), turn(point, width - width * d))
        out_ref[d * rows:d * rows + dets, :] = jnp.where(group < 2, body, loading)
        out_ref[d * rows + dets:(d + 1) * rows, :] = jnp.concatenate(
            [band_ref[...].astype(F32), noise_ref[...], jnp.zeros((EXTRA - 2, dets), F32)], axis=0
        )


def project_kernel(nx, modes, pad, got_ref, out_ref):
    rows = got_ref.shape[0] // nx
    dets = rows - EXTRA
    width = 128 // nx
    per = modes * width // 128
    group = lanes(dets, width)
    slot = lax.broadcasted_iota(jnp.int32, (pad, dets), 0).astype(F32)
    left, right = [], []
    for s in range(nx):
        chunk = got_ref[s * rows:s * rows + dets, :]
        loading_t = chunk.T[128 - modes:, :]
        ts = jnp.where(group == 0, chunk, 0.0)
        pick = jnp.where(slot == got_ref[s * rows + dets:s * rows + dets + 1, :], 1.0, 0.0)
        for j in range(modes // per):
            part = loading_t[j * per:(j + 1) * per, :]
            left.append((part[:, None, :] * pick[None]).reshape(per * pad, dets).astype(BF16))
            right.append(turn(ts, width * j).astype(BF16))
    out_ref[...] = jnp.dot(
        jnp.concatenate(left, axis=1), jnp.concatenate(right, axis=0), preferred_element_type=F32
    )


def row(ref, i, times):
    return jnp.broadcast_to(ref[pl.ds(i, 1), :], (16, times)).astype(BF16)[None]


def add_bins(value_ref, hi_ref, lo_ref, acc_ref):
    dets, times = value_ref.shape
    ids = lax.broadcasted_iota(jnp.int32, (HALF, times), 0).astype(F32).astype(BF16)
    ids = ids.reshape(HALF // 16, 16, times)
    one = jnp.ones((), BF16)
    zero = jnp.zeros((), BF16)

    def body(g, carry):
        left, right = [], []
        for k in range(GROUP):
            i = g * GROUP + k
            upper = row(hi_ref, i, times) == ids
            lower = row(lo_ref, i, times) == ids
            left.append(jnp.where(upper, one, zero).reshape(HALF, times))
            right.append(jnp.where(lower, row(value_ref, i, times), zero).reshape(HALF, times))
        added = lax.dot_general(
            jnp.concatenate(left, axis=1),
            jnp.concatenate(right, axis=1),
            (((1,), (1,)), ((), ())),
            preferred_element_type=F32,
        )
        acc_ref[:HALF, :] += added[:, :TILE_PIX]
        acc_ref[HALF:, :] += added[:, TILE_PIX:]
        return carry

    lax.fori_loop(0, dets // GROUP, body, 0, unroll=4)


def sum_kernel(count, parts_ref, out_ref):
    rows = parts_ref.shape[0] // count
    total = parts_ref[:rows, :]
    for s in range(1, count):
        total = total + parts_ref[s * rows:(s + 1) * rows, :]
    for s in range(out_ref.shape[0] // rows):
        out_ref[s * rows:(s + 1) * rows, :] = total


def weighted_kernel(
    nx, bands, modes, got_ref, own_ref, wide_ref, noise_ref, hi_ref, lo_ref, acc_ref, place_ref, value_s
):
    tiles = place_ref.shape[0]
    own = own_ref[...]
    own = jnp.broadcast_to(((own & 1) * HALF + (own >> 1)).astype(F32), (128, tiles))
    step = min(128, tiles)
    source = lax.broadcasted_iota(jnp.int32, (step, 2 * HALF), 1).astype(F32)
    for r in range(0, tiles, step):
        here = own[:, r:r + step].T[:, 0:1]
        place_ref[r:r + step, :] = jnp.where(
            jnp.broadcast_to(here, (step, 2 * HALF)) == source, 1.0, 0.0
        ).astype(BF16)
    rows = got_ref.shape[0] // nx
    dets = rows - EXTRA
    width = 128 // nx
    group = lanes(dets, width)
    half = lanes(dets, modes)
    for s in range(nx):
        chunk = got_ref[s * rows:s * rows + dets, :]
        tail = got_ref[s * rows + dets:(s + 1) * rows, :]
        columns = jnp.concatenate([tail, jnp.zeros((128 - EXTRA, dets), F32)], axis=0).T
        band_off = jnp.broadcast_to(columns[:, 0:1], (dets, 128)) - half.astype(F32)
        loading2 = jnp.where(half == 0, turn(chunk, modes), chunk)
        for b in range(0, bands, 2):
            wide_ref[s * dets:(s + 1) * dets, b * modes:(b + 2) * modes] = jnp.where(
                band_off == float(b), loading2, 0.0
            ).astype(BF16)
        here = (
            jnp.broadcast_to(columns[:, 1:2], (dets, 128)),
            turn(chunk, width * s),
            turn(chunk, width * (s - 1)),
        )
        total = here if s == 0 else tuple(
            jnp.where(group == s, a, b) for a, b in zip(here, total)
        )
    noise, ts, point = total
    noise_ref[...] = noise
    value_s[...] = (noise * ts).astype(BF16).astype(F32)
    point = point.astype(jnp.int32)
    hi_ref[...] = (point >> 8).astype(F32)
    lo_ref[...] = (point & 255).astype(F32)
    acc_ref[...] = jnp.zeros_like(acc_ref)
    add_bins(value_s, hi_ref, lo_ref, acc_ref)


def correct_kernel(
    nx, nz, nt, bands, pad, proj_ref, mix_ref, wide_ref, noise_ref, hi_ref, lo_ref, start_ref, place_ref,
    amp_ref, map_ref, value_s, acc_s
):
    modes = mix_ref.shape[1]
    dets = noise_ref.shape[0]
    width = 128 // nx
    per = modes // nx
    group = lanes(per, width)
    rounded = []
    for b in range(bands):
        mine = proj_ref[pl.ds(b, per, stride=pad), :]
        turned = [turn(mine, width * k) for k in range(nx)]
        pieces = []
        for j in range(nx):
            piece = turned[(0 - j) % nx]
            for g in range(1, nx):
                piece = jnp.where(group == g, turned[(g - j) % nx], piece)
            pieces.append(piece)
        p = jnp.concatenate(pieces, axis=0)
        mh, ml = split(mix_ref[b])
        ph, plow = split(p)
        amp = p + jnp.dot(
            jnp.concatenate([mh, ml, mh], axis=1),
            jnp.concatenate([ph, ph, plow], axis=0),
            preferred_element_type=F32,
        )
        rounded.append(amp.astype(BF16))
        packed = amp[:per, :]
        for j in range(1, nx):
            packed = jnp.where(group == j, amp[j * per:(j + 1) * per, :], packed)
        amp_ref[b * per:(b + 1) * per, :] = packed
    fits = jnp.dot(wide_ref[...], jnp.concatenate(rounded, axis=0), preferred_element_type=F32)
    group = lanes(dets, width)
    fitted = fits[:dets, :]
    for s in range(1, nx):
        fitted = jnp.where(group == s, fits[s * dets:(s + 1) * dets, :], fitted)
    value_s[...] = -(noise_ref[...] * fitted).astype(BF16).astype(F32)
    acc_s[...] = start_ref[...]
    add_bins(value_s, hi_ref, lo_ref, acc_s)
    high, low = split(acc_s[...])
    placed = jnp.dot(place_ref[...], jnp.concatenate([high, low], axis=1), preferred_element_type=F32)
    acc_s[:placed.shape[0], :] = placed[:, :TILE_PIX] + placed[:, TILE_PIX:]
    for x in range(nx):
        for k in range(nt):
            at = (x * nt + k) * nz
            map_ref[at:at + nz, :] = acc_s[pl.ds(x * nz * nt + k, nz, stride=nt), :]


def gather_kernel(nx, bands, *refs):
    parts, out_ref = refs[:nx], refs[nx]
    per = parts[0].shape[0] // bands
    width = 128 // nx
    group = lanes(per, width)
    mine = lax.axis_index("x")
    sources = [lax.rem(mine + nx - k, nx) for k in range(nx)]
    for b in range(bands):
        for j in range(nx):
            total = jnp.zeros((per, 128), F32)
            for k in range(nx):
                piece = parts[k][b * per:(b + 1) * per, :]
                moved = pltpu.roll(piece, lax.rem(sources[k] + nx - j, nx) * width, 1)
                total = jnp.where(group == sources[k], moved, total)
            out_ref[(b * nx + j) * per:(b * nx + j + 1) * per, :] = total


def add_over(x, axes):
    swapped = lax.all_to_all(x, axes, 0, 0, tiled=True)
    return swapped.reshape((lax.axis_size(axes), -1) + x.shape[1:]).sum(0)


def copy_over(x, axes):
    count = lax.axis_size(axes)
    spread = jnp.broadcast_to(x[None], (count,) + x.shape).reshape((-1,) + x.shape[1:])
    return lax.all_to_all(spread, axes, 0, 0, tiled=True)


def per_device(
    timestream, pointing, detector_band, mode_loading, mode_mix, noise_weight, ownership
):
    dets, times = timestream.shape
    bands, modes = mode_mix.shape[:2]
    pad = -(-bands // 8) * 8
    tiles = ownership.shape[0]
    nx, nh, nl = lax.axis_size("x"), lax.axis_size("zh"), lax.axis_size("zl")
    nz = nh * nl
    nt = lax.axis_size("y") * lax.axis_size("core")
    vmem = pl.BlockSpec(memory_space=pltpu.VMEM)
    params = pltpu.CompilerParams(vmem_limit_bytes=32 * 1024 * 1024)

    bin_cost = pl.CostEstimate(
        flops=2 * dets * times * HALF * HALF, bytes_accessed=1 << 21, transcendentals=0
    )

    def call(kernel, shapes, args, specs=None, scratch=(), cost=None, limit=params, types=None):
        return pl.pallas_call(
            kernel,
            out_shape=tuple(
                jax.ShapeDtypeStruct(s, t) for s, t in zip(shapes, types or [F32] * len(shapes))
            ),
            in_specs=specs or [vmem] * len(args),
            out_specs=tuple(vmem for _ in shapes),
            scratch_shapes=scratch,
            compiler_params=limit,
            cost_estimate=cost,
        )(*args)

    inputs = (mode_loading.T, detector_band[None, :], noise_weight[None, :], timestream, pointing)
    (packed,) = call(
        functools.partial(pack_kernel, nx),
        [(nx * (dets + EXTRA), 128)],
        inputs,
        specs=[pl.BlockSpec(memory_space=pltpu.HBM)] * 5,
        scratch=[pltpu.VMEM(a.shape, a.dtype) for a in inputs] + [pltpu.SemaphoreType.DMA((5,))],
        limit=None,
    )
    got = lax.all_to_all(packed, "x", 0, 0, tiled=True)
    (local,) = call(
        functools.partial(project_kernel, nx, modes, pad), [(nz * pad, 128)], (got,)
    )
    swapped = lax.all_to_all(local, "zl", 0, 0, tiled=True)
    (copies,) = call(
        functools.partial(sum_kernel, nl), [(nh * local.shape[0] // nl, 128)], (swapped,)
    )
    copies, got = lax.optimization_barrier((copies, got))
    wide, noise, hi, lo, start, place = call(
        functools.partial(weighted_kernel, nx, bands, modes),
        [(nx * dets, bands * modes)] + [(dets, times)] * 3 + [(2 * HALF, TILE_PIX), (tiles, 2 * HALF)],
        (got, ownership[None, :]),
        scratch=[pltpu.VMEM((dets, times), F32)],
        cost=bin_cost,
        types=[BF16] + [F32] * 4 + [BF16],
    )
    share = add_over(copies, "zh")
    share, wide, noise, hi, lo, start, place = lax.optimization_barrier(
        (share, wide, noise, hi, lo, start, place)
    )
    projected = copy_over(share, "zl")
    amp, part = call(
        functools.partial(correct_kernel, nx, nz, nt, bands, pad),
        [(bands * modes // nx, 128), (tiles, TILE_PIX)],
        (projected, mode_mix, wide, noise, hi, lo, start, place),
        scratch=[pltpu.VMEM((dets, times), F32), pltpu.VMEM((2 * HALF, TILE_PIX), F32)],
        cost=bin_cost,
    )
    moved = [
        lax.ppermute(amp, "x", [(i, (i + k) % nx) for i in range(nx)]) for k in range(1, nx)
    ]
    share = add_over(part, ("x", "y", "core"))
    spread = jnp.broadcast_to(share[:, None, None], (nz, nt, 1, TILE_PIX)).reshape(nz * nt, TILE_PIX)
    spread, *moved = lax.optimization_barrier((spread, *moved))
    swapped = lax.all_to_all(spread, ("zh", "zl", "y", "core"), 0, 0, tiled=True)
    sky_map = swapped.reshape(nz, nt, TILE_PIX).sum(0)
    (amplitudes,) = call(
        functools.partial(gather_kernel, nx, bands), [(bands * modes, times)], (amp, *moved)
    )
    return amplitudes, sky_map


def solution(mesh):
    fine = Mesh(mesh.devices.reshape(4, 4, 4, 4, 2), ("x", "zh", "zl", "y", "core"))
    det, tm = ("x", "zh", "zl"), ("y", "core")
    placed = (P(det, tm), P(det, tm), P(det), P(det, None), P(), P(det), P())
    return jax.shard_map(
        per_device,
        mesh=fine,
        in_specs=placed,
        out_specs=(P(None, tm), P(det, None)),
        check_vma=False,
    )
```

```python
import functools

import jax
import jax.numpy as jnp
from jax import lax
from jax.experimental import pallas as pl
from jax.experimental.pallas import tpu as pltpu
from jax.sharding import Mesh, PartitionSpec as P

TILE_PIX = 128
HALF = 256
GROUP = 8
EXTRA = 8
F32 = jnp.float32
BF16 = jnp.bfloat16


def lanes(rows, width):
    return lax.broadcasted_iota(jnp.int32, (rows, 128), 1) // width


def turn(x, amount):
    amount %= 128
    return pltpu.roll(x, amount, 1) if amount else x


def split(x):
    high = x.astype(BF16)
    low = (x - high.astype(F32)).astype(BF16)
    return high, low


def pack_kernel(nx, *refs):
    sources, (out_ref, *held, sems) = refs[:5], refs[5:]
    copies = [
        pltpu.make_async_copy(src, dst, sems.at[n]) for n, (src, dst) in enumerate(zip(sources, held))
    ]
    for copy in copies:
        copy.start()
    for copy in copies:
        copy.wait()
    loading_t_ref, band_ref, noise_ref, ts_ref, point_ref = held
    modes, dets = loading_t_ref.shape
    width = ts_ref.shape[1] // nx
    rows = dets + EXTRA
    ts = ts_ref[...].astype(F32)
    point = point_ref[...].astype(F32)
    loading_t = loading_t_ref[...].astype(F32)
    loading = jnp.concatenate([jnp.zeros((128 - modes, dets), F32), loading_t], axis=0).T
    group = lanes(dets, width)
    for d in range(nx):
        body = jnp.where(group == 0, turn(ts, -width * d), turn(point, width - width * d))
        out_ref[d * rows:d * rows + dets, :] = jnp.where(group < 2, body, loading)
        out_ref[d * rows + dets:(d + 1) * rows, :] = jnp.concatenate(
            [band_ref[...].astype(F32), noise_ref[...], jnp.zeros((EXTRA - 2, dets), F32)], axis=0
        )


def project_kernel(ns, owners, bands, modes, got_ref, out_ref):
    rows = got_ref.shape[0] // ns
    dets = rows - EXTRA
    width = 128 // ns
    per = modes * width // 128
    quad = per // owners
    pair = 8 // quad
    group = lanes(dets, width)
    slot = (lax.broadcasted_iota(jnp.int32, (bands * quad, dets), 0) // quad).astype(F32)
    left, right = [], []
    for s in range(ns):
        chunk = got_ref[s * rows:s * rows + dets, :]
        loading_t = chunk.T[128 - modes:, :]
        ts = jnp.where(group == 0, chunk, 0.0)
        pick = jnp.where(slot == got_ref[s * rows + dets:s * rows + dets + 1, :], 1.0, 0.0)
        pick = pick.reshape(bands // pair, 8, dets)
        for j in range(modes // per):
            parts = [loading_t[j * per + o * quad:j * per + (o + 1) * quad, :] for o in range(owners)]
            part = jnp.stack([jnp.concatenate([p] * pair, axis=0) for p in parts])
            wide = (part[:, None] * pick[None]).reshape(owners * bands * quad, dets)
            left.append(wide.astype(BF16))
            right.append(turn(ts, width * j).astype(BF16))
    out_ref[...] = jnp.dot(
        jnp.concatenate(left, axis=1), jnp.concatenate(right, axis=0), preferred_element_type=F32
    )


def row(ref, i, times):
    return jnp.broadcast_to(ref[pl.ds(i, 1), :], (16, times)).astype(BF16)[None]


def add_bins(value_ref, hi_ref, lo_ref, acc_ref):
    dets, times = value_ref.shape
    ids = lax.broadcasted_iota(jnp.int32, (HALF, times), 0).astype(F32).astype(BF16)
    ids = ids.reshape(HALF // 16, 16, times)
    one = jnp.ones((), BF16)
    zero = jnp.zeros((), BF16)

    def body(g, carry):
        left, right = [], []
        for k in range(GROUP):
            i = g * GROUP + k
            upper = row(hi_ref, i, times) == ids
            lower = row(lo_ref, i, times) == ids
            left.append(jnp.where(upper, one, zero).reshape(HALF, times))
            right.append(jnp.where(lower, row(value_ref, i, times), zero).reshape(HALF, times))
        added = lax.dot_general(
            jnp.concatenate(left, axis=1),
            jnp.concatenate(right, axis=1),
            (((1,), (1,)), ((), ())),
            preferred_element_type=F32,
        )
        acc_ref[:HALF, :] += added[:, :TILE_PIX]
        acc_ref[HALF:, :] += added[:, TILE_PIX:]
        return carry

    lax.fori_loop(0, dets // GROUP, body, 0, unroll=4)


def sum_kernel(count, parts_ref, out_ref):
    rows = parts_ref.shape[0] // count
    total = parts_ref[:rows, :]
    for s in range(1, count):
        total = total + parts_ref[s * rows:(s + 1) * rows, :]
    for s in range(out_ref.shape[0] // rows):
        out_ref[s * rows:(s + 1) * rows, :] = total


def weighted_kernel(
    nx, bands, modes, got_ref, own_ref, wide_ref, noise_ref, hi_ref, lo_ref, acc_ref, place_ref, value_s
):
    tiles = place_ref.shape[0]
    own = own_ref[...]
    own = jnp.broadcast_to(((own & 1) * HALF + (own >> 1)).astype(F32), (128, tiles))
    step = min(128, tiles)
    source = lax.broadcasted_iota(jnp.int32, (step, 2 * HALF), 1).astype(F32)
    for r in range(0, tiles, step):
        here = own[:, r:r + step].T[:, 0:1]
        place_ref[r:r + step, :] = jnp.where(
            jnp.broadcast_to(here, (step, 2 * HALF)) == source, 1.0, 0.0
        ).astype(BF16)
    rows = got_ref.shape[0] // nx
    dets = rows - EXTRA
    width = 128 // nx
    group = lanes(dets, width)
    half = lanes(dets, modes)
    for s in range(nx):
        chunk = got_ref[s * rows:s * rows + dets, :]
        tail = got_ref[s * rows + dets:(s + 1) * rows, :]
        columns = jnp.concatenate([tail, jnp.zeros((128 - EXTRA, dets), F32)], axis=0).T
        band_off = jnp.broadcast_to(columns[:, 0:1], (dets, 128)) - half.astype(F32)
        loading2 = jnp.where(half == 0, turn(chunk, modes), chunk)
        for b in range(0, bands, 2):
            wide_ref[s * dets:(s + 1) * dets, b * modes:(b + 2) * modes] = jnp.where(
                band_off == float(b), loading2, 0.0
            ).astype(BF16)
        here = (
            jnp.broadcast_to(columns[:, 1:2], (dets, 128)),
            turn(chunk, width * s),
            turn(chunk, width * (s - 1)),
        )
        total = here if s == 0 else tuple(
            jnp.where(group == s, a, b) for a, b in zip(here, total)
        )
    noise, ts, point = total
    noise_ref[...] = noise
    value_s[...] = (noise * ts).astype(BF16).astype(F32)
    point = point.astype(jnp.int32)
    hi_ref[...] = (point >> 8).astype(F32)
    lo_ref[...] = (point & 255).astype(F32)
    acc_ref[...] = jnp.zeros_like(acc_ref)
    add_bins(value_s, hi_ref, lo_ref, acc_ref)


def correct_kernel(
    nx, owners, bands, proj_ref, mix_ref, wide_ref, noise_ref, hi_ref, lo_ref, start_ref, place_ref,
    amp_ref, map_ref, value_s, acc_s
):
    modes = mix_ref.shape[1]
    dets = noise_ref.shape[0]
    width = 128 // nx
    per = modes // nx
    quad = per // owners
    group = lanes(per, width)
    rounded = []
    for b in range(bands):
        starts = [(o * bands + b) * quad for o in range(owners)]
        mine = jnp.concatenate([proj_ref[at:at + quad, :] for at in starts], axis=0)
        turned = [turn(mine, width * k) for k in range(nx)]
        pieces = []
        for j in range(nx):
            piece = turned[(0 - j) % nx]
            for g in range(1, nx):
                piece = jnp.where(group == g, turned[(g - j) % nx], piece)
            pieces.append(piece)
        p = jnp.concatenate(pieces, axis=0)
        mh, ml = split(mix_ref[b])
        ph, plow = split(p)
        amp = p + jnp.dot(
            jnp.concatenate([mh, ml, mh], axis=1),
            jnp.concatenate([ph, ph, plow], axis=0),
            preferred_element_type=F32,
        )
        rounded.append(amp.astype(BF16))
        packed = amp[:per, :]
        for j in range(1, nx):
            packed = jnp.where(group == j, amp[j * per:(j + 1) * per, :], packed)
        amp_ref[b * per:(b + 1) * per, :] = packed
    fits = jnp.dot(wide_ref[...], jnp.concatenate(rounded, axis=0), preferred_element_type=F32)
    group = lanes(dets, width)
    fitted = fits[:dets, :]
    for s in range(1, nx):
        fitted = jnp.where(group == s, fits[s * dets:(s + 1) * dets, :], fitted)
    value_s[...] = -(noise_ref[...] * fitted).astype(BF16).astype(F32)
    acc_s[...] = start_ref[...]
    add_bins(value_s, hi_ref, lo_ref, acc_s)
    high, low = split(acc_s[...])
    placed = jnp.dot(place_ref[...], jnp.concatenate([high, low], axis=1), preferred_element_type=F32)
    map_ref[...] = placed[:, :TILE_PIX] + placed[:, TILE_PIX:]


def gather_kernel(nx, bands, *refs):
    parts, out_ref = refs[:nx], refs[nx]
    per = parts[0].shape[0] // bands
    width = 128 // nx
    group = lanes(per, width)
    mine = lax.axis_index("zl")
    sources = [jnp.bitwise_xor(mine, k) for k in range(nx)]
    for b in range(bands):
        for j in range(nx):
            total = jnp.zeros((per, 128), F32)
            for k in range(nx):
                piece = parts[k][b * per:(b + 1) * per, :]
                moved = pltpu.roll(piece, lax.rem(sources[k] + nx - j, nx) * width, 1)
                total = jnp.where(group == sources[k], moved, total)
            out_ref[(b * nx + j) * per:(b * nx + j + 1) * per, :] = total


def add_over(x, axes):
    swapped = lax.all_to_all(x, axes, 0, 0, tiled=True)
    return swapped.reshape((lax.axis_size(axes), -1) + x.shape[1:]).sum(0)


def copy_over(x, axes):
    count = lax.axis_size(axes)
    spread = jnp.broadcast_to(x[None], (count,) + x.shape).reshape((-1,) + x.shape[1:])
    return lax.all_to_all(spread, axes, 0, 0, tiled=True)


def per_device(
    timestream, pointing, detector_band, mode_loading, mode_mix, noise_weight, ownership
):
    dets, times = timestream.shape
    bands, modes = mode_mix.shape[:2]
    tiles = ownership.shape[0]
    nx, nh, nl = lax.axis_size("x"), lax.axis_size("zh"), lax.axis_size("zl")
    nt = lax.axis_size("y") * lax.axis_size("core")
    vmem = pl.BlockSpec(memory_space=pltpu.VMEM)
    params = pltpu.CompilerParams(vmem_limit_bytes=32 * 1024 * 1024)

    bin_cost = pl.CostEstimate(
        flops=2 * dets * times * HALF * HALF, bytes_accessed=1 << 21, transcendentals=0
    )

    def call(kernel, shapes, args, specs=None, scratch=(), cost=None, limit=params, types=None):
        return pl.pallas_call(
            kernel,
            out_shape=tuple(
                jax.ShapeDtypeStruct(s, t) for s, t in zip(shapes, types or [F32] * len(shapes))
            ),
            in_specs=specs or [vmem] * len(args),
            out_specs=tuple(vmem for _ in shapes),
            scratch_shapes=scratch,
            compiler_params=limit,
            cost_estimate=cost,
        )(*args)

    inputs = (mode_loading.T, detector_band[None, :], noise_weight[None, :], timestream, pointing)
    (packed,) = call(
        functools.partial(pack_kernel, nl),
        [(nl * (dets + EXTRA), 128)],
        inputs,
        specs=[pl.BlockSpec(memory_space=pltpu.HBM)] * 5,
        scratch=[pltpu.VMEM(a.shape, a.dtype) for a in inputs] + [pltpu.SemaphoreType.DMA((5,))],
        limit=None,
    )
    got = lax.all_to_all(packed, "zl", 0, 0, tiled=True)
    (local,) = call(
        functools.partial(project_kernel, nl, nx, bands, modes),
        [(bands * modes // nl, 128)],
        (got,),
    )
    swapped = lax.all_to_all(local, "x", 0, 0, tiled=True)
    (copies,) = call(
        functools.partial(sum_kernel, nx), [(nh * local.shape[0] // nx, 128)], (swapped,)
    )
    copies, got = lax.optimization_barrier((copies, got))
    wide, noise, hi, lo, start, place = call(
        functools.partial(weighted_kernel, nl, bands, modes),
        [(nl * dets, bands * modes)] + [(dets, times)] * 3 + [(2 * HALF, TILE_PIX), (tiles, 2 * HALF)],
        (got, ownership[None, :]),
        scratch=[pltpu.VMEM((dets, times), F32)],
        cost=bin_cost,
        types=[BF16] + [F32] * 4 + [BF16],
    )
    share = add_over(copies, "zh")
    share, wide, noise, hi, lo, start, place = lax.optimization_barrier(
        (share, wide, noise, hi, lo, start, place)
    )
    projected = copy_over(share, "x")
    amp, part = call(
        functools.partial(correct_kernel, nl, nx, bands),
        [(bands * modes // nl, 128), (tiles, TILE_PIX)],
        (projected, mode_mix, wide, noise, hi, lo, start, place),
        scratch=[pltpu.VMEM((dets, times), F32), pltpu.VMEM((2 * HALF, TILE_PIX), F32)],
        cost=bin_cost,
    )
    moved = [
        lax.ppermute(amp, "zl", [(i, i ^ k) for i in range(nl)]) for k in range(1, nl)
    ]
    share = add_over(part, ("x", "zh", "zl"))
    share, *moved = lax.optimization_barrier((share, *moved))
    sky_map = copy_over(share, ("y", "core")).reshape((nt,) + share.shape).sum(0)
    (amplitudes,) = call(
        functools.partial(gather_kernel, nl, bands), [(bands * modes, times)], (amp, *moved)
    )
    return amplitudes, sky_map


def solution(mesh):
    fine = Mesh(mesh.devices.reshape(4, 4, 4, 4, 2), ("x", "zh", "zl", "y", "core"))
    det, tm = ("x", "zh", "zl"), ("y", "core")
    placed = (P(det, tm), P(det, tm), P(det), P(det, None), P(), P(det), P())
    return jax.shard_map(
        per_device,
        mesh=fine,
        in_specs=placed,
        out_specs=(P(None, tm), P(det, None)),
        check_vma=False,
    )
```

```python
import functools

import jax
import jax.numpy as jnp
from jax import lax
from jax.experimental import pallas as pl
from jax.experimental.pallas import tpu as pltpu
from jax.sharding import Mesh, PartitionSpec as P

TILE_PIX = 128
HALF = 256
GROUP = 8
EXTRA = 8
F32 = jnp.float32
BF16 = jnp.bfloat16


def lanes(rows, width):
    return lax.broadcasted_iota(jnp.int32, (rows, 128), 1) // width


def turn(x, amount):
    amount %= 128
    return pltpu.roll(x, amount, 1) if amount else x


def split(x):
    high = x.astype(BF16)
    low = (x - high.astype(F32)).astype(BF16)
    return high, low


def pack_kernel(nx, *refs):
    sources, (out_ref, *held, sems) = refs[:5], refs[5:]
    copies = [
        pltpu.make_async_copy(src, dst, sems.at[n]) for n, (src, dst) in enumerate(zip(sources, held))
    ]
    for copy in copies:
        copy.start()
    for copy in copies:
        copy.wait()
    loading_t_ref, band_ref, noise_ref, ts_ref, point_ref = held
    modes, dets = loading_t_ref.shape
    width = ts_ref.shape[1] // nx
    rows = dets + EXTRA
    ts = ts_ref[...].astype(F32)
    point = point_ref[...].astype(F32)
    loading_t = loading_t_ref[...].astype(F32)
    loading = jnp.concatenate([jnp.zeros((128 - modes, dets), F32), loading_t], axis=0).T
    group = lanes(dets, width)
    for d in range(nx):
        body = jnp.where(group == 0, turn(ts, -width * d), turn(point, width - width * d))
        out_ref[d * rows:d * rows + dets, :] = jnp.where(group < 2, body, loading)
        out_ref[d * rows + dets:(d + 1) * rows, :] = jnp.concatenate(
            [band_ref[...].astype(F32), noise_ref[...], jnp.zeros((EXTRA - 2, dets), F32)], axis=0
        )


def project_kernel(ns, owners, bands, modes, got_ref, out_ref):
    rows = got_ref.shape[0] // ns
    dets = rows - EXTRA
    width = 128 // ns
    per = modes * width // 128
    quad = per // owners
    pair = 8 // quad
    group = lanes(dets, width)
    slot = (lax.broadcasted_iota(jnp.int32, (bands * quad, dets), 0) // quad).astype(F32)
    left, right = [], []
    for s in range(ns):
        chunk = got_ref[s * rows:s * rows + dets, :]
        loading_t = chunk.T[128 - modes:, :]
        ts = jnp.where(group == 0, chunk, 0.0)
        pick = jnp.where(slot == got_ref[s * rows + dets:s * rows + dets + 1, :], 1.0, 0.0)
        pick = pick.reshape(bands // pair, 8, dets)
        for j in range(modes // per):
            parts = [loading_t[j * per + o * quad:j * per + (o + 1) * quad, :] for o in range(owners)]
            part = jnp.stack([jnp.concatenate([p] * pair, axis=0) for p in parts])
            wide = (part[:, None] * pick[None]).reshape(owners * bands * quad, dets)
            left.append(wide.astype(BF16))
            right.append(turn(ts, width * j).astype(BF16))
    out_ref[...] = jnp.dot(
        jnp.concatenate(left, axis=1), jnp.concatenate(right, axis=0), preferred_element_type=F32
    )


def row(ref, i, times):
    return jnp.broadcast_to(ref[pl.ds(i, 1), :], (16, times)).astype(BF16)[None]


def add_bins(value_ref, hi_ref, lo_ref, acc_ref):
    dets, times = value_ref.shape
    ids = lax.broadcasted_iota(jnp.int32, (HALF, times), 0).astype(F32).astype(BF16)
    ids = ids.reshape(HALF // 16, 16, times)
    one = jnp.ones((), BF16)
    zero = jnp.zeros((), BF16)

    def body(g, carry):
        left, right = [], []
        for k in range(GROUP):
            i = g * GROUP + k
            upper = row(hi_ref, i, times) == ids
            lower = row(lo_ref, i, times) == ids
            left.append(jnp.where(upper, one, zero).reshape(HALF, times))
            right.append(jnp.where(lower, row(value_ref, i, times), zero).reshape(HALF, times))
        added = lax.dot_general(
            jnp.concatenate(left, axis=1),
            jnp.concatenate(right, axis=1),
            (((1,), (1,)), ((), ())),
            preferred_element_type=F32,
        )
        acc_ref[:HALF, :] += added[:, :TILE_PIX]
        acc_ref[HALF:, :] += added[:, TILE_PIX:]
        return carry

    lax.fori_loop(0, dets // GROUP, body, 0, unroll=4)


def sum_kernel(count, parts_ref, out_ref):
    rows = parts_ref.shape[0] // count
    total = parts_ref[:rows, :]
    for s in range(1, count):
        total = total + parts_ref[s * rows:(s + 1) * rows, :]
    for s in range(out_ref.shape[0] // rows):
        out_ref[s * rows:(s + 1) * rows, :] = total


def weighted_kernel(
    nx, bands, modes, got_ref, own_ref, wide_ref, noise_ref, hi_ref, lo_ref, acc_ref, place_ref, value_s
):
    tiles = place_ref.shape[0]
    own = own_ref[...]
    own = jnp.broadcast_to(((own & 1) * HALF + (own >> 1)).astype(F32), (128, tiles))
    step = min(128, tiles)
    source = lax.broadcasted_iota(jnp.int32, (step, 2 * HALF), 1).astype(F32)
    for r in range(0, tiles, step):
        here = own[:, r:r + step].T[:, 0:1]
        place_ref[r:r + step, :] = jnp.where(
            jnp.broadcast_to(here, (step, 2 * HALF)) == source, 1.0, 0.0
        ).astype(BF16)
    rows = got_ref.shape[0] // nx
    dets = rows - EXTRA
    width = 128 // nx
    group = lanes(dets, width)
    half = lanes(dets, modes)
    for s in range(nx):
        chunk = got_ref[s * rows:s * rows + dets, :]
        tail = got_ref[s * rows + dets:(s + 1) * rows, :]
        columns = jnp.concatenate([tail, jnp.zeros((128 - EXTRA, dets), F32)], axis=0).T
        band_off = jnp.broadcast_to(columns[:, 0:1], (dets, 128)) - half.astype(F32)
        loading2 = jnp.where(half == 0, turn(chunk, modes), chunk)
        for b in range(0, bands, 2):
            wide_ref[s * dets:(s + 1) * dets, b * modes:(b + 2) * modes] = jnp.where(
                band_off == float(b), loading2, 0.0
            ).astype(BF16)
        here = (
            jnp.broadcast_to(columns[:, 1:2], (dets, 128)),
            turn(chunk, width * s),
            turn(chunk, width * (s - 1)),
        )
        total = here if s == 0 else tuple(
            jnp.where(group == s, a, b) for a, b in zip(here, total)
        )
    noise, ts, point = total
    noise_ref[...] = noise
    value_s[...] = (noise * ts).astype(BF16).astype(F32)
    point = point.astype(jnp.int32)
    hi_ref[...] = (point >> 8).astype(F32)
    lo_ref[...] = (point & 255).astype(F32)
    acc_ref[...] = jnp.zeros_like(acc_ref)
    add_bins(value_s, hi_ref, lo_ref, acc_ref)


def correct_kernel(
    nx, owners, bands, proj_ref, mix_ref, wide_ref, noise_ref, hi_ref, lo_ref, start_ref, place_ref,
    amp_ref, map_ref, value_s, acc_s
):
    modes = mix_ref.shape[1]
    dets = noise_ref.shape[0]
    width = 128 // nx
    per = modes // nx
    quad = per // owners
    group = lanes(per, width)
    rounded = []
    for b in range(bands):
        starts = [(o * bands + b) * quad for o in range(owners)]
        mine = jnp.concatenate([proj_ref[at:at + quad, :] for at in starts], axis=0)
        turned = [turn(mine, width * k) for k in range(nx)]
        pieces = []
        for j in range(nx):
            piece = turned[(0 - j) % nx]
            for g in range(1, nx):
                piece = jnp.where(group == g, turned[(g - j) % nx], piece)
            pieces.append(piece)
        p = jnp.concatenate(pieces, axis=0)
        mh, ml = split(mix_ref[b])
        ph, plow = split(p)
        amp = p + jnp.dot(
            jnp.concatenate([mh, ml, mh], axis=1),
            jnp.concatenate([ph, ph, plow], axis=0),
            preferred_element_type=F32,
        )
        rounded.append(amp.astype(BF16))
        packed = amp[:per, :]
        for j in range(1, nx):
            packed = jnp.where(group == j, amp[j * per:(j + 1) * per, :], packed)
        amp_ref[b * per:(b + 1) * per, :] = packed
    fits = jnp.dot(wide_ref[...], jnp.concatenate(rounded, axis=0), preferred_element_type=F32)
    group = lanes(dets, width)
    fitted = fits[:dets, :]
    for s in range(1, nx):
        fitted = jnp.where(group == s, fits[s * dets:(s + 1) * dets, :], fitted)
    value_s[...] = -(noise_ref[...] * fitted).astype(BF16).astype(F32)
    acc_s[...] = start_ref[...]
    add_bins(value_s, hi_ref, lo_ref, acc_s)
    high, low = split(acc_s[...])
    placed = jnp.dot(place_ref[...], jnp.concatenate([high, low], axis=1), preferred_element_type=F32)
    map_ref[...] = placed[:, :TILE_PIX] + placed[:, TILE_PIX:]


def gather_kernel(nx, bands, *refs):
    parts, out_ref = refs[:nx], refs[nx]
    per = parts[0].shape[0] // bands
    width = 128 // nx
    group = lanes(per, width)
    mine = lax.axis_index("x")
    sources = [lax.rem(mine + nx - k, nx) for k in range(nx)]
    for b in range(bands):
        for j in range(nx):
            total = jnp.zeros((per, 128), F32)
            for k in range(nx):
                piece = parts[k][b * per:(b + 1) * per, :]
                moved = pltpu.roll(piece, lax.rem(sources[k] + nx - j, nx) * width, 1)
                total = jnp.where(group == sources[k], moved, total)
            out_ref[(b * nx + j) * per:(b * nx + j + 1) * per, :] = total


def add_over(x, axes):
    swapped = lax.all_to_all(x, axes, 0, 0, tiled=True)
    return swapped.reshape((lax.axis_size(axes), -1) + x.shape[1:]).sum(0)


def copy_over(x, axes):
    count = lax.axis_size(axes)
    spread = jnp.broadcast_to(x[None], (count,) + x.shape).reshape((-1,) + x.shape[1:])
    return lax.all_to_all(spread, axes, 0, 0, tiled=True)


def per_device(
    timestream, pointing, detector_band, mode_loading, mode_mix, noise_weight, ownership
):
    dets, times = timestream.shape
    bands, modes = mode_mix.shape[:2]
    tiles = ownership.shape[0]
    nx, nh, nl = lax.axis_size("x"), lax.axis_size("zh"), lax.axis_size("zl")
    nt = lax.axis_size("y") * lax.axis_size("core")
    vmem = pl.BlockSpec(memory_space=pltpu.VMEM)
    params = pltpu.CompilerParams(vmem_limit_bytes=32 * 1024 * 1024)

    bin_cost = pl.CostEstimate(
        flops=2 * dets * times * HALF * HALF, bytes_accessed=1 << 21, transcendentals=0
    )

    def call(kernel, shapes, args, specs=None, scratch=(), cost=None, limit=params, types=None):
        return pl.pallas_call(
            kernel,
            out_shape=tuple(
                jax.ShapeDtypeStruct(s, t) for s, t in zip(shapes, types or [F32] * len(shapes))
            ),
            in_specs=specs or [vmem] * len(args),
            out_specs=tuple(vmem for _ in shapes),
            scratch_shapes=scratch,
            compiler_params=limit,
            cost_estimate=cost,
        )(*args)

    inputs = (mode_loading.T, detector_band[None, :], noise_weight[None, :], timestream, pointing)
    (packed,) = call(
        functools.partial(pack_kernel, nx),
        [(nx * (dets + EXTRA), 128)],
        inputs,
        specs=[pl.BlockSpec(memory_space=pltpu.HBM)] * 5,
        scratch=[pltpu.VMEM(a.shape, a.dtype) for a in inputs] + [pltpu.SemaphoreType.DMA((5,))],
        limit=None,
    )
    got = lax.all_to_all(packed, "x", 0, 0, tiled=True)
    (local,) = call(
        functools.partial(project_kernel, nx, nl, bands, modes),
        [(bands * modes // nx, 128)],
        (got,),
    )
    swapped = lax.all_to_all(local, "zl", 0, 0, tiled=True)
    (copies,) = call(
        functools.partial(sum_kernel, nl), [(nh * local.shape[0] // nl, 128)], (swapped,)
    )
    copies, got = lax.optimization_barrier((copies, got))
    wide, noise, hi, lo, start, place = call(
        functools.partial(weighted_kernel, nx, bands, modes),
        [(nx * dets, bands * modes)] + [(dets, times)] * 3 + [(2 * HALF, TILE_PIX), (tiles, 2 * HALF)],
        (got, ownership[None, :]),
        scratch=[pltpu.VMEM((dets, times), F32)],
        cost=bin_cost,
        types=[BF16] + [F32] * 4 + [BF16],
    )
    share = add_over(copies, "zh")
    share, wide, noise, hi, lo, start, place = lax.optimization_barrier(
        (share, wide, noise, hi, lo, start, place)
    )
    projected = copy_over(share, "zl")
    amp, part = call(
        functools.partial(correct_kernel, nx, nl, bands),
        [(bands * modes // nx, 128), (tiles, TILE_PIX)],
        (projected, mode_mix, wide, noise, hi, lo, start, place),
        scratch=[pltpu.VMEM((dets, times), F32), pltpu.VMEM((2 * HALF, TILE_PIX), F32)],
        cost=bin_cost,
    )
    moved = [
        lax.ppermute(amp, "x", [(i, (i + k) % nx) for i in range(nx)]) for k in range(1, nx)
    ]
    share = add_over(part, ("x", "zh", "zl"))
    share, *moved = lax.optimization_barrier((share, *moved))
    sky_map = copy_over(share, ("y", "core")).reshape((nt,) + share.shape).sum(0)
    (amplitudes,) = call(
        functools.partial(gather_kernel, nx, bands), [(bands * modes, times)], (amp, *moved)
    )
    return amplitudes, sky_map


def solution(mesh):
    fine = Mesh(mesh.devices.reshape(4, 4, 4, 4, 2), ("x", "zh", "zl", "y", "core"))
    det, tm = ("x", "zh", "zl"), ("y", "core")
    placed = (P(det, tm), P(det, tm), P(det), P(det, None), P(), P(det), P())
    return jax.shard_map(
        per_device,
        mesh=fine,
        in_specs=placed,
        out_specs=(P(None, tm), P(det, None)),
        check_vma=False,
    )
```

```python
import functools

import jax
import jax.numpy as jnp
from jax import lax
from jax.experimental import pallas as pl
from jax.experimental.pallas import tpu as pltpu
from jax.sharding import Mesh, PartitionSpec as P

TILE_PIX = 128
HALF = 256
GROUP = 8
EXTRA = 8
F32 = jnp.float32
BF16 = jnp.bfloat16


def lanes(rows, width):
    return lax.broadcasted_iota(jnp.int32, (rows, 128), 1) // width


def turn(x, amount):
    amount %= 128
    return pltpu.roll(x, amount, 1) if amount else x


def split(x):
    high = x.astype(BF16)
    low = (x - high.astype(F32)).astype(BF16)
    return high, low


def place_of(owner, owners, size):
    turned = jnp.where(lax.axis_index("z") >= lax.axis_size("z") // 2, owners // 2, 0)
    return pl.multiple_of(lax.rem(owner + turned, owners) * size, 8)


def pack_kernel(nx, *refs):
    sources, (out_ref, *held, sems) = refs[:5], refs[5:]
    copies = [
        pltpu.make_async_copy(src, dst, sems.at[n]) for n, (src, dst) in enumerate(zip(sources, held))
    ]
    for copy in copies:
        copy.start()
    for copy in copies:
        copy.wait()
    loading_t_ref, band_ref, noise_ref, ts_ref, point_ref = held
    modes, dets = loading_t_ref.shape
    width = ts_ref.shape[1] // nx
    rows = dets + EXTRA
    ts = ts_ref[...].astype(F32)
    point = point_ref[...].astype(F32)
    loading_t = loading_t_ref[...].astype(F32)
    loading = jnp.concatenate([jnp.zeros((128 - modes, dets), F32), loading_t], axis=0).T
    group = lanes(dets, width)
    for d in range(nx):
        body = jnp.where(group == 0, turn(ts, -width * d), turn(point, width - width * d))
        out_ref[d * rows:d * rows + dets, :] = jnp.where(group < 2, body, loading)
        out_ref[d * rows + dets:(d + 1) * rows, :] = jnp.concatenate(
            [band_ref[...].astype(F32), noise_ref[...], jnp.zeros((EXTRA - 2, dets), F32)], axis=0
        )


def project_kernel(ns, owners, bands, modes, got_ref, out_ref):
    rows = got_ref.shape[0] // ns
    dets = rows - EXTRA
    width = 128 // ns
    per = modes * width // 128
    quad = per // owners
    pair = 8 // quad
    group = lanes(dets, width)
    slot = (lax.broadcasted_iota(jnp.int32, (bands * quad, dets), 0) // quad).astype(F32)
    left, right = [], []
    for s in range(ns):
        chunk = got_ref[s * rows:s * rows + dets, :]
        loading_t = chunk.T[128 - modes:, :]
        ts = jnp.where(group == 0, chunk, 0.0)
        pick = jnp.where(slot == got_ref[s * rows + dets:s * rows + dets + 1, :], 1.0, 0.0)
        pick = pick.reshape(bands // pair, 8, dets)
        for j in range(modes // per):
            parts = [loading_t[j * per + o * quad:j * per + (o + 1) * quad, :] for o in range(owners)]
            part = jnp.stack([jnp.concatenate([p] * pair, axis=0) for p in parts])
            wide = (part[:, None] * pick[None]).reshape(owners * bands * quad, dets)
            left.append(wide.astype(BF16))
            right.append(turn(ts, width * j).astype(BF16))
    total = jnp.dot(
        jnp.concatenate(left, axis=1), jnp.concatenate(right, axis=0), preferred_element_type=F32
    )
    size = bands * quad
    for o in range(owners):
        out_ref[pl.ds(place_of(o, owners, size), size), :] = total[o * size:(o + 1) * size, :]


def row(ref, i, times):
    return jnp.broadcast_to(ref[pl.ds(i, 1), :], (16, times)).astype(BF16)[None]


def add_bins(value_ref, hi_ref, lo_ref, acc_ref):
    dets, times = value_ref.shape
    ids = lax.broadcasted_iota(jnp.int32, (HALF, times), 0).astype(F32).astype(BF16)
    ids = ids.reshape(HALF // 16, 16, times)
    one = jnp.ones((), BF16)
    zero = jnp.zeros((), BF16)

    def body(g, carry):
        left, right = [], []
        for k in range(GROUP):
            i = g * GROUP + k
            upper = row(hi_ref, i, times) == ids
            lower = row(lo_ref, i, times) == ids
            left.append(jnp.where(upper, one, zero).reshape(HALF, times))
            right.append(jnp.where(lower, row(value_ref, i, times), zero).reshape(HALF, times))
        added = lax.dot_general(
            jnp.concatenate(left, axis=1),
            jnp.concatenate(right, axis=1),
            (((1,), (1,)), ((), ())),
            preferred_element_type=F32,
        )
        acc_ref[:HALF, :] += added[:, :TILE_PIX]
        acc_ref[HALF:, :] += added[:, TILE_PIX:]
        return carry

    lax.fori_loop(0, dets // GROUP, body, 0, unroll=4)


def sum_kernel(count, parts_ref, out_ref):
    rows = parts_ref.shape[0] // count
    total = parts_ref[:rows, :]
    for s in range(1, count):
        total = total + parts_ref[s * rows:(s + 1) * rows, :]
    for s in range(out_ref.shape[0] // rows):
        out_ref[s * rows:(s + 1) * rows, :] = total


def weighted_kernel(
    nx, bands, modes, got_ref, own_ref, wide_ref, noise_ref, hi_ref, lo_ref, acc_ref, place_ref, value_s
):
    tiles = place_ref.shape[0]
    own = own_ref[...]
    own = jnp.broadcast_to(((own & 1) * HALF + (own >> 1)).astype(F32), (128, tiles))
    step = min(128, tiles)
    source = lax.broadcasted_iota(jnp.int32, (step, 2 * HALF), 1).astype(F32)
    for r in range(0, tiles, step):
        here = own[:, r:r + step].T[:, 0:1]
        place_ref[r:r + step, :] = jnp.where(
            jnp.broadcast_to(here, (step, 2 * HALF)) == source, 1.0, 0.0
        ).astype(BF16)
    rows = got_ref.shape[0] // nx
    dets = rows - EXTRA
    width = 128 // nx
    group = lanes(dets, width)
    half = lanes(dets, modes)
    for s in range(nx):
        chunk = got_ref[s * rows:s * rows + dets, :]
        tail = got_ref[s * rows + dets:(s + 1) * rows, :]
        columns = jnp.concatenate([tail, jnp.zeros((128 - EXTRA, dets), F32)], axis=0).T
        band_off = jnp.broadcast_to(columns[:, 0:1], (dets, 128)) - half.astype(F32)
        loading2 = jnp.where(half == 0, turn(chunk, modes), chunk)
        for b in range(0, bands, 2):
            wide_ref[s * dets:(s + 1) * dets, b * modes:(b + 2) * modes] = jnp.where(
                band_off == float(b), loading2, 0.0
            ).astype(BF16)
        here = (
            jnp.broadcast_to(columns[:, 1:2], (dets, 128)),
            turn(chunk, width * s),
            turn(chunk, width * (s - 1)),
        )
        total = here if s == 0 else tuple(
            jnp.where(group == s, a, b) for a, b in zip(here, total)
        )
    noise, ts, point = total
    noise_ref[...] = noise
    value_s[...] = (noise * ts).astype(BF16).astype(F32)
    point = point.astype(jnp.int32)
    hi_ref[...] = (point >> 8).astype(F32)
    lo_ref[...] = (point & 255).astype(F32)
    acc_ref[...] = jnp.zeros_like(acc_ref)
    add_bins(value_s, hi_ref, lo_ref, acc_ref)


def correct_kernel(
    nx, owners, bands, proj_ref, mix_ref, wide_ref, noise_ref, hi_ref, lo_ref, start_ref, place_ref,
    amp_ref, map_ref, value_s, acc_s, shares_s
):
    modes = mix_ref.shape[1]
    dets = noise_ref.shape[0]
    width = 128 // nx
    per = modes // nx
    quad = per // owners
    group = lanes(per, width)
    rounded = []
    size = bands * quad
    for o in range(owners):
        shares_s[o * size:(o + 1) * size, :] = proj_ref[pl.ds(place_of(o, owners, size), size), :]
    for b in range(bands):
        starts = [(o * bands + b) * quad for o in range(owners)]
        mine = jnp.concatenate([shares_s[at:at + quad, :] for at in starts], axis=0)
        turned = [turn(mine, width * k) for k in range(nx)]
        pieces = []
        for j in range(nx):
            piece = turned[(0 - j) % nx]
            for g in range(1, nx):
                piece = jnp.where(group == g, turned[(g - j) % nx], piece)
            pieces.append(piece)
        p = jnp.concatenate(pieces, axis=0)
        mh, ml = split(mix_ref[b])
        ph, plow = split(p)
        amp = p + jnp.dot(
            jnp.concatenate([mh, ml, mh], axis=1),
            jnp.concatenate([ph, ph, plow], axis=0),
            preferred_element_type=F32,
        )
        rounded.append(amp.astype(BF16))
        packed = amp[:per, :]
        for j in range(1, nx):
            packed = jnp.where(group == j, amp[j * per:(j + 1) * per, :], packed)
        amp_ref[b * per:(b + 1) * per, :] = packed
    fits = jnp.dot(wide_ref[...], jnp.concatenate(rounded, axis=0), preferred_element_type=F32)
    group = lanes(dets, width)
    fitted = fits[:dets, :]
    for s in range(1, nx):
        fitted = jnp.where(group == s, fits[s * dets:(s + 1) * dets, :], fitted)
    value_s[...] = -(noise_ref[...] * fitted).astype(BF16).astype(F32)
    acc_s[...] = start_ref[...]
    add_bins(value_s, hi_ref, lo_ref, acc_s)
    high, low = split(acc_s[...])
    placed = jnp.dot(place_ref[...], jnp.concatenate([high, low], axis=1), preferred_element_type=F32)
    map_ref[...] = placed[:, :TILE_PIX] + placed[:, TILE_PIX:]


def gather_kernel(nx, bands, *refs):
    parts, out_ref = refs[:nx], refs[nx]
    per = parts[0].shape[0] // bands
    width = 128 // nx
    group = lanes(per, width)
    mine = lax.axis_index("x")
    sources = [lax.rem(mine + nx - k, nx) for k in range(nx)]
    for b in range(bands):
        for j in range(nx):
            total = jnp.zeros((per, 128), F32)
            for k in range(nx):
                piece = parts[k][b * per:(b + 1) * per, :]
                moved = pltpu.roll(piece, lax.rem(sources[k] + nx - j, nx) * width, 1)
                total = jnp.where(group == sources[k], moved, total)
            out_ref[(b * nx + j) * per:(b * nx + j + 1) * per, :] = total


def add_over(x, axes, groups=None):
    swapped = lax.all_to_all(x, axes, 0, 0, tiled=True, axis_index_groups=groups)
    count = len(groups[0]) if groups else lax.axis_size(axes)
    return swapped.reshape((count, -1) + x.shape[1:]).sum(0)


def copy_over(x, axes, groups=None):
    count = len(groups[0]) if groups else lax.axis_size(axes)
    spread = jnp.broadcast_to(x[None], (count,) + x.shape).reshape((-1,) + x.shape[1:])
    return lax.all_to_all(spread, axes, 0, 0, tiled=True, axis_index_groups=groups)


def per_device(
    timestream, pointing, detector_band, mode_loading, mode_mix, noise_weight, ownership
):
    dets, times = timestream.shape
    bands, modes = mode_mix.shape[:2]
    tiles = ownership.shape[0]
    nx, nz = lax.axis_size("x"), lax.axis_size("z")
    nl = 4
    nh = nz // nl
    quads = [[h * nl + p for p in range(nl)] for h in range(nh)]
    rings = [
        [h * nl + (o + (nl // 2 if h >= nh // 2 else 0)) % nl for h in range(nh)] for o in range(nl)
    ]
    nt = lax.axis_size("y") * lax.axis_size("core")
    vmem = pl.BlockSpec(memory_space=pltpu.VMEM)
    params = pltpu.CompilerParams(vmem_limit_bytes=32 * 1024 * 1024)

    bin_cost = pl.CostEstimate(
        flops=2 * dets * times * HALF * HALF, bytes_accessed=1 << 21, transcendentals=0
    )

    def call(kernel, shapes, args, specs=None, scratch=(), cost=None, limit=params, types=None):
        return pl.pallas_call(
            kernel,
            out_shape=tuple(
                jax.ShapeDtypeStruct(s, t) for s, t in zip(shapes, types or [F32] * len(shapes))
            ),
            in_specs=specs or [vmem] * len(args),
            out_specs=tuple(vmem for _ in shapes),
            scratch_shapes=scratch,
            compiler_params=limit,
            cost_estimate=cost,
        )(*args)

    inputs = (mode_loading.T, detector_band[None, :], noise_weight[None, :], timestream, pointing)
    (packed,) = call(
        functools.partial(pack_kernel, nx),
        [(nx * (dets + EXTRA), 128)],
        inputs,
        specs=[pl.BlockSpec(memory_space=pltpu.HBM)] * 5,
        scratch=[pltpu.VMEM(a.shape, a.dtype) for a in inputs] + [pltpu.SemaphoreType.DMA((5,))],
        limit=None,
    )
    got = lax.all_to_all(packed, "x", 0, 0, tiled=True)
    (local,) = call(
        functools.partial(project_kernel, nx, nl, bands, modes),
        [(bands * modes // nx, 128)],
        (got,),
    )
    swapped = lax.all_to_all(local, "z", 0, 0, tiled=True, axis_index_groups=quads)
    (copies,) = call(
        functools.partial(sum_kernel, nl), [(nh * local.shape[0] // nl, 128)], (swapped,)
    )
    copies, got = lax.optimization_barrier((copies, got))
    wide, noise, hi, lo, start, place = call(
        functools.partial(weighted_kernel, nx, bands, modes),
        [(nx * dets, bands * modes)] + [(dets, times)] * 3 + [(2 * HALF, TILE_PIX), (tiles, 2 * HALF)],
        (got, ownership[None, :]),
        scratch=[pltpu.VMEM((dets, times), F32)],
        cost=bin_cost,
        types=[BF16] + [F32] * 4 + [BF16],
    )
    share = add_over(copies, "z", rings)
    share, wide, noise, hi, lo, start, place = lax.optimization_barrier(
        (share, wide, noise, hi, lo, start, place)
    )
    projected = copy_over(share, "z", quads)
    amp, part = call(
        functools.partial(correct_kernel, nx, nl, bands),
        [(bands * modes // nx, 128), (tiles, TILE_PIX)],
        (projected, mode_mix, wide, noise, hi, lo, start, place),
        scratch=[
            pltpu.VMEM((dets, times), F32),
            pltpu.VMEM((2 * HALF, TILE_PIX), F32),
            pltpu.VMEM((bands * modes // nx, 128), F32),
        ],
        cost=bin_cost,
    )
    moved = [
        lax.ppermute(amp, "x", [(i, (i + k) % nx) for i in range(nx)]) for k in range(1, nx)
    ]
    share = add_over(part, ("x", "z"))
    share, *moved = lax.optimization_barrier((share, *moved))
    sky_map = copy_over(share, ("y", "core")).reshape((nt,) + share.shape).sum(0)
    (amplitudes,) = call(
        functools.partial(gather_kernel, nx, bands), [(bands * modes, times)], (amp, *moved)
    )
    return amplitudes, sky_map


def solution(mesh):
    fine = Mesh(mesh.devices.reshape(4, 16, 4, 2), ("x", "z", "y", "core"))
    det, tm = ("x", "z"), ("y", "core")
    placed = (P(det, tm), P(det, tm), P(det), P(det, None), P(), P(det), P())
    return jax.shard_map(
        per_device,
        mesh=fine,
        in_specs=placed,
        out_specs=(P(None, tm), P(det, None)),
        check_vma=False,
    )
```

```python
import functools

import jax
import jax.numpy as jnp
from jax import lax
from jax.experimental import pallas as pl
from jax.experimental.pallas import tpu as pltpu
from jax.sharding import Mesh, PartitionSpec as P

TILE_PIX = 128
HALF = 256
GROUP = 8
EXTRA = 8
F32 = jnp.float32
BF16 = jnp.bfloat16


def lanes(rows, width):
    return lax.broadcasted_iota(jnp.int32, (rows, 128), 1) // width


def turn(x, amount):
    amount %= 128
    return pltpu.roll(x, amount, 1) if amount else x


def split(x):
    high = x.astype(BF16)
    low = (x - high.astype(F32)).astype(BF16)
    return high, low


def place_of(owner, owners, size):
    turned = jnp.where(lax.axis_index("z") >= lax.axis_size("z") // 2, owners // 2, 0)
    return pl.multiple_of(lax.rem(owner + turned, owners) * size, 8)


def pack_kernel(nx, *refs):
    sources, (out_ref, *held, sems) = refs[:5], refs[5:]
    copies = [
        pltpu.make_async_copy(src, dst, sems.at[n]) for n, (src, dst) in enumerate(zip(sources, held))
    ]
    for copy in copies:
        copy.start()
    for copy in copies:
        copy.wait()
    loading_t_ref, band_ref, noise_ref, ts_ref, point_ref = held
    modes, dets = loading_t_ref.shape
    width = ts_ref.shape[1] // nx
    rows = dets + EXTRA
    ts = ts_ref[...].astype(F32)
    point = point_ref[...].astype(F32)
    loading_t = loading_t_ref[...].astype(F32)
    loading = jnp.concatenate([jnp.zeros((128 - modes, dets), F32), loading_t], axis=0).T
    group = lanes(dets, width)
    for d in range(nx):
        body = jnp.where(group == 0, turn(ts, -width * d), turn(point, width - width * d))
        out_ref[d * rows:d * rows + dets, :] = jnp.where(group < 2, body, loading)
        out_ref[d * rows + dets:(d + 1) * rows, :] = jnp.concatenate(
            [band_ref[...].astype(F32), noise_ref[...], jnp.zeros((EXTRA - 2, dets), F32)], axis=0
        )


def project_kernel(ns, owners, bands, modes, got_ref, out_ref):
    rows = got_ref.shape[0] // ns
    dets = rows - EXTRA
    width = 128 // ns
    per = modes * width // 128
    quad = per // owners
    pair = 8 // quad
    group = lanes(dets, width)
    slot = (lax.broadcasted_iota(jnp.int32, (bands * quad, dets), 0) // quad).astype(F32)
    left, right = [], []
    for s in range(ns):
        chunk = got_ref[s * rows:s * rows + dets, :]
        loading_t = chunk.T[128 - modes:, :]
        ts = jnp.where(group == 0, chunk, 0.0)
        pick = jnp.where(slot == got_ref[s * rows + dets:s * rows + dets + 1, :], 1.0, 0.0)
        pick = pick.reshape(bands // pair, 8, dets)
        for j in range(modes // per):
            parts = [loading_t[j * per + o * quad:j * per + (o + 1) * quad, :] for o in range(owners)]
            part = jnp.stack([jnp.concatenate([p] * pair, axis=0) for p in parts])
            wide = (part[:, None] * pick[None]).reshape(owners * bands * quad, dets)
            left.append(wide.astype(BF16))
            right.append(turn(ts, width * j).astype(BF16))
    total = jnp.dot(
        jnp.concatenate(left, axis=1), jnp.concatenate(right, axis=0), preferred_element_type=F32
    )
    size = bands * quad
    for o in range(owners):
        out_ref[pl.ds(place_of(o, owners, size), size), :] = total[o * size:(o + 1) * size, :]


def row(ref, i, times):
    return jnp.broadcast_to(ref[pl.ds(i, 1), :], (16, times)).astype(BF16)[None]


def add_bins(value_ref, hi_ref, lo_ref, acc_ref, upper_ref):
    dets, times = value_ref.shape
    ids = lax.broadcasted_iota(jnp.int32, (HALF, times), 0).astype(F32).astype(BF16)
    ids = ids.reshape(HALF // 16, 16, times)
    one = jnp.ones((), BF16)
    zero = jnp.zeros((), BF16)
    span = GROUP * times

    def body(g, carry):
        left, right = [], []
        for k in range(GROUP):
            i = g * GROUP + k
            lower = row(lo_ref, i, times) == ids
            right.append(jnp.where(lower, row(value_ref, i, times), zero).reshape(HALF, times))
            if hi_ref is not None:
                upper = row(hi_ref, i, times) == ids
                left.append(jnp.where(upper, one, zero).reshape(HALF, times))
        at = pl.ds(pl.multiple_of(g * span, span), span)
        if hi_ref is None:
            left = upper_ref[:, at]
        else:
            left = jnp.concatenate(left, axis=1)
            upper_ref[:, at] = left
        added = lax.dot_general(
            left,
            jnp.concatenate(right, axis=1),
            (((1,), (1,)), ((), ())),
            preferred_element_type=F32,
        )
        acc_ref[:HALF, :] += added[:, :TILE_PIX]
        acc_ref[HALF:, :] += added[:, TILE_PIX:]
        return carry

    lax.fori_loop(0, dets // GROUP, body, 0, unroll=4)


def sum_kernel(count, parts_ref, out_ref):
    rows = parts_ref.shape[0] // count
    total = parts_ref[:rows, :]
    for s in range(1, count):
        total = total + parts_ref[s * rows:(s + 1) * rows, :]
    for s in range(out_ref.shape[0] // rows):
        out_ref[s * rows:(s + 1) * rows, :] = total


def weighted_kernel(
    nx, bands, modes, got_ref, own_ref, wide_ref, noise_ref, upper_ref, lo_ref, acc_ref, place_ref,
    hi_s, value_s
):
    tiles = place_ref.shape[0]
    own = own_ref[...]
    own = jnp.broadcast_to(((own & 1) * HALF + (own >> 1)).astype(F32), (128, tiles))
    step = min(128, tiles)
    source = lax.broadcasted_iota(jnp.int32, (step, 2 * HALF), 1).astype(F32)
    for r in range(0, tiles, step):
        here = own[:, r:r + step].T[:, 0:1]
        place_ref[r:r + step, :] = jnp.where(
            jnp.broadcast_to(here, (step, 2 * HALF)) == source, 1.0, 0.0
        ).astype(BF16)
    rows = got_ref.shape[0] // nx
    dets = rows - EXTRA
    width = 128 // nx
    group = lanes(dets, width)
    half = lanes(dets, modes)
    for s in range(nx):
        chunk = got_ref[s * rows:s * rows + dets, :]
        tail = got_ref[s * rows + dets:(s + 1) * rows, :]
        columns = jnp.concatenate([tail, jnp.zeros((128 - EXTRA, dets), F32)], axis=0).T
        band_off = jnp.broadcast_to(columns[:, 0:1], (dets, 128)) - half.astype(F32)
        loading2 = jnp.where(half == 0, turn(chunk, modes), chunk)
        for b in range(0, bands, 2):
            wide_ref[s * dets:(s + 1) * dets, b * modes:(b + 2) * modes] = jnp.where(
                band_off == float(b), loading2, 0.0
            ).astype(BF16)
        here = (
            jnp.broadcast_to(columns[:, 1:2], (dets, 128)),
            turn(chunk, width * s),
            turn(chunk, width * (s - 1)),
        )
        total = here if s == 0 else tuple(
            jnp.where(group == s, a, b) for a, b in zip(here, total)
        )
    noise, ts, point = total
    noise_ref[...] = noise
    value_s[...] = (noise * ts).astype(BF16).astype(F32)
    point = point.astype(jnp.int32)
    hi_s[...] = (point >> 8).astype(F32)
    lo_ref[...] = (point & 255).astype(F32)
    acc_ref[...] = jnp.zeros_like(acc_ref)
    add_bins(value_s, hi_s, lo_ref, acc_ref, upper_ref)


def correct_kernel(
    nx, owners, bands, proj_ref, mix_ref, wide_ref, noise_ref, upper_ref, lo_ref, start_ref, place_ref,
    amp_ref, map_ref, value_s, acc_s, shares_s
):
    modes = mix_ref.shape[1]
    dets = noise_ref.shape[0]
    width = 128 // nx
    per = modes // nx
    quad = per // owners
    group = lanes(per, width)
    rounded = []
    size = bands * quad
    for o in range(owners):
        shares_s[o * size:(o + 1) * size, :] = proj_ref[pl.ds(place_of(o, owners, size), size), :]
    for b in range(bands):
        starts = [(o * bands + b) * quad for o in range(owners)]
        mine = jnp.concatenate([shares_s[at:at + quad, :] for at in starts], axis=0)
        turned = [turn(mine, width * k) for k in range(nx)]
        pieces = []
        for j in range(nx):
            piece = turned[(0 - j) % nx]
            for g in range(1, nx):
                piece = jnp.where(group == g, turned[(g - j) % nx], piece)
            pieces.append(piece)
        p = jnp.concatenate(pieces, axis=0)
        mh, ml = split(mix_ref[b])
        ph, plow = split(p)
        mixed = jnp.dot(
            jnp.concatenate([mh, ml], axis=0),
            jnp.concatenate([ph, plow], axis=1),
            preferred_element_type=F32,
        )
        amp = p + (mixed[:modes, :128] + (mixed[:modes, 128:] + mixed[modes:, :128]))
        rounded.append(amp.astype(BF16))
        packed = amp[:per, :]
        for j in range(1, nx):
            packed = jnp.where(group == j, amp[j * per:(j + 1) * per, :], packed)
        amp_ref[b * per:(b + 1) * per, :] = packed
    fits = jnp.dot(wide_ref[...], jnp.concatenate(rounded, axis=0), preferred_element_type=F32)
    group = lanes(dets, width)
    fitted = fits[:dets, :]
    for s in range(1, nx):
        fitted = jnp.where(group == s, fits[s * dets:(s + 1) * dets, :], fitted)
    value_s[...] = -(noise_ref[...] * fitted).astype(BF16).astype(F32)
    acc_s[...] = start_ref[...]
    add_bins(value_s, None, lo_ref, acc_s, upper_ref)
    high, low = split(acc_s[...])
    placed = jnp.dot(place_ref[...], jnp.concatenate([high, low], axis=1), preferred_element_type=F32)
    map_ref[...] = placed[:, :TILE_PIX] + placed[:, TILE_PIX:]


def gather_kernel(nx, bands, *refs):
    parts, out_ref = refs[:nx], refs[nx]
    per = parts[0].shape[0] // bands
    width = 128 // nx
    group = lanes(per, width)
    mine = lax.axis_index("x")
    sources = [lax.rem(mine + nx - k, nx) for k in range(nx)]
    for b in range(bands):
        for j in range(nx):
            total = jnp.zeros((per, 128), F32)
            for k in range(nx):
                piece = parts[k][b * per:(b + 1) * per, :]
                moved = pltpu.roll(piece, lax.rem(sources[k] + nx - j, nx) * width, 1)
                total = jnp.where(group == sources[k], moved, total)
            out_ref[(b * nx + j) * per:(b * nx + j + 1) * per, :] = total


def add_over(x, axes, groups=None):
    swapped = lax.all_to_all(x, axes, 0, 0, tiled=True, axis_index_groups=groups)
    count = len(groups[0]) if groups else lax.axis_size(axes)
    return swapped.reshape((count, -1) + x.shape[1:]).sum(0)


def copy_over(x, axes, groups=None):
    count = len(groups[0]) if groups else lax.axis_size(axes)
    spread = jnp.broadcast_to(x[None], (count,) + x.shape).reshape((-1,) + x.shape[1:])
    return lax.all_to_all(spread, axes, 0, 0, tiled=True, axis_index_groups=groups)


def per_device(
    timestream, pointing, detector_band, mode_loading, mode_mix, noise_weight, ownership
):
    dets, times = timestream.shape
    bands, modes = mode_mix.shape[:2]
    tiles = ownership.shape[0]
    nx, nz = lax.axis_size("x"), lax.axis_size("z")
    nl = 4
    nh = nz // nl
    quads = [[h * nl + p for p in range(nl)] for h in range(nh)]
    rings = [
        [h * nl + (o + (nl // 2 if h >= nh // 2 else 0)) % nl for h in range(nh)] for o in range(nl)
    ]
    nt = lax.axis_size("y") * lax.axis_size("core")
    vmem = pl.BlockSpec(memory_space=pltpu.VMEM)
    params = pltpu.CompilerParams(vmem_limit_bytes=32 * 1024 * 1024)

    bin_cost = pl.CostEstimate(
        flops=2 * dets * times * HALF * HALF, bytes_accessed=1 << 21, transcendentals=0
    )

    def call(kernel, shapes, args, specs=None, scratch=(), cost=None, limit=params, types=None):
        return pl.pallas_call(
            kernel,
            out_shape=tuple(
                jax.ShapeDtypeStruct(s, t) for s, t in zip(shapes, types or [F32] * len(shapes))
            ),
            in_specs=specs or [vmem] * len(args),
            out_specs=tuple(vmem for _ in shapes),
            scratch_shapes=scratch,
            compiler_params=limit,
            cost_estimate=cost,
        )(*args)

    inputs = (mode_loading.T, detector_band[None, :], noise_weight[None, :], timestream, pointing)
    (packed,) = call(
        functools.partial(pack_kernel, nx),
        [(nx * (dets + EXTRA), 128)],
        inputs,
        specs=[pl.BlockSpec(memory_space=pltpu.HBM)] * 5,
        scratch=[pltpu.VMEM(a.shape, a.dtype) for a in inputs] + [pltpu.SemaphoreType.DMA((5,))],
        limit=None,
    )
    got = lax.all_to_all(packed, "x", 0, 0, tiled=True)
    (local,) = call(
        functools.partial(project_kernel, nx, nl, bands, modes),
        [(bands * modes // nx, 128)],
        (got,),
    )
    swapped = lax.all_to_all(local, "z", 0, 0, tiled=True, axis_index_groups=quads)
    (copies,) = call(
        functools.partial(sum_kernel, nl), [(nh * local.shape[0] // nl, 128)], (swapped,)
    )
    copies, got = lax.optimization_barrier((copies, got))
    wide, noise, upper, lo, start, place = call(
        functools.partial(weighted_kernel, nx, bands, modes),
        [
            (nx * dets, bands * modes),
            (dets, times),
            (HALF, dets * times),
            (dets, times),
            (2 * HALF, TILE_PIX),
            (tiles, 2 * HALF),
        ],
        (got, ownership[None, :]),
        scratch=[pltpu.VMEM((dets, times), F32)] * 2,
        cost=bin_cost,
        types=[BF16, F32, BF16, F32, F32, BF16],
    )
    share = add_over(copies, "z", rings)
    share, wide, noise, upper, lo, start, place = lax.optimization_barrier(
        (share, wide, noise, upper, lo, start, place)
    )
    projected = copy_over(share, "z", quads)
    amp, part = call(
        functools.partial(correct_kernel, nx, nl, bands),
        [(bands * modes // nx, 128), (tiles, TILE_PIX)],
        (projected, mode_mix, wide, noise, upper, lo, start, place),
        scratch=[
            pltpu.VMEM((dets, times), F32),
            pltpu.VMEM((2 * HALF, TILE_PIX), F32),
            pltpu.VMEM((bands * modes // nx, 128), F32),
        ],
        cost=bin_cost,
    )
    moved = [
        lax.ppermute(amp, "x", [(i, (i + k) % nx) for i in range(nx)]) for k in range(1, nx)
    ]
    share = add_over(part, ("x", "z"))
    share, *moved = lax.optimization_barrier((share, *moved))
    sky_map = copy_over(share, ("y", "core")).reshape((nt,) + share.shape).sum(0)
    (amplitudes,) = call(
        functools.partial(gather_kernel, nx, bands), [(bands * modes, times)], (amp, *moved)
    )
    return amplitudes, sky_map


def solution(mesh):
    fine = Mesh(mesh.devices.reshape(4, 16, 4, 2), ("x", "z", "y", "core"))
    det, tm = ("x", "z"), ("y", "core")
    placed = (P(det, tm), P(det, tm), P(det), P(det, None), P(), P(det), P())
    return jax.shard_map(
        per_device,
        mesh=fine,
        in_specs=placed,
        out_specs=(P(None, tm), P(det, None)),
        check_vma=False,
    )
```

```python
import functools

import jax
import jax.numpy as jnp
from jax import lax
from jax.experimental import pallas as pl
from jax.experimental.pallas import tpu as pltpu
from jax.sharding import Mesh, PartitionSpec as P

TILE_PIX = 128
HALF = 256
GROUP = 8
EXTRA = 8
F32 = jnp.float32
BF16 = jnp.bfloat16


def lanes(rows, width):
    return lax.broadcasted_iota(jnp.int32, (rows, 128), 1) // width


def turn(x, amount):
    amount %= 128
    return pltpu.roll(x, amount, 1) if amount else x


def split(x):
    high = x.astype(BF16)
    low = (x - high.astype(F32)).astype(BF16)
    return high, low


def place_of(owner, owners, size):
    turned = jnp.where(lax.axis_index("z") >= lax.axis_size("z") // 2, owners // 2, 0)
    return pl.multiple_of(lax.rem(owner + turned, owners) * size, 8)


def pack_kernel(nx, *refs):
    sources, (out_ref, *held, sems) = refs[:5], refs[5:]
    copies = [
        pltpu.make_async_copy(src, dst, sems.at[n]) for n, (src, dst) in enumerate(zip(sources, held))
    ]
    for copy in copies:
        copy.start()
    for copy in copies:
        copy.wait()
    loading_t_ref, band_ref, noise_ref, ts_ref, point_ref = held
    modes, dets = loading_t_ref.shape
    width = ts_ref.shape[1] // nx
    rows = dets + EXTRA
    ts = ts_ref[...].astype(F32)
    point = point_ref[...].astype(F32)
    loading_t = loading_t_ref[...].astype(F32)
    loading = jnp.concatenate([jnp.zeros((128 - modes, dets), F32), loading_t], axis=0).T
    group = lanes(dets, width)
    for d in range(nx):
        body = jnp.where(group == 0, turn(ts, -width * d), turn(point, width - width * d))
        out_ref[d * rows:d * rows + dets, :] = jnp.where(group < 2, body, loading)
        out_ref[d * rows + dets:(d + 1) * rows, :] = jnp.concatenate(
            [band_ref[...].astype(F32), noise_ref[...], jnp.zeros((EXTRA - 2, dets), F32)], axis=0
        )


def project_kernel(ns, owners, bands, modes, got_ref, out_ref):
    rows = got_ref.shape[0] // ns
    dets = rows - EXTRA
    width = 128 // ns
    per = modes * width // 128
    quad = per // owners
    pair = 8 // quad
    group = lanes(dets, width)
    slot = (lax.broadcasted_iota(jnp.int32, (bands * quad, dets), 0) // quad).astype(F32)
    left, right = [], []
    for s in range(ns):
        chunk = got_ref[s * rows:s * rows + dets, :]
        loading_t = chunk.T[128 - modes:, :]
        ts = jnp.where(group == 0, chunk, 0.0)
        pick = jnp.where(slot == got_ref[s * rows + dets:s * rows + dets + 1, :], 1.0, 0.0)
        pick = pick.reshape(bands // pair, 8, dets)
        for j in range(modes // per):
            parts = [loading_t[j * per + o * quad:j * per + (o + 1) * quad, :] for o in range(owners)]
            part = jnp.stack([jnp.concatenate([p] * pair, axis=0) for p in parts])
            wide = (part[:, None] * pick[None]).reshape(owners * bands * quad, dets)
            left.append(wide.astype(BF16))
            right.append(turn(ts, width * j).astype(BF16))
    total = jnp.dot(
        jnp.concatenate(left, axis=1), jnp.concatenate(right, axis=0), preferred_element_type=F32
    )
    size = bands * quad
    for o in range(owners):
        out_ref[pl.ds(place_of(o, owners, size), size), :] = total[o * size:(o + 1) * size, :]


def row(ref, i, times):
    return jnp.broadcast_to(ref[pl.ds(i, 1), :], (16, times)).astype(BF16)[None]


def add_bins(value_ref, hi_ref, lo_ref, acc_ref):
    dets, times = value_ref.shape
    ids = lax.broadcasted_iota(jnp.int32, (HALF, times), 0).astype(F32).astype(BF16)
    ids = ids.reshape(HALF // 16, 16, times)
    one = jnp.ones((), BF16)
    zero = jnp.zeros((), BF16)

    def body(g, carry):
        left, right = [], []
        for k in range(GROUP):
            i = g * GROUP + k
            upper = row(hi_ref, i, times) == ids
            lower = row(lo_ref, i, times) == ids
            left.append(jnp.where(upper, one, zero).reshape(HALF, times))
            right.append(jnp.where(lower, row(value_ref, i, times), zero).reshape(HALF, times))
        added = lax.dot_general(
            jnp.concatenate(left, axis=1),
            jnp.concatenate(right, axis=1),
            (((1,), (1,)), ((), ())),
            preferred_element_type=F32,
        )
        acc_ref[:HALF, :] += added[:, :TILE_PIX]
        acc_ref[HALF:, :] += added[:, TILE_PIX:]
        return carry

    lax.fori_loop(0, dets // GROUP, body, 0, unroll=True)


def sum_kernel(count, parts_ref, out_ref):
    rows = parts_ref.shape[0] // count
    total = parts_ref[:rows, :]
    for s in range(1, count):
        total = total + parts_ref[s * rows:(s + 1) * rows, :]
    for s in range(out_ref.shape[0] // rows):
        out_ref[s * rows:(s + 1) * rows, :] = total


def weighted_kernel(
    nx, bands, modes, got_ref, own_ref, wide_ref, noise_ref, hi_ref, lo_ref, acc_ref, place_ref, value_s
):
    tiles = place_ref.shape[0]
    own = own_ref[...]
    own = jnp.broadcast_to(((own & 1) * HALF + (own >> 1)).astype(F32), (128, tiles))
    step = min(128, tiles)
    source = lax.broadcasted_iota(jnp.int32, (step, 2 * HALF), 1).astype(F32)
    for r in range(0, tiles, step):
        here = own[:, r:r + step].T[:, 0:1]
        place_ref[r:r + step, :] = jnp.where(
            jnp.broadcast_to(here, (step, 2 * HALF)) == source, 1.0, 0.0
        ).astype(BF16)
    rows = got_ref.shape[0] // nx
    dets = rows - EXTRA
    width = 128 // nx
    group = lanes(dets, width)
    half = lanes(dets, modes)
    for s in range(nx):
        chunk = got_ref[s * rows:s * rows + dets, :]
        tail = got_ref[s * rows + dets:(s + 1) * rows, :]
        columns = jnp.concatenate([tail, jnp.zeros((128 - EXTRA, dets), F32)], axis=0).T
        band_off = jnp.broadcast_to(columns[:, 0:1], (dets, 128)) - half.astype(F32)
        loading2 = jnp.where(half == 0, turn(chunk, modes), chunk)
        for b in range(0, bands, 2):
            wide_ref[s * dets:(s + 1) * dets, b * modes:(b + 2) * modes] = jnp.where(
                band_off == float(b), loading2, 0.0
            ).astype(BF16)
        here = (
            jnp.broadcast_to(columns[:, 1:2], (dets, 128)),
            turn(chunk, width * s),
            turn(chunk, width * (s - 1)),
        )
        total = here if s == 0 else tuple(
            jnp.where(group == s, a, b) for a, b in zip(here, total)
        )
    noise, ts, point = total
    noise_ref[...] = noise
    value_s[...] = (noise * ts).astype(BF16).astype(F32)
    point = point.astype(jnp.int32)
    hi_ref[...] = (point >> 8).astype(F32)
    lo_ref[...] = (point & 255).astype(F32)
    acc_ref[...] = jnp.zeros_like(acc_ref)
    add_bins(value_s, hi_ref, lo_ref, acc_ref)


def correct_kernel(
    nx, owners, bands, proj_ref, mix_ref, wide_ref, noise_ref, hi_ref, lo_ref, start_ref, place_ref,
    amp_ref, map_ref, value_s, acc_s, shares_s
):
    modes = mix_ref.shape[1]
    dets = noise_ref.shape[0]
    width = 128 // nx
    per = modes // nx
    quad = per // owners
    group = lanes(per, width)
    rounded = []
    size = bands * quad
    for o in range(owners):
        shares_s[o * size:(o + 1) * size, :] = proj_ref[pl.ds(place_of(o, owners, size), size), :]
    for b in range(bands):
        starts = [(o * bands + b) * quad for o in range(owners)]
        mine = jnp.concatenate([shares_s[at:at + quad, :] for at in starts], axis=0)
        turned = [turn(mine, width * k) for k in range(nx)]
        pieces = []
        for j in range(nx):
            piece = turned[(0 - j) % nx]
            for g in range(1, nx):
                piece = jnp.where(group == g, turned[(g - j) % nx], piece)
            pieces.append(piece)
        p = jnp.concatenate(pieces, axis=0)
        mh, ml = split(mix_ref[b])
        ph, plow = split(p)
        mixed = jnp.dot(
            jnp.concatenate([mh, ml], axis=0),
            jnp.concatenate([ph, plow], axis=1),
            preferred_element_type=F32,
        )
        amp = p + (mixed[:modes, :128] + (mixed[:modes, 128:] + mixed[modes:, :128]))
        rounded.append(amp.astype(BF16))
        packed = amp[:per, :]
        for j in range(1, nx):
            packed = jnp.where(group == j, amp[j * per:(j + 1) * per, :], packed)
        amp_ref[b * per:(b + 1) * per, :] = packed
    fits = jnp.dot(wide_ref[...], jnp.concatenate(rounded, axis=0), preferred_element_type=F32)
    group = lanes(dets, width)
    fitted = fits[:dets, :]
    for s in range(1, nx):
        fitted = jnp.where(group == s, fits[s * dets:(s + 1) * dets, :], fitted)
    value_s[...] = -(noise_ref[...] * fitted).astype(BF16).astype(F32)
    acc_s[...] = start_ref[...]
    add_bins(value_s, hi_ref, lo_ref, acc_s)
    high, low = split(acc_s[...])
    placed = jnp.dot(place_ref[...], jnp.concatenate([high, low], axis=1), preferred_element_type=F32)
    map_ref[...] = placed[:, :TILE_PIX] + placed[:, TILE_PIX:]


def gather_kernel(nx, bands, *refs):
    parts, out_ref = refs[:nx], refs[nx]
    per = parts[0].shape[0] // bands
    width = 128 // nx
    group = lanes(per, width)
    mine = lax.axis_index("x")
    sources = [lax.rem(mine + nx - k, nx) for k in range(nx)]
    for b in range(bands):
        for j in range(nx):
            total = jnp.zeros((per, 128), F32)
            for k in range(nx):
                piece = parts[k][b * per:(b + 1) * per, :]
                moved = pltpu.roll(piece, lax.rem(sources[k] + nx - j, nx) * width, 1)
                total = jnp.where(group == sources[k], moved, total)
            out_ref[(b * nx + j) * per:(b * nx + j + 1) * per, :] = total


def add_over(x, axes, groups=None):
    swapped = lax.all_to_all(x, axes, 0, 0, tiled=True, axis_index_groups=groups)
    count = len(groups[0]) if groups else lax.axis_size(axes)
    return swapped.reshape((count, -1) + x.shape[1:]).sum(0)


def copy_over(x, axes, groups=None):
    count = len(groups[0]) if groups else lax.axis_size(axes)
    spread = jnp.broadcast_to(x[None], (count,) + x.shape).reshape((-1,) + x.shape[1:])
    return lax.all_to_all(spread, axes, 0, 0, tiled=True, axis_index_groups=groups)


def per_device(
    timestream, pointing, detector_band, mode_loading, mode_mix, noise_weight, ownership
):
    dets, times = timestream.shape
    bands, modes = mode_mix.shape[:2]
    tiles = ownership.shape[0]
    nx, nz = lax.axis_size("x"), lax.axis_size("z")
    nl = 4
    nh = nz // nl
    quads = [[h * nl + p for p in range(nl)] for h in range(nh)]
    rings = [
        [h * nl + (o + (nl // 2 if h >= nh // 2 else 0)) % nl for h in range(nh)] for o in range(nl)
    ]
    nt = lax.axis_size("y") * lax.axis_size("core")
    vmem = pl.BlockSpec(memory_space=pltpu.VMEM)
    params = pltpu.CompilerParams(vmem_limit_bytes=32 * 1024 * 1024)

    bin_cost = pl.CostEstimate(
        flops=2 * dets * times * HALF * HALF, bytes_accessed=1 << 21, transcendentals=0
    )

    def call(kernel, shapes, args, specs=None, scratch=(), cost=None, limit=params, types=None):
        return pl.pallas_call(
            kernel,
            out_shape=tuple(
                jax.ShapeDtypeStruct(s, t) for s, t in zip(shapes, types or [F32] * len(shapes))
            ),
            in_specs=specs or [vmem] * len(args),
            out_specs=tuple(vmem for _ in shapes),
            scratch_shapes=scratch,
            compiler_params=limit,
            cost_estimate=cost,
        )(*args)

    inputs = (mode_loading.T, detector_band[None, :], noise_weight[None, :], timestream, pointing)
    (packed,) = call(
        functools.partial(pack_kernel, nx),
        [(nx * (dets + EXTRA), 128)],
        inputs,
        specs=[pl.BlockSpec(memory_space=pltpu.HBM)] * 5,
        scratch=[pltpu.VMEM(a.shape, a.dtype) for a in inputs] + [pltpu.SemaphoreType.DMA((5,))],
        limit=None,
    )
    got = lax.all_to_all(packed, "x", 0, 0, tiled=True)
    (local,) = call(
        functools.partial(project_kernel, nx, nl, bands, modes),
        [(bands * modes // nx, 128)],
        (got,),
    )
    swapped = lax.all_to_all(local, "z", 0, 0, tiled=True, axis_index_groups=quads)
    (copies,) = call(
        functools.partial(sum_kernel, nl), [(nh * local.shape[0] // nl, 128)], (swapped,)
    )
    copies, got = lax.optimization_barrier((copies, got))
    wide, noise, hi, lo, start, place = call(
        functools.partial(weighted_kernel, nx, bands, modes),
        [(nx * dets, bands * modes)] + [(dets, times)] * 3 + [(2 * HALF, TILE_PIX), (tiles, 2 * HALF)],
        (got, ownership[None, :]),
        scratch=[pltpu.VMEM((dets, times), F32)],
        cost=bin_cost,
        types=[BF16] + [F32] * 4 + [BF16],
    )
    share = add_over(copies, "z", rings)
    share, wide, noise, hi, lo, start, place = lax.optimization_barrier(
        (share, wide, noise, hi, lo, start, place)
    )
    projected = lax.all_gather(share, "z", axis=0, tiled=True, axis_index_groups=quads)
    amp, part = call(
        functools.partial(correct_kernel, nx, nl, bands),
        [(bands * modes // nx, 128), (tiles, TILE_PIX)],
        (projected, mode_mix, wide, noise, hi, lo, start, place),
        scratch=[
            pltpu.VMEM((dets, times), F32),
            pltpu.VMEM((2 * HALF, TILE_PIX), F32),
            pltpu.VMEM((bands * modes // nx, 128), F32),
        ],
        cost=bin_cost,
    )
    moved = [
        lax.ppermute(amp, "x", [(i, (i + k) % nx) for i in range(nx)]) for k in range(1, nx)
    ]
    swapped = lax.all_to_all(part, ("x", "z"), 0, 0, tiled=True)
    swapped, *moved = lax.optimization_barrier((swapped, *moved))
    (copies,) = call(
        functools.partial(sum_kernel, nx * nz), [(nt * tiles // (nx * nz), TILE_PIX)], (swapped,)
    )
    sky_map = add_over(copies, ("y", "core"))
    (amplitudes,) = call(
        functools.partial(gather_kernel, nx, bands), [(bands * modes, times)], (amp, *moved)
    )
    return amplitudes, sky_map


def solution(mesh):
    fine = Mesh(mesh.devices.reshape(4, 16, 4, 2), ("x", "z", "y", "core"))
    det, tm = ("x", "z"), ("y", "core")
    placed = (P(det, tm), P(det, tm), P(det), P(det, None), P(), P(det), P())
    return jax.shard_map(
        per_device,
        mesh=fine,
        in_specs=placed,
        out_specs=(P(None, tm), P(det, None)),
        check_vma=False,
    )
```

```python
import functools

import jax
import jax.numpy as jnp
from jax import lax
from jax.experimental import pallas as pl
from jax.experimental.pallas import tpu as pltpu
from jax.sharding import Mesh, PartitionSpec as P

TILE_PIX = 128
HALF = 256
GROUP = 16
EXTRA = 8
F32 = jnp.float32
BF16 = jnp.bfloat16


def lanes(rows, width):
    return lax.broadcasted_iota(jnp.int32, (rows, 128), 1) // width


def turn(x, amount):
    amount %= 128
    return pltpu.roll(x, amount, 1) if amount else x


def split(x):
    high = x.astype(BF16)
    low = (x - high.astype(F32)).astype(BF16)
    return high, low


def place_of(owner, owners, size):
    turned = jnp.where(lax.axis_index("z") >= lax.axis_size("z") // 2, owners // 2, 0)
    return pl.multiple_of(lax.rem(owner + turned, owners) * size, 8)


def pack_kernel(nx, *refs):
    sources, (out_ref, *held, sems) = refs[:5], refs[5:]
    copies = [
        pltpu.make_async_copy(src, dst, sems.at[n]) for n, (src, dst) in enumerate(zip(sources, held))
    ]
    for copy in copies:
        copy.start()
    for copy in copies:
        copy.wait()
    loading_t_ref, band_ref, noise_ref, ts_ref, point_ref = held
    modes, dets = loading_t_ref.shape
    width = ts_ref.shape[1] // nx
    rows = dets + EXTRA
    ts = ts_ref[...].astype(F32)
    point = point_ref[...].astype(F32)
    loading_t = loading_t_ref[...].astype(F32)
    loading = jnp.concatenate([jnp.zeros((128 - modes, dets), F32), loading_t], axis=0).T
    group = lanes(dets, width)
    for d in range(nx):
        body = jnp.where(group == 0, turn(ts, -width * d), turn(point, width - width * d))
        out_ref[d * rows:d * rows + dets, :] = jnp.where(group < 2, body, loading)
        out_ref[d * rows + dets:(d + 1) * rows, :] = jnp.concatenate(
            [band_ref[...].astype(F32), noise_ref[...], jnp.zeros((EXTRA - 2, dets), F32)], axis=0
        )


def project_kernel(ns, owners, bands, modes, got_ref, out_ref):
    rows = got_ref.shape[0] // ns
    dets = rows - EXTRA
    width = 128 // ns
    per = modes * width // 128
    quad = per // owners
    pair = 8 // quad
    group = lanes(dets, width)
    slot = (lax.broadcasted_iota(jnp.int32, (bands * quad, dets), 0) // quad).astype(F32)
    left, right = [], []
    for s in range(ns):
        chunk = got_ref[s * rows:s * rows + dets, :]
        loading_t = chunk.T[128 - modes:, :]
        ts = jnp.where(group == 0, chunk, 0.0)
        pick = jnp.where(slot == got_ref[s * rows + dets:s * rows + dets + 1, :], 1.0, 0.0)
        pick = pick.reshape(bands // pair, 8, dets)
        for j in range(modes // per):
            parts = [loading_t[j * per + o * quad:j * per + (o + 1) * quad, :] for o in range(owners)]
            part = jnp.stack([jnp.concatenate([p] * pair, axis=0) for p in parts])
            wide = (part[:, None] * pick[None]).reshape(owners * bands * quad, dets)
            left.append(wide.astype(BF16))
            right.append(turn(ts, width * j).astype(BF16))
    total = jnp.dot(
        jnp.concatenate(left, axis=1), jnp.concatenate(right, axis=0), preferred_element_type=F32
    )
    size = bands * quad
    for o in range(owners):
        out_ref[pl.ds(place_of(o, owners, size), size), :] = total[o * size:(o + 1) * size, :]


def row(ref, i, times):
    return jnp.broadcast_to(ref[pl.ds(i, 1), :], (16, times)).astype(BF16)[None]


def add_bins(value_ref, hi_ref, lo_ref, acc_ref):
    dets, times = value_ref.shape
    ids = lax.broadcasted_iota(jnp.int32, (HALF, times), 0).astype(F32).astype(BF16)
    ids = ids.reshape(HALF // 16, 16, times)
    one = jnp.ones((), BF16)
    zero = jnp.zeros((), BF16)

    def body(g, carry):
        left, right = [], []
        for k in range(GROUP):
            i = g * GROUP + k
            upper = row(hi_ref, i, times) == ids
            lower = row(lo_ref, i, times) == ids
            left.append(jnp.where(upper, one, zero).reshape(HALF, times))
            right.append(jnp.where(lower, row(value_ref, i, times), zero).reshape(HALF, times))
        added = lax.dot_general(
            jnp.concatenate(left, axis=1),
            jnp.concatenate(right, axis=1),
            (((1,), (1,)), ((), ())),
            preferred_element_type=F32,
        )
        acc_ref[:HALF, :] += added[:, :TILE_PIX]
        acc_ref[HALF:, :] += added[:, TILE_PIX:]
        return carry

    lax.fori_loop(0, dets // GROUP, body, 0, unroll=True)


def sum_kernel(count, parts_ref, out_ref):
    rows = parts_ref.shape[0] // count
    total = parts_ref[:rows, :]
    for s in range(1, count):
        total = total + parts_ref[s * rows:(s + 1) * rows, :]
    for s in range(out_ref.shape[0] // rows):
        out_ref[s * rows:(s + 1) * rows, :] = total


def weighted_kernel(
    nx, bands, modes, got_ref, own_ref, wide_ref, noise_ref, hi_ref, lo_ref, acc_ref, place_ref, value_s
):
    tiles = place_ref.shape[0]
    own = own_ref[...]
    own = jnp.broadcast_to(((own & 1) * HALF + (own >> 1)).astype(F32), (128, tiles))
    step = min(128, tiles)
    source = lax.broadcasted_iota(jnp.int32, (step, 2 * HALF), 1).astype(F32)
    for r in range(0, tiles, step):
        here = own[:, r:r + step].T[:, 0:1]
        place_ref[r:r + step, :] = jnp.where(
            jnp.broadcast_to(here, (step, 2 * HALF)) == source, 1.0, 0.0
        ).astype(BF16)
    rows = got_ref.shape[0] // nx
    dets = rows - EXTRA
    width = 128 // nx
    group = lanes(dets, width)
    half = lanes(dets, modes)
    for s in range(nx):
        chunk = got_ref[s * rows:s * rows + dets, :]
        tail = got_ref[s * rows + dets:(s + 1) * rows, :]
        columns = jnp.concatenate([tail, jnp.zeros((128 - EXTRA, dets), F32)], axis=0).T
        band_off = jnp.broadcast_to(columns[:, 0:1], (dets, 128)) - half.astype(F32)
        loading2 = jnp.where(half == 0, turn(chunk, modes), chunk)
        for b in range(0, bands, 2):
            wide_ref[s * dets:(s + 1) * dets, b * modes:(b + 2) * modes] = jnp.where(
                band_off == float(b), loading2, 0.0
            ).astype(BF16)
        here = (
            jnp.broadcast_to(columns[:, 1:2], (dets, 128)),
            turn(chunk, width * s),
            turn(chunk, width * (s - 1)),
        )
        total = here if s == 0 else tuple(
            jnp.where(group == s, a, b) for a, b in zip(here, total)
        )
    noise, ts, point = total
    noise_ref[...] = noise
    value_s[...] = (noise * ts).astype(BF16).astype(F32)
    point = point.astype(jnp.int32)
    hi_ref[...] = (point >> 8).astype(F32)
    lo_ref[...] = (point & 255).astype(F32)
    acc_ref[...] = jnp.zeros_like(acc_ref)
    add_bins(value_s, hi_ref, lo_ref, acc_ref)


def correct_kernel(
    nx, owners, bands, proj_ref, mix_ref, wide_ref, noise_ref, hi_ref, lo_ref, start_ref, place_ref,
    amp_ref, map_ref, value_s, acc_s, shares_s
):
    modes = mix_ref.shape[1]
    dets = noise_ref.shape[0]
    width = 128 // nx
    per = modes // nx
    quad = per // owners
    group = lanes(per, width)
    rounded = []
    size = bands * quad
    for o in range(owners):
        shares_s[o * size:(o + 1) * size, :] = proj_ref[pl.ds(place_of(o, owners, size), size), :]
    for b in range(bands):
        starts = [(o * bands + b) * quad for o in range(owners)]
        mine = jnp.concatenate([shares_s[at:at + quad, :] for at in starts], axis=0)
        turned = [turn(mine, width * k) for k in range(nx)]
        pieces = []
        for j in range(nx):
            piece = turned[(0 - j) % nx]
            for g in range(1, nx):
                piece = jnp.where(group == g, turned[(g - j) % nx], piece)
            pieces.append(piece)
        p = jnp.concatenate(pieces, axis=0)
        mh, ml = split(mix_ref[b])
        ph, plow = split(p)
        amp = p + jnp.dot(
            jnp.concatenate([mh, ml, mh], axis=1),
            jnp.concatenate([ph, ph, plow], axis=0),
            preferred_element_type=F32,
        )
        rounded.append(amp.astype(BF16))
        packed = amp[:per, :]
        for j in range(1, nx):
            packed = jnp.where(group == j, amp[j * per:(j + 1) * per, :], packed)
        amp_ref[b * per:(b + 1) * per, :] = packed
    fits = jnp.dot(wide_ref[...], jnp.concatenate(rounded, axis=0), preferred_element_type=F32)
    group = lanes(dets, width)
    fitted = fits[:dets, :]
    for s in range(1, nx):
        fitted = jnp.where(group == s, fits[s * dets:(s + 1) * dets, :], fitted)
    value_s[...] = -(noise_ref[...] * fitted).astype(BF16).astype(F32)
    acc_s[...] = start_ref[...]
    add_bins(value_s, hi_ref, lo_ref, acc_s)
    high, low = split(acc_s[...])
    placed = jnp.dot(place_ref[...], jnp.concatenate([high, low], axis=1), preferred_element_type=F32)
    map_ref[...] = placed[:, :TILE_PIX] + placed[:, TILE_PIX:]


def gather_kernel(nx, bands, *refs):
    parts, out_ref = refs[:nx], refs[nx]
    per = parts[0].shape[0] // bands
    width = 128 // nx
    group = lanes(per, width)
    mine = lax.axis_index("x")
    sources = [lax.rem(mine + nx - k, nx) for k in range(nx)]
    for b in range(bands):
        for j in range(nx):
            total = jnp.zeros((per, 128), F32)
            for k in range(nx):
                piece = parts[k][b * per:(b + 1) * per, :]
                moved = pltpu.roll(piece, lax.rem(sources[k] + nx - j, nx) * width, 1)
                total = jnp.where(group == sources[k], moved, total)
            out_ref[(b * nx + j) * per:(b * nx + j + 1) * per, :] = total


def add_over(x, axes, groups=None):
    swapped = lax.all_to_all(x, axes, 0, 0, tiled=True, axis_index_groups=groups)
    count = len(groups[0]) if groups else lax.axis_size(axes)
    return swapped.reshape((count, -1) + x.shape[1:]).sum(0)


def copy_over(x, axes, groups=None):
    count = len(groups[0]) if groups else lax.axis_size(axes)
    spread = jnp.broadcast_to(x[None], (count,) + x.shape).reshape((-1,) + x.shape[1:])
    return lax.all_to_all(spread, axes, 0, 0, tiled=True, axis_index_groups=groups)


def per_device(
    timestream, pointing, detector_band, mode_loading, mode_mix, noise_weight, ownership
):
    dets, times = timestream.shape
    bands, modes = mode_mix.shape[:2]
    tiles = ownership.shape[0]
    nx, nz = lax.axis_size("x"), lax.axis_size("z")
    nl = 4
    nh = nz // nl
    quads = [[h * nl + p for p in range(nl)] for h in range(nh)]
    rings = [
        [h * nl + (o + (nl // 2 if h >= nh // 2 else 0)) % nl for h in range(nh)] for o in range(nl)
    ]
    nt = lax.axis_size("y") * lax.axis_size("core")
    vmem = pl.BlockSpec(memory_space=pltpu.VMEM)
    params = pltpu.CompilerParams(vmem_limit_bytes=32 * 1024 * 1024)

    bin_cost = pl.CostEstimate(
        flops=2 * dets * times * HALF * HALF, bytes_accessed=1 << 21, transcendentals=0
    )

    def call(kernel, shapes, args, specs=None, scratch=(), cost=None, limit=params, types=None):
        return pl.pallas_call(
            kernel,
            out_shape=tuple(
                jax.ShapeDtypeStruct(s, t) for s, t in zip(shapes, types or [F32] * len(shapes))
            ),
            in_specs=specs or [vmem] * len(args),
            out_specs=tuple(vmem for _ in shapes),
            scratch_shapes=scratch,
            compiler_params=limit,
            cost_estimate=cost,
        )(*args)

    inputs = (mode_loading.T, detector_band[None, :], noise_weight[None, :], timestream, pointing)
    (packed,) = call(
        functools.partial(pack_kernel, nx),
        [(nx * (dets + EXTRA), 128)],
        inputs,
        specs=[pl.BlockSpec(memory_space=pltpu.HBM)] * 5,
        scratch=[pltpu.VMEM(a.shape, a.dtype) for a in inputs] + [pltpu.SemaphoreType.DMA((5,))],
        limit=None,
    )
    got = lax.all_to_all(packed, "x", 0, 0, tiled=True)
    (local,) = call(
        functools.partial(project_kernel, nx, nl, bands, modes),
        [(bands * modes // nx, 128)],
        (got,),
    )
    swapped = lax.all_to_all(local, "z", 0, 0, tiled=True, axis_index_groups=quads)
    (copies,) = call(
        functools.partial(sum_kernel, nl), [(nh * local.shape[0] // nl, 128)], (swapped,)
    )
    copies, got = lax.optimization_barrier((copies, got))
    wide, noise, hi, lo, start, place = call(
        functools.partial(weighted_kernel, nx, bands, modes),
        [(nx * dets, bands * modes)] + [(dets, times)] * 3 + [(2 * HALF, TILE_PIX), (tiles, 2 * HALF)],
        (got, ownership[None, :]),
        scratch=[pltpu.VMEM((dets, times), F32)],
        cost=bin_cost,
        types=[BF16] + [F32] * 4 + [BF16],
    )
    share = add_over(copies, "z", rings)
    share, wide, noise, hi, lo, start, place = lax.optimization_barrier(
        (share, wide, noise, hi, lo, start, place)
    )
    projected = copy_over(share, "z", quads)
    amp, part = call(
        functools.partial(correct_kernel, nx, nl, bands),
        [(bands * modes // nx, 128), (tiles, TILE_PIX)],
        (projected, mode_mix, wide, noise, hi, lo, start, place),
        scratch=[
            pltpu.VMEM((dets, times), F32),
            pltpu.VMEM((2 * HALF, TILE_PIX), F32),
            pltpu.VMEM((bands * modes // nx, 128), F32),
        ],
        cost=bin_cost,
    )
    moved = [
        lax.ppermute(amp, "x", [(i, (i + k) % nx) for i in range(nx)]) for k in range(1, nx)
    ]
    share = add_over(part, ("x", "z"))
    share, *moved = lax.optimization_barrier((share, *moved))
    sky_map = copy_over(share, ("y", "core")).reshape((nt,) + share.shape).sum(0)
    (amplitudes,) = call(
        functools.partial(gather_kernel, nx, bands), [(bands * modes, times)], (amp, *moved)
    )
    return amplitudes, sky_map


def solution(mesh):
    fine = Mesh(mesh.devices.reshape(4, 16, 4, 2), ("x", "z", "y", "core"))
    det, tm = ("x", "z"), ("y", "core")
    placed = (P(det, tm), P(det, tm), P(det), P(det, None), P(), P(det), P())
    return jax.shard_map(
        per_device,
        mesh=fine,
        in_specs=placed,
        out_specs=(P(None, tm), P(det, None)),
        check_vma=False,
    )
```

```python
import functools

import jax
import jax.numpy as jnp
from jax import lax
from jax.experimental import pallas as pl
from jax.experimental.pallas import tpu as pltpu
from jax.sharding import Mesh, PartitionSpec as P

TILE_PIX = 128
HALF = 256
EXTRA = 8
F32 = jnp.float32
BF16 = jnp.bfloat16


def lanes(rows, width):
    return lax.broadcasted_iota(jnp.int32, (rows, 128), 1) // width


def turn(x, amount):
    amount %= 128
    return pltpu.roll(x, amount, 1) if amount else x


def split(x):
    high = x.astype(BF16)
    low = (x - high.astype(F32)).astype(BF16)
    return high, low


def place_of(owner, owners, size):
    turned = jnp.where(lax.axis_index("z") >= lax.axis_size("z") // 2, owners // 2, 0)
    return pl.multiple_of(lax.rem(owner + turned, owners) * size, 8)


def pack_kernel(nx, *refs):
    sources, (out_ref, *held, sems) = refs[:5], refs[5:]
    copies = [
        pltpu.make_async_copy(src, dst, sems.at[n]) for n, (src, dst) in enumerate(zip(sources, held))
    ]
    for copy in copies:
        copy.start()
    for copy in copies:
        copy.wait()
    loading_t_ref, band_ref, noise_ref, ts_ref, point_ref = held
    modes, dets = loading_t_ref.shape
    width = ts_ref.shape[1] // nx
    rows = dets + EXTRA
    ts = ts_ref[...].astype(F32)
    point = point_ref[...].astype(F32)
    loading_t = loading_t_ref[...].astype(F32)
    loading = jnp.concatenate([jnp.zeros((128 - modes, dets), F32), loading_t], axis=0).T
    group = lanes(dets, width)
    for d in range(nx):
        body = jnp.where(group == 0, turn(ts, -width * d), turn(point, width - width * d))
        out_ref[d * rows:d * rows + dets, :] = jnp.where(group < 2, body, loading)
        out_ref[d * rows + dets:(d + 1) * rows, :] = jnp.concatenate(
            [band_ref[...].astype(F32), noise_ref[...], jnp.zeros((EXTRA - 2, dets), F32)], axis=0
        )


def project_kernel(ns, owners, bands, modes, got_ref, out_ref):
    rows = got_ref.shape[0] // ns
    dets = rows - EXTRA
    width = 128 // ns
    per = modes * width // 128
    quad = per // owners
    pair = 8 // quad
    group = lanes(dets, width)
    slot = (lax.broadcasted_iota(jnp.int32, (bands * quad, dets), 0) // quad).astype(F32)
    left, right = [], []
    for s in range(ns):
        chunk = got_ref[s * rows:s * rows + dets, :]
        loading_t = chunk.T[128 - modes:, :]
        ts = jnp.where(group == 0, chunk, 0.0)
        pick = jnp.where(slot == got_ref[s * rows + dets:s * rows + dets + 1, :], 1.0, 0.0)
        pick = pick.reshape(bands // pair, 8, dets)
        for j in range(modes // per):
            parts = [loading_t[j * per + o * quad:j * per + (o + 1) * quad, :] for o in range(owners)]
            part = jnp.stack([jnp.concatenate([p] * pair, axis=0) for p in parts])
            wide = (part[:, None] * pick[None]).reshape(owners * bands * quad, dets)
            left.append(wide.astype(BF16))
            right.append(turn(ts, width * j).astype(BF16))
    total = jnp.dot(
        jnp.concatenate(left, axis=1), jnp.concatenate(right, axis=0), preferred_element_type=F32
    )
    size = bands * quad
    for o in range(owners):
        out_ref[pl.ds(place_of(o, owners, size), size), :] = total[o * size:(o + 1) * size, :]


def row(ref, i, times):
    return jnp.broadcast_to(ref[pl.ds(i, 1), :], (16, times)).astype(BF16)[None]


def add_bins(value_ref, hi_ref, lo_ref, acc_ref, size, unroll):
    dets, times = value_ref.shape
    ids = lax.broadcasted_iota(jnp.int32, (HALF, times), 0).astype(F32).astype(BF16)
    ids = ids.reshape(HALF // 16, 16, times)
    one = jnp.ones((), BF16)
    zero = jnp.zeros((), BF16)

    def body(g, carry):
        left, right = [], []
        for k in range(size):
            i = g * size + k
            upper = row(hi_ref, i, times) == ids
            lower = row(lo_ref, i, times) == ids
            left.append(jnp.where(upper, one, zero).reshape(HALF, times))
            right.append(jnp.where(lower, row(value_ref, i, times), zero).reshape(HALF, times))
        added = lax.dot_general(
            jnp.concatenate(left, axis=1),
            jnp.concatenate(right, axis=1),
            (((1,), (1,)), ((), ())),
            preferred_element_type=F32,
        )
        acc_ref[:HALF, :] += added[:, :TILE_PIX]
        acc_ref[HALF:, :] += added[:, TILE_PIX:]
        return carry

    lax.fori_loop(0, dets // size, body, 0, unroll=unroll)


def weighted_kernel(
    nx, bands, modes, got_ref, own_ref, wide_ref, noise_ref, hi_ref, lo_ref, acc_ref, place_ref, value_s
):
    tiles = place_ref.shape[0]
    own = own_ref[...]
    own = jnp.broadcast_to(((own & 1) * HALF + (own >> 1)).astype(F32), (128, tiles))
    step = min(128, tiles)
    source = lax.broadcasted_iota(jnp.int32, (step, 2 * HALF), 1).astype(F32)
    for r in range(0, tiles, step):
        here = own[:, r:r + step].T[:, 0:1]
        place_ref[r:r + step, :] = jnp.where(
            jnp.broadcast_to(here, (step, 2 * HALF)) == source, 1.0, 0.0
        ).astype(BF16)
    rows = got_ref.shape[0] // nx
    dets = rows - EXTRA
    width = 128 // nx
    group = lanes(dets, width)
    half = lanes(dets, modes)
    for s in range(nx):
        chunk = got_ref[s * rows:s * rows + dets, :]
        tail = got_ref[s * rows + dets:(s + 1) * rows, :]
        columns = jnp.concatenate([tail, jnp.zeros((128 - EXTRA, dets), F32)], axis=0).T
        band_off = jnp.broadcast_to(columns[:, 0:1], (dets, 128)) - half.astype(F32)
        loading2 = jnp.where(half == 0, turn(chunk, modes), chunk)
        for b in range(0, bands, 2):
            wide_ref[s * dets:(s + 1) * dets, b * modes:(b + 2) * modes] = jnp.where(
                band_off == float(b), loading2, 0.0
            ).astype(BF16)
        here = (
            jnp.broadcast_to(columns[:, 1:2], (dets, 128)),
            turn(chunk, width * s),
            turn(chunk, width * (s - 1)),
        )
        total = here if s == 0 else tuple(
            jnp.where(group == s, a, b) for a, b in zip(here, total)
        )
    noise, ts, point = total
    noise_ref[...] = noise
    value_s[...] = (noise * ts).astype(BF16).astype(F32)
    point = point.astype(jnp.int32)
    hi_ref[...] = (point >> 8).astype(F32)
    lo_ref[...] = (point & 255).astype(F32)
    acc_ref[...] = jnp.zeros_like(acc_ref)
    add_bins(value_s, hi_ref, lo_ref, acc_ref, 16, True)


def correct_kernel(
    nx, owners, bands, proj_ref, mix_ref, wide_ref, noise_ref, hi_ref, lo_ref, start_ref, place_ref,
    amp_ref, map_ref, value_s, acc_s, shares_s
):
    modes = mix_ref.shape[1]
    dets = noise_ref.shape[0]
    width = 128 // nx
    per = modes // nx
    quad = per // owners
    group = lanes(per, width)
    rounded = []
    size = bands * quad
    for o in range(owners):
        shares_s[o * size:(o + 1) * size, :] = proj_ref[pl.ds(place_of(o, owners, size), size), :]
    for b in range(bands):
        starts = [(o * bands + b) * quad for o in range(owners)]
        mine = jnp.concatenate([shares_s[at:at + quad, :] for at in starts], axis=0)
        turned = [turn(mine, width * k) for k in range(nx)]
        pieces = []
        for j in range(nx):
            piece = turned[(0 - j) % nx]
            for g in range(1, nx):
                piece = jnp.where(group == g, turned[(g - j) % nx], piece)
            pieces.append(piece)
        p = jnp.concatenate(pieces, axis=0)
        mh, ml = split(mix_ref[b])
        ph, plow = split(p)
        amp = p + jnp.dot(
            jnp.concatenate([mh, ml, mh], axis=1),
            jnp.concatenate([ph, ph, plow], axis=0),
            preferred_element_type=F32,
        )
        rounded.append(amp.astype(BF16))
        packed = amp[:per, :]
        for j in range(1, nx):
            packed = jnp.where(group == j, amp[j * per:(j + 1) * per, :], packed)
        amp_ref[b * per:(b + 1) * per, :] = packed
    fits = jnp.dot(wide_ref[...], jnp.concatenate(rounded, axis=0), preferred_element_type=F32)
    group = lanes(dets, width)
    fitted = fits[:dets, :]
    for s in range(1, nx):
        fitted = jnp.where(group == s, fits[s * dets:(s + 1) * dets, :], fitted)
    value_s[...] = -(noise_ref[...] * fitted).astype(BF16).astype(F32)
    acc_s[...] = start_ref[...]
    add_bins(value_s, hi_ref, lo_ref, acc_s, 8, 4)
    high, low = split(acc_s[...])
    placed = jnp.dot(place_ref[...], jnp.concatenate([high, low], axis=1), preferred_element_type=F32)
    map_ref[...] = placed[:, :TILE_PIX] + placed[:, TILE_PIX:]


def gather_kernel(nx, bands, *refs):
    parts, out_ref = refs[:nx], refs[nx]
    per = parts[0].shape[0] // bands
    width = 128 // nx
    group = lanes(per, width)
    mine = lax.axis_index("x")
    sources = [lax.rem(mine + nx - k, nx) for k in range(nx)]
    for b in range(bands):
        for j in range(nx):
            total = jnp.zeros((per, 128), F32)
            for k in range(nx):
                piece = parts[k][b * per:(b + 1) * per, :]
                moved = pltpu.roll(piece, lax.rem(sources[k] + nx - j, nx) * width, 1)
                total = jnp.where(group == sources[k], moved, total)
            out_ref[(b * nx + j) * per:(b * nx + j + 1) * per, :] = total


def add_over(x, axes, groups=None):
    swapped = lax.all_to_all(x, axes, 0, 0, tiled=True, axis_index_groups=groups)
    count = len(groups[0]) if groups else lax.axis_size(axes)
    return swapped.reshape((count, -1) + x.shape[1:]).sum(0)


def copy_over(x, axes, groups=None):
    count = len(groups[0]) if groups else lax.axis_size(axes)
    spread = jnp.broadcast_to(x[None], (count,) + x.shape).reshape((-1,) + x.shape[1:])
    return lax.all_to_all(spread, axes, 0, 0, tiled=True, axis_index_groups=groups)


def per_device(
    timestream, pointing, detector_band, mode_loading, mode_mix, noise_weight, ownership
):
    dets, times = timestream.shape
    bands, modes = mode_mix.shape[:2]
    tiles = ownership.shape[0]
    nx, nz = lax.axis_size("x"), lax.axis_size("z")
    nl = 4
    nh = nz // nl
    quads = [[h * nl + p for p in range(nl)] for h in range(nh)]
    rings = [
        [h * nl + (o + (nl // 2 if h >= nh // 2 else 0)) % nl for h in range(nh)] for o in range(nl)
    ]
    nt = lax.axis_size("y") * lax.axis_size("core")
    vmem = pl.BlockSpec(memory_space=pltpu.VMEM)
    params = pltpu.CompilerParams(vmem_limit_bytes=32 * 1024 * 1024)

    bin_cost = pl.CostEstimate(
        flops=2 * dets * times * HALF * HALF, bytes_accessed=1 << 21, transcendentals=0
    )

    def call(kernel, shapes, args, specs=None, scratch=(), cost=None, limit=params, types=None):
        return pl.pallas_call(
            kernel,
            out_shape=tuple(
                jax.ShapeDtypeStruct(s, t) for s, t in zip(shapes, types or [F32] * len(shapes))
            ),
            in_specs=specs or [vmem] * len(args),
            out_specs=tuple(vmem for _ in shapes),
            scratch_shapes=scratch,
            compiler_params=limit,
            cost_estimate=cost,
        )(*args)

    inputs = (mode_loading.T, detector_band[None, :], noise_weight[None, :], timestream, pointing)
    (packed,) = call(
        functools.partial(pack_kernel, nx),
        [(nx * (dets + EXTRA), 128)],
        inputs,
        specs=[pl.BlockSpec(memory_space=pltpu.HBM)] * 5,
        scratch=[pltpu.VMEM(a.shape, a.dtype) for a in inputs] + [pltpu.SemaphoreType.DMA((5,))],
        limit=None,
    )
    got = lax.all_to_all(packed, "x", 0, 0, tiled=True)
    (local,) = call(
        functools.partial(project_kernel, nx, nl, bands, modes),
        [(bands * modes // nx, 128)],
        (got,),
    )
    local, got = lax.optimization_barrier((local, got))
    share = add_over(local, "z", quads)
    wide, noise, hi, lo, start, place = call(
        functools.partial(weighted_kernel, nx, bands, modes),
        [(nx * dets, bands * modes)] + [(dets, times)] * 3 + [(2 * HALF, TILE_PIX), (tiles, 2 * HALF)],
        (got, ownership[None, :]),
        scratch=[pltpu.VMEM((dets, times), F32)],
        cost=bin_cost,
        types=[BF16] + [F32] * 4 + [BF16],
    )
    share, wide, noise, hi, lo, start, place = lax.optimization_barrier(
        (share, wide, noise, hi, lo, start, place)
    )
    share = copy_over(share, "z", rings).reshape((nh,) + share.shape).sum(0)
    projected = copy_over(share, "z", quads)
    amp, part = call(
        functools.partial(correct_kernel, nx, nl, bands),
        [(bands * modes // nx, 128), (tiles, TILE_PIX)],
        (projected, mode_mix, wide, noise, hi, lo, start, place),
        scratch=[
            pltpu.VMEM((dets, times), F32),
            pltpu.VMEM((2 * HALF, TILE_PIX), F32),
            pltpu.VMEM((bands * modes // nx, 128), F32),
        ],
        cost=bin_cost,
    )
    moved = [
        lax.ppermute(amp, "x", [(i, (i + k) % nx) for i in range(nx)]) for k in range(1, nx)
    ]
    share = add_over(part, ("x", "z"))
    share, *moved = lax.optimization_barrier((share, *moved))
    sky_map = copy_over(share, ("y", "core")).reshape((nt,) + share.shape).sum(0)
    (amplitudes,) = call(
        functools.partial(gather_kernel, nx, bands), [(bands * modes, times)], (amp, *moved)
    )
    return amplitudes, sky_map


def solution(mesh):
    fine = Mesh(mesh.devices.reshape(4, 16, 4, 2), ("x", "z", "y", "core"))
    det, tm = ("x", "z"), ("y", "core")
    placed = (P(det, tm), P(det, tm), P(det), P(det, None), P(), P(det), P())
    return jax.shard_map(
        per_device,
        mesh=fine,
        in_specs=placed,
        out_specs=(P(None, tm), P(det, None)),
        check_vma=False,
    )
```

```python
import functools

import jax
import jax.numpy as jnp
from jax import lax
from jax.experimental import pallas as pl
from jax.experimental.pallas import tpu as pltpu
from jax.sharding import Mesh, PartitionSpec as P

TILE_PIX = 128
HALF = 256
GROUP = 8
EXTRA = 8
F32 = jnp.float32
BF16 = jnp.bfloat16


def lanes(rows, width):
    return lax.broadcasted_iota(jnp.int32, (rows, 128), 1) // width


def turn(x, amount):
    amount %= 128
    return pltpu.roll(x, amount, 1) if amount else x


def split(x):
    high = x.astype(BF16)
    low = (x - high.astype(F32)).astype(BF16)
    return high, low


def place_of(owner, owners, size):
    turned = jnp.where(lax.axis_index("z") >= lax.axis_size("z") // 2, owners // 2, 0)
    return pl.multiple_of(lax.rem(owner + turned, owners) * size, 8)


def pack_kernel(nx, *refs):
    sources, (out_ref, *held, sems) = refs[:5], refs[5:]
    copies = [
        pltpu.make_async_copy(src, dst, sems.at[n]) for n, (src, dst) in enumerate(zip(sources, held))
    ]
    for copy in copies:
        copy.start()
    for copy in copies:
        copy.wait()
    loading_t_ref, band_ref, noise_ref, ts_ref, point_ref = held
    modes, dets = loading_t_ref.shape
    width = ts_ref.shape[1] // nx
    rows = dets + EXTRA
    ts = ts_ref[...].astype(F32)
    point = point_ref[...].astype(F32)
    loading_t = loading_t_ref[...].astype(F32)
    loading = jnp.concatenate([jnp.zeros((128 - modes, dets), F32), loading_t], axis=0).T
    group = lanes(dets, width)
    for d in range(nx):
        body = jnp.where(group == 0, turn(ts, -width * d), turn(point, width - width * d))
        out_ref[d * rows:d * rows + dets, :] = jnp.where(group < 2, body, loading)
        out_ref[d * rows + dets:(d + 1) * rows, :] = jnp.concatenate(
            [band_ref[...].astype(F32), noise_ref[...], jnp.zeros((EXTRA - 2, dets), F32)], axis=0
        )


def project_kernel(ns, owners, bands, modes, got_ref, out_ref):
    rows = got_ref.shape[0] // ns
    dets = rows - EXTRA
    width = 128 // ns
    per = modes * width // 128
    quad = per // owners
    pair = 8 // quad
    group = lanes(dets, width)
    slot = (lax.broadcasted_iota(jnp.int32, (bands * quad, dets), 0) // quad).astype(F32)
    left, right = [], []
    for s in range(ns):
        chunk = got_ref[s * rows:s * rows + dets, :]
        loading_t = chunk.T[128 - modes:, :]
        ts = jnp.where(group == 0, chunk, 0.0)
        pick = jnp.where(slot == got_ref[s * rows + dets:s * rows + dets + 1, :], 1.0, 0.0)
        pick = pick.reshape(bands // pair, 8, dets)
        for j in range(modes // per):
            parts = [loading_t[j * per + o * quad:j * per + (o + 1) * quad, :] for o in range(owners)]
            part = jnp.stack([jnp.concatenate([p] * pair, axis=0) for p in parts])
            wide = (part[:, None] * pick[None]).reshape(owners * bands * quad, dets)
            left.append(wide.astype(BF16))
            right.append(turn(ts, width * j).astype(BF16))
    total = jnp.dot(
        jnp.concatenate(left, axis=1), jnp.concatenate(right, axis=0), preferred_element_type=F32
    )
    size = bands * quad
    for o in range(owners):
        out_ref[pl.ds(place_of(o, owners, size), size), :] = total[o * size:(o + 1) * size, :]


def row(ref, i, times):
    return jnp.broadcast_to(ref[pl.ds(i, 1), :], (16, times)).astype(BF16)[None]


def add_bins(value_ref, hi_ref, lo_ref, acc_ref):
    dets, times = value_ref.shape
    ids = lax.broadcasted_iota(jnp.int32, (HALF, times), 0).astype(F32).astype(BF16)
    ids = ids.reshape(HALF // 16, 16, times)
    one = jnp.ones((), BF16)
    zero = jnp.zeros((), BF16)

    def body(g, carry):
        left, right = [], []
        for k in range(GROUP):
            i = g * GROUP + k
            upper = row(hi_ref, i, times) == ids
            lower = row(lo_ref, i, times) == ids
            left.append(jnp.where(upper, one, zero).reshape(HALF, times))
            right.append(jnp.where(lower, row(value_ref, i, times), zero).reshape(HALF, times))
        added = lax.dot_general(
            jnp.concatenate(left, axis=1),
            jnp.concatenate(right, axis=1),
            (((1,), (1,)), ((), ())),
            preferred_element_type=F32,
        )
        acc_ref[:HALF, :] += added[:, :TILE_PIX]
        acc_ref[HALF:, :] += added[:, TILE_PIX:]
        return carry

    lax.fori_loop(0, dets // GROUP, body, 0, unroll=4)


def sum_kernel(count, parts_ref, out_ref):
    rows = parts_ref.shape[0] // count
    total = parts_ref[:rows, :]
    for s in range(1, count):
        total = total + parts_ref[s * rows:(s + 1) * rows, :]
    for s in range(out_ref.shape[0] // rows):
        out_ref[s * rows:(s + 1) * rows, :] = total


def weighted_kernel(
    nx, bands, modes, got_ref, own_ref, mix_ref, parts_ref, wide_ref, noise_ref, hi_ref, lo_ref, acc_ref, place_ref, value_s
):
    for b in range(bands):
        mh, ml = split(mix_ref[b])
        parts_ref[b * modes:(b + 1) * modes, :] = jnp.concatenate([mh, ml, mh], axis=1)
    tiles = place_ref.shape[0]
    own = own_ref[...]
    own = jnp.broadcast_to(((own & 1) * HALF + (own >> 1)).astype(F32), (128, tiles))
    step = min(128, tiles)
    source = lax.broadcasted_iota(jnp.int32, (step, 2 * HALF), 1).astype(F32)
    for r in range(0, tiles, step):
        here = own[:, r:r + step].T[:, 0:1]
        place_ref[r:r + step, :] = jnp.where(
            jnp.broadcast_to(here, (step, 2 * HALF)) == source, 1.0, 0.0
        ).astype(BF16)
    rows = got_ref.shape[0] // nx
    dets = rows - EXTRA
    width = 128 // nx
    group = lanes(dets, width)
    half = lanes(dets, modes)
    for s in range(nx):
        chunk = got_ref[s * rows:s * rows + dets, :]
        tail = got_ref[s * rows + dets:(s + 1) * rows, :]
        columns = jnp.concatenate([tail, jnp.zeros((128 - EXTRA, dets), F32)], axis=0).T
        band_off = jnp.broadcast_to(columns[:, 0:1], (dets, 128)) - half.astype(F32)
        loading2 = jnp.where(half == 0, turn(chunk, modes), chunk)
        for b in range(0, bands, 2):
            wide_ref[s * dets:(s + 1) * dets, b * modes:(b + 2) * modes] = jnp.where(
                band_off == float(b), loading2, 0.0
            ).astype(BF16)
        here = (
            jnp.broadcast_to(columns[:, 1:2], (dets, 128)),
            turn(chunk, width * s),
            turn(chunk, width * (s - 1)),
        )
        total = here if s == 0 else tuple(
            jnp.where(group == s, a, b) for a, b in zip(here, total)
        )
    noise, ts, point = total
    noise_ref[...] = noise
    value_s[...] = (noise * ts).astype(BF16).astype(F32)
    point = point.astype(jnp.int32)
    hi_ref[...] = (point >> 8).astype(F32)
    lo_ref[...] = (point & 255).astype(F32)
    acc_ref[...] = jnp.zeros_like(acc_ref)
    add_bins(value_s, hi_ref, lo_ref, acc_ref)


def correct_kernel(
    nx, owners, bands, proj_ref, parts_ref, wide_ref, noise_ref, hi_ref, lo_ref, start_ref, place_ref,
    amp_ref, map_ref, value_s, acc_s, shares_s
):
    modes = parts_ref.shape[0] // bands
    dets = noise_ref.shape[0]
    width = 128 // nx
    per = modes // nx
    quad = per // owners
    group = lanes(per, width)
    rounded = []
    size = bands * quad
    for o in range(owners):
        shares_s[o * size:(o + 1) * size, :] = proj_ref[pl.ds(place_of(o, owners, size), size), :]
    for b in range(bands):
        starts = [(o * bands + b) * quad for o in range(owners)]
        mine = jnp.concatenate([shares_s[at:at + quad, :] for at in starts], axis=0)
        turned = [turn(mine, width * k) for k in range(nx)]
        pieces = []
        for j in range(nx):
            piece = turned[(0 - j) % nx]
            for g in range(1, nx):
                piece = jnp.where(group == g, turned[(g - j) % nx], piece)
            pieces.append(piece)
        p = jnp.concatenate(pieces, axis=0)
        ph, plow = split(p)
        amp = p + jnp.dot(
            parts_ref[b * modes:(b + 1) * modes, :],
            jnp.concatenate([ph, ph, plow], axis=0),
            preferred_element_type=F32,
        )
        rounded.append(amp.astype(BF16))
        packed = amp[:per, :]
        for j in range(1, nx):
            packed = jnp.where(group == j, amp[j * per:(j + 1) * per, :], packed)
        amp_ref[b * per:(b + 1) * per, :] = packed
    fits = jnp.dot(wide_ref[...], jnp.concatenate(rounded, axis=0), preferred_element_type=F32)
    group = lanes(dets, width)
    fitted = fits[:dets, :]
    for s in range(1, nx):
        fitted = jnp.where(group == s, fits[s * dets:(s + 1) * dets, :], fitted)
    value_s[...] = -(noise_ref[...] * fitted).astype(BF16).astype(F32)
    acc_s[...] = start_ref[...]
    add_bins(value_s, hi_ref, lo_ref, acc_s)
    high, low = split(acc_s[...])
    placed = jnp.dot(place_ref[...], jnp.concatenate([high, low], axis=1), preferred_element_type=F32)
    map_ref[...] = placed[:, :TILE_PIX] + placed[:, TILE_PIX:]


def gather_kernel(nx, bands, *refs):
    parts, out_ref = refs[:nx], refs[nx]
    per = parts[0].shape[0] // bands
    width = 128 // nx
    group = lanes(per, width)
    mine = lax.axis_index("x")
    sources = [lax.rem(mine + nx - k, nx) for k in range(nx)]
    for b in range(bands):
        for j in range(nx):
            total = jnp.zeros((per, 128), F32)
            for k in range(nx):
                piece = parts[k][b * per:(b + 1) * per, :]
                moved = pltpu.roll(piece, lax.rem(sources[k] + nx - j, nx) * width, 1)
                total = jnp.where(group == sources[k], moved, total)
            out_ref[(b * nx + j) * per:(b * nx + j + 1) * per, :] = total


def add_over(x, axes, groups=None):
    swapped = lax.all_to_all(x, axes, 0, 0, tiled=True, axis_index_groups=groups)
    count = len(groups[0]) if groups else lax.axis_size(axes)
    return swapped.reshape((count, -1) + x.shape[1:]).sum(0)


def copy_over(x, axes, groups=None):
    count = len(groups[0]) if groups else lax.axis_size(axes)
    spread = jnp.broadcast_to(x[None], (count,) + x.shape).reshape((-1,) + x.shape[1:])
    return lax.all_to_all(spread, axes, 0, 0, tiled=True, axis_index_groups=groups)


def per_device(
    timestream, pointing, detector_band, mode_loading, mode_mix, noise_weight, ownership
):
    dets, times = timestream.shape
    bands, modes = mode_mix.shape[:2]
    tiles = ownership.shape[0]
    nx, nz = lax.axis_size("x"), lax.axis_size("z")
    nl = 4
    nh = nz // nl
    quads = [[h * nl + p for p in range(nl)] for h in range(nh)]
    rings = [
        [h * nl + (o + (nl // 2 if h >= nh // 2 else 0)) % nl for h in range(nh)] for o in range(nl)
    ]
    nt = lax.axis_size("y") * lax.axis_size("core")
    vmem = pl.BlockSpec(memory_space=pltpu.VMEM)
    params = pltpu.CompilerParams(vmem_limit_bytes=32 * 1024 * 1024)

    bin_cost = pl.CostEstimate(
        flops=2 * dets * times * HALF * HALF, bytes_accessed=1 << 21, transcendentals=0
    )

    def call(kernel, shapes, args, specs=None, scratch=(), cost=None, limit=params, types=None):
        return pl.pallas_call(
            kernel,
            out_shape=tuple(
                jax.ShapeDtypeStruct(s, t) for s, t in zip(shapes, types or [F32] * len(shapes))
            ),
            in_specs=specs or [vmem] * len(args),
            out_specs=tuple(vmem for _ in shapes),
            scratch_shapes=scratch,
            compiler_params=limit,
            cost_estimate=cost,
        )(*args)

    inputs = (mode_loading.T, detector_band[None, :], noise_weight[None, :], timestream, pointing)
    (packed,) = call(
        functools.partial(pack_kernel, nx),
        [(nx * (dets + EXTRA), 128)],
        inputs,
        specs=[pl.BlockSpec(memory_space=pltpu.HBM)] * 5,
        scratch=[pltpu.VMEM(a.shape, a.dtype) for a in inputs] + [pltpu.SemaphoreType.DMA((5,))],
        limit=None,
    )
    got = lax.all_to_all(packed, "x", 0, 0, tiled=True)
    (local,) = call(
        functools.partial(project_kernel, nx, nl, bands, modes),
        [(bands * modes // nx, 128)],
        (got,),
    )
    swapped = lax.all_to_all(local, "z", 0, 0, tiled=True, axis_index_groups=quads)
    (copies,) = call(
        functools.partial(sum_kernel, nl), [(nh * local.shape[0] // nl, 128)], (swapped,)
    )
    copies, got = lax.optimization_barrier((copies, got))
    parts, wide, noise, hi, lo, start, place = call(
        functools.partial(weighted_kernel, nx, bands, modes),
        [(bands * modes, 3 * modes), (nx * dets, bands * modes)] + [(dets, times)] * 3 + [(2 * HALF, TILE_PIX), (tiles, 2 * HALF)],
        (got, ownership[None, :], mode_mix),
        scratch=[pltpu.VMEM((dets, times), F32)],
        cost=bin_cost,
        types=[BF16] * 2 + [F32] * 4 + [BF16],
    )
    share = add_over(copies, "z", rings)
    share, parts, wide, noise, hi, lo, start, place = lax.optimization_barrier(
        (share, parts, wide, noise, hi, lo, start, place)
    )
    projected = copy_over(share, "z", quads)
    amp, part = call(
        functools.partial(correct_kernel, nx, nl, bands),
        [(bands * modes // nx, 128), (tiles, TILE_PIX)],
        (projected, parts, wide, noise, hi, lo, start, place),
        scratch=[
            pltpu.VMEM((dets, times), F32),
            pltpu.VMEM((2 * HALF, TILE_PIX), F32),
            pltpu.VMEM((bands * modes // nx, 128), F32),
        ],
        cost=bin_cost,
    )
    moved = [
        lax.ppermute(amp, "x", [(i, (i + k) % nx) for i in range(nx)]) for k in range(1, nx)
    ]
    share = add_over(part, ("x", "z"))
    share, *moved = lax.optimization_barrier((share, *moved))
    sky_map = copy_over(share, ("y", "core")).reshape((nt,) + share.shape).sum(0)
    (amplitudes,) = call(
        functools.partial(gather_kernel, nx, bands), [(bands * modes, times)], (amp, *moved)
    )
    return amplitudes, sky_map


def solution(mesh):
    fine = Mesh(mesh.devices.reshape(4, 16, 4, 2), ("x", "z", "y", "core"))
    det, tm = ("x", "z"), ("y", "core")
    placed = (P(det, tm), P(det, tm), P(det), P(det, None), P(), P(det), P())
    return jax.shard_map(
        per_device,
        mesh=fine,
        in_specs=placed,
        out_specs=(P(None, tm), P(det, None)),
        check_vma=False,
    )
```
